32 devices in a mesh: seq: 16 (over z, y, x), head: 2 (over core).
Axes of the slice: x: 2, y: 2, z: 4, core: 2. Of those that a mesh axis runs over, the one named last changes fastest.
Arguments:
- inner_acts: bfloat16 [4096, 8192], P('seq', 'head'), may hold values from -0.4375 to 0.4375
- out_grad: bfloat16 [4096, 8192], P('seq', 'head'), may hold values from -0.4375 to 0.4375
- write_proj: bfloat16 [4096, 128], P('seq'), may hold values from -3 to 3
- read_proj: bfloat16 [4096, 128], P('seq'), may hold values from -3 to 3
- log_decay: float32 [4096, 64], P('seq', 'head'), may hold values from -2.5 to 0, as said below
- w_in: bfloat16 [4096, 8192], P('seq', 'head'), may hold values from -0.09375 to 0.09375
Outputs:
- input_grad: bfloat16 [4096, 4096], P('seq', 'head')
- act_grad: bfloat16 [4096, 8192], P('seq', 'head')
- write_grad: float32 [4096, 128], P('seq')
- read_grad: float32 [4096, 128], P('seq')
The draws below stay inside these ranges and needn't reach their ends.
Inputs may be any that keep to these rules, and one draw needn't show every extreme that they name: `log_decay`: natural log of a decay factor of each head at each token; every entry is negative.
All inputs are finite; a program needn't handle non-finite values.
Results may differ from the reference program's by a relative error of at most 0.019.
Values may be sent and summed in bfloat16 or wider, within the bound.
No kernel may reach another device: no remote copies, remote signals or barrier semaphores. Data moves between devices by JAX's collectives and lax.ppermute only.
A program may use at most 192 MiB of HBM per device.

```python
import jax
import jax.numpy as jnp
from jax import lax

D = 4096
STATE_HEADS = 64
P_SIZE = 128
N = 128
SPAN = 256
TOK_DEV = 256
SEQUENCE_TOKENS = 4096
N_HEAD = 2


def draw_log_decay(key, part):
    key_slow, key_rate, key_block, key_token, pivotal_position, pivotal_loss = jax.random.split(key, 6)
    share = 0.5
    slow_heads = jax.random.uniform(key_slow, (STATE_HEADS,), jnp.float32) < share
    unit_draw = jax.random.uniform(key_rate, (STATE_HEADS,), jnp.float32)
    slow_rate = jnp.exp(jnp.log(0.1 / SEQUENCE_TOKENS) + unit_draw * jnp.log(6.0))
    fast_low = jnp.log(4.0 / SEQUENCE_TOKENS)
    fast_rate = jnp.exp(fast_low + unit_draw * (jnp.log(1.0 / 30.0) - fast_low))
    head_decay_rate = jnp.where(slow_heads, slow_rate, fast_rate)
    block_count = SEQUENCE_TOKENS // TOK_DEV
    block_multiplier = jnp.exp(jax.random.uniform(key_block, (block_count, STATE_HEADS), jnp.float32, -0.6931, 0.6931))
    block_multiplier = jnp.repeat(block_multiplier, TOK_DEV, axis=0)
    token_multiplier = jnp.exp(jax.random.uniform(key_token, (SEQUENCE_TOKENS, STATE_HEADS), jnp.float32, -0.6931, 0.6931))
    surge_positions = jax.random.randint(pivotal_position, (3,), 0, SEQUENCE_TOKENS)
    surge_losses = jnp.log(jax.random.uniform(pivotal_loss, (3, STATE_HEADS), jnp.float32, 0.5, 0.8))
    agreement_flags = jnp.arange(SEQUENCE_TOKENS)[:, None] == surge_positions[None, :]
    surge_events = jnp.sum(jnp.where(agreement_flags[:, :, None], surge_losses[None, :, :], 0.0), axis=1)
    return (surge_events - head_decay_rate[None, :] * block_multiplier * token_multiplier).astype(jnp.float32)


def with_spikes(values, rng, source, target, blocks, factor):
    def block_of(position):
        return (jnp.arange(values.shape[position]) // (values.shape[position] // blocks)).reshape((-1,) + (1,) * (values.ndim - 1 - position))

    near = jax.random.permutation(rng, blocks)[block_of(target)]
    second = (block_of(target) + blocks // 2) % blocks
    return jnp.where((block_of(source) == near) | (block_of(source) == second), factor * values, values)


def steps_of(key, extent, cuts, least, high):
    def one(axis_at, blocks):
        draws = jax.random.uniform(jax.random.fold_in(jax.random.fold_in(key, 6), axis_at), (blocks,), jnp.float32, least / len(cuts), high / len(cuts))
        return jnp.repeat(jnp.exp(draws), extent[axis_at] // blocks).reshape((-1,) + (1,) * (len(extent) - axis_at - 1))

    level = one(*cuts[0])
    for cut in cuts[1:]:
        level = level * one(*cut)
    return level


def scatter_about(own_key, extent, spread, reach, pieces=(), held_as=jnp.bfloat16):
    drawn = jax.random.normal(own_key, extent, jnp.float32) * spread
    if len(pieces) > 0:
        drawn = steps_of(own_key, extent, pieces, -0.22, 0.18) * drawn
    return jnp.clip(drawn, min=-reach, max=reach).astype(held_as)


def noise_with(rng, dims, scale, most, pieces, heavy, held_as=jnp.bfloat16):
    array = scale * jax.random.normal(rng, dims, jnp.float32)
    if pieces:
        array = array * steps_of(rng, dims, pieces, -0.22, 0.18)
    return jnp.clip(with_spikes(array, jax.random.fold_in(rng, 3), *heavy), -most, most).astype(held_as)


def setup_inputs(seed: int = 0) -> dict:
    key_of = jax.random.split(jax.random.key(seed), 7)
    inner_acts = scatter_about(key_of[0], (SEQUENCE_TOKENS, STATE_HEADS * P_SIZE), 0.03, 0.4375, ((0, 16), (1, 2)))
    out_grad = scatter_about(key_of[1], (SEQUENCE_TOKENS, STATE_HEADS * P_SIZE), 0.03, 0.4375, ((0, 16), (1, 2)))
    write_proj = scatter_about(key_of[2], (SEQUENCE_TOKENS, N), 0.2, 3.0, ((0, 16),))
    read_proj = scatter_about(key_of[3], (SEQUENCE_TOKENS, N), 0.2, 3.0, ((0, 16),))
    log_decay = draw_log_decay(jax.random.fold_in(key_of[6], 71), 0)
    w_in = noise_with(key_of[5], (D, STATE_HEADS * P_SIZE), (STATE_HEADS * P_SIZE) ** -0.5, 0.09375, ((0, 16), (1, 2)), (1, 0, 16, 2.0))
    return {"inner_acts": inner_acts, "out_grad": out_grad, "write_proj": write_proj, "read_proj": read_proj, "log_decay": log_decay, "w_in": w_in}


exact_mode = lax.Precision.HIGHEST


def decay_square(cumulative):
    count = cumulative.shape[0]
    by_head = cumulative.T
    spread_log = by_head[:, :, None] - by_head[:, None, :]
    below_diag = jnp.arange(count)[:, None] >= jnp.arange(count)[None, :]
    return jnp.exp(jnp.where(below_diag[None], spread_log, -jnp.inf))


def span_terms(act_span, grad_span, log_span):
    cumulative = jnp.cumsum(log_span, axis=0)
    decays = decay_square(cumulative)
    weighted = decays * jnp.einsum('ahp,bhp->hab', grad_span, act_span, precision=exact_mode)
    return cumulative, decays, weighted


def reference(inner_acts, out_grad, write_proj, read_proj, log_decay, w_in):
    blocks = SEQUENCE_TOKENS // SPAN
    act_blocks = inner_acts.astype(jnp.float32).reshape(blocks, SPAN, STATE_HEADS, P_SIZE)
    grad_blocks = out_grad.astype(jnp.float32).reshape(blocks, SPAN, STATE_HEADS, P_SIZE)
    write_blocks = write_proj.astype(jnp.float32).reshape(blocks, SPAN, N)
    read_blocks = read_proj.astype(jnp.float32).reshape(blocks, SPAN, N)
    log_blocks = log_decay.reshape(blocks, SPAN, STATE_HEADS)
    inputs = (act_blocks, grad_blocks, write_blocks, read_blocks, log_blocks)

    def forward(state_now, block):
        act_span, grad_span, write_span, read_span, log_span = block
        cumulative, decays, weighted = span_terms(act_span, grad_span, log_span)
        local_part = jnp.einsum('hab,bn->an', weighted, write_span, precision=exact_mode)
        carried = jnp.einsum('ahp,hpn->an', grad_span * jnp.exp(cumulative)[:, :, None], state_now, precision=exact_mode)
        tail_decay = jnp.exp(cumulative[-1][None, :] - cumulative)
        new_state = jnp.exp(cumulative[-1])[:, None, None] * state_now + jnp.einsum(
            'bhp,bn->hpn', act_span * tail_decay[:, :, None], write_span, precision=exact_mode)
        return new_state, local_part + carried

    start_state = jnp.zeros((STATE_HEADS, P_SIZE, N), jnp.float32)
    unused_state, read_parts = lax.scan(forward, start_state, inputs)

    def backward(carry_grad, block):
        act_span, grad_span, write_span, read_span, log_span = block
        cumulative, decays, weighted = span_terms(act_span, grad_span, log_span)
        tail_decay = jnp.exp(cumulative[-1][None, :] - cumulative)
        scores = jnp.einsum('an,bn->ab', read_span, write_span, precision=exact_mode)
        act_local = jnp.einsum('hab,ahp->bhp', decays * scores[None], grad_span, precision=exact_mode)
        act_carry = jnp.einsum('hpn,bn->bhp', carry_grad, write_span, precision=exact_mode) * tail_decay[:, :, None]
        write_local = jnp.einsum('hab,an->bn', weighted, read_span, precision=exact_mode)
        write_carry = jnp.einsum('bhp,hpn->bn', act_span * tail_decay[:, :, None], carry_grad, precision=exact_mode)
        new_grad = jnp.exp(cumulative[-1])[:, None, None] * carry_grad + jnp.einsum(
            'ahp,an->hpn', grad_span * jnp.exp(cumulative)[:, :, None], read_span, precision=exact_mode)
        return new_grad, (act_local + act_carry, write_local + write_carry)

    unused_grad, (act_parts, write_parts) = lax.scan(backward, start_state, inputs, reverse=True)
    act_grad = act_parts.reshape(SEQUENCE_TOKENS, STATE_HEADS * P_SIZE).astype(jnp.bfloat16)
    write_grad = write_parts.reshape(SEQUENCE_TOKENS, N)
    read_grad = read_parts.reshape(SEQUENCE_TOKENS, N)
    group_cols = (STATE_HEADS // N_HEAD) * P_SIZE
    summed = jnp.zeros((SEQUENCE_TOKENS, D), jnp.float32)
    for group_idx in range(N_HEAD):
        lower_col = group_idx * group_cols
        group_term = jnp.dot(act_grad[:, lower_col:lower_col + group_cols],
                             w_in[:, lower_col:lower_col + group_cols].T,
                             preferred_element_type=jnp.float32)
        summed = summed + lax.optimization_barrier(group_term.astype(jnp.bfloat16)).astype(jnp.float32)
    return summed.astype(jnp.bfloat16), act_grad, write_grad, read_grad
```

```python
import functools

import jax
import jax.numpy as jnp
from jax import lax
from jax.experimental import pallas as pl
from jax.experimental.pallas import tpu as pltpu
from jax.sharding import PartitionSpec as P

RING = 4
NT = (((1,), (1,)), ((), ()))
TN = (((0,), (0,)), ((), ()))
NN = (((1,), (0,)), ((), ()))


def mm(a, b, dims):
    return lax.dot_general(a, b, dims, preferred_element_type=jnp.float32)


def mm_exact(a, b, dims):
    return lax.dot_general(
        a, b, dims, precision=lax.Precision.HIGHEST, preferred_element_type=jnp.float32
    )


def spread(columns, width):
    rows = columns.shape[0]
    return jnp.concatenate(
        [jnp.broadcast_to(columns[:, h : h + 1], (rows, width)) for h in range(columns.shape[1])],
        axis=1,
    )


def own_kernel(heads, x, dy, b, c, cum, cum_t, ends, write_local, read_local, total):
    g = pl.program_id(0)
    rows = x.shape[0]
    half = rows // 2
    width = x.shape[1] // heads

    @pl.when(g == 0)
    def _():
        total[...] = jnp.zeros_like(total)

    col = cum[0]
    mid = col[half - 1 : half, :]
    last = col[rows - 1 : rows, :]
    later = lax.broadcasted_iota(jnp.int32, (half, half), 1) >= lax.broadcasted_iota(
        jnp.int32, (half, half), 0
    )
    for i in range(2):
        lo = i * half
        acc = jnp.zeros((half, half), jnp.float32)
        for h in range(heads):
            span = slice(h * width, (h + 1) * width)
            log = cum_t[0, h : h + 1, lo : lo + half] - col[lo : lo + half, h : h + 1]
            decay = jnp.exp(jnp.where(later, log, -jnp.inf))
            acc += decay * mm(x[lo : lo + half, span], dy[lo : lo + half, span], NT)
        total[lo : lo + half, lo : lo + half] += acc
    xf = x[...].astype(jnp.float32)
    early = (xf[:half] * spread(jnp.exp(mid - col[:half]), width)).astype(jnp.bfloat16)
    late = (
        dy[half:, :].astype(jnp.float32) * spread(jnp.exp(col[half:] - mid), width)
    ).astype(jnp.bfloat16)
    total[:half, half:] += mm(early, late, NT)
    tailed = (xf * spread(jnp.exp(last - col), width)).astype(jnp.bfloat16)
    ends[0] = mm(b[...], tailed, TN).astype(ends.dtype)

    @pl.when(g == pl.num_programs(0) - 1)
    def _():
        write_local[...] = mm_exact(total[...], c[...].astype(jnp.float32), NN)
        read_local[...] = mm_exact(total[...], b[...].astype(jnp.float32), TN)


def front_kernel(heads, top, bottom, c, cum, fronts):
    half = top.shape[0]
    width = top.shape[1] // heads
    decay = jnp.exp(cum[0])
    first = (top[...].astype(jnp.float32) * spread(decay[:half], width)).astype(jnp.bfloat16)
    second = (bottom[...].astype(jnp.float32) * spread(decay[half:], width)).astype(jnp.bfloat16)
    fronts[0] = (mm(c[:half], first, TN) + mm(c[half:], second, TN)).astype(fronts.dtype)


def act_kernel(heads, with_write, coef, top, bottom, b, c, cum, cum_t, *rest):
    if with_write:
        x, *rest = rest
    fronts, (carried, act, *rest) = rest[:RING], rest[RING:]
    g = pl.program_id(0)
    half = top.shape[0]
    rows = 2 * half
    width = top.shape[1] // heads
    col = cum[0]
    mid = col[half - 1 : half, :]
    last = col[rows - 1 : rows, :]
    tail = jnp.exp(last - col)
    later = lax.broadcasted_iota(jnp.int32, (half, half), 1) >= lax.broadcasted_iota(
        jnp.int32, (half, half), 0
    )
    pieces = []
    for h in range(heads):
        span = slice(h * width, (h + 1) * width)
        at = g * heads + h
        piece = carried[0, :, span].astype(jnp.float32) * coef[RING, at]
        for i in range(RING):
            piece += fronts[i][0, :, span].astype(jnp.float32) * coef[i, at]
        pieces.append(piece.astype(jnp.bfloat16))
    grads = jnp.concatenate(pieces, axis=1)
    carry = mm(b[...], grads, NN)
    scores = mm(b[...], c[...], NT)
    late = (
        bottom[...].astype(jnp.float32) * spread(jnp.exp(col[half:] - mid), width)
    ).astype(jnp.bfloat16)
    cross = mm(scores[:half, half:].astype(jnp.bfloat16), late, NN)
    to_mid = jnp.exp(mid - col[:half])
    for i, dy in enumerate((top, bottom)):
        lo = i * half
        score = scores[lo : lo + half, lo : lo + half]
        for h in range(heads):
            span = slice(h * width, (h + 1) * width)
            log = cum_t[0, h : h + 1, lo : lo + half] - col[lo : lo + half, h : h + 1]
            decay = jnp.exp(jnp.where(later, log, -jnp.inf))
            out = mm((decay * score).astype(jnp.bfloat16), dy[:, span], NN)
            out += carry[lo : lo + half, span] * tail[lo : lo + half, h : h + 1]
            if i == 0:
                out += cross[:, span] * to_mid[:, h : h + 1]
            act[lo : lo + half, span] = out.astype(act.dtype)
    if with_write:
        (write,) = rest
        tailed = (x[...].astype(jnp.float32) * spread(tail, width)).astype(jnp.bfloat16)

        @pl.when(g == 0)
        def _():
            write[...] = jnp.zeros_like(write)

        write[...] += mm(tailed, grads, NT)


def read_kernel(heads, quarter, coef, *refs):
    dys, refs = refs[: RING + 1], refs[RING + 1 :]
    cums, refs = refs[:RING], refs[RING:]
    ends, carried, out = refs[:RING], refs[RING], refs[RING + 1]
    rows = out.shape[1]
    width = carried.shape[1] // heads
    for j in range(RING):
        pieces = []
        for h in range(heads):
            span = slice(h * width, (h + 1) * width)
            piece = carried[:, span].astype(jnp.float32) * coef[j * (RING + 1) + RING, h]
            for i in range(RING):
                piece += ends[i][:, span].astype(jnp.float32) * coef[j * (RING + 1) + i, h]
            pieces.append(piece.astype(jnp.bfloat16))
        states = jnp.concatenate(pieces, axis=1)
        decay = spread(jnp.exp(cums[j][0]), width)
        if j < RING - 1:
            dy = (dys[j][...].astype(jnp.float32) * decay).astype(jnp.bfloat16)
            out[j] = mm(dy, states, NT).astype(out.dtype)
        else:
            half = rows // 2
            for i in range(2):
                at = slice(i * half, (i + 1) * half)
                dy = (dys[j + i][...].astype(jnp.float32) * decay[at]).astype(jnp.bfloat16)
                out[j, at] = mm(dy, states, NT).astype(out.dtype)


def product_kernel(*refs):
    acts, (w, out, total) = refs[:RING], refs[RING:]
    k = pl.program_id(0)
    for j in range(RING):
        part = mm(acts[j][...], w[...], NT)

        @pl.when(k == 0)
        def _():
            total[j] = part

        @pl.when(k > 0)
        def _():
            total[j] += part

    @pl.when(k == pl.num_programs(0) - 1)
    def _():
        out[...] = total[...].astype(out.dtype)


def params():
    return pltpu.CompilerParams(vmem_limit_bytes=48 * 2**20)


def cost(flops, size):
    return pl.CostEstimate(flops=int(flops), bytes_accessed=int(size), transcendentals=0)


def whole(shape):
    return pl.BlockSpec(shape, lambda g: (0,) * len(shape))


def local(x, dy, write_proj, read_proj, log_decay, w_in):
    rows, columns = x.shape
    half = rows // 2
    state_dim = write_proj.shape[1]
    n_heads = log_decay.shape[1]
    heads = n_heads // RING
    width = columns // n_heads
    part = heads * width
    n_seq, n_head = lax.axis_size("seq"), lax.axis_size("head")
    outer = n_seq // RING
    place = lax.axis_index("seq")
    p, z = place % RING, place // RING
    bf16, f32 = jnp.bfloat16, jnp.float32

    def swap(value, j):
        return lax.ppermute(value, "seq", [(s, s ^ j) for s in range(n_seq)])

    def along(value, d):
        return lax.ppermute(
            value, "seq", [(s, s + d * RING) for s in range(n_seq) if 0 <= s + d * RING < n_seq]
        )

    logs = [log_decay] + [swap(log_decay, j) for j in range(1, RING)]
    projections = jnp.concatenate([write_proj, read_proj], axis=1)
    projections = [projections] + [swap(projections, j) for j in range(1, RING)]
    dy_x, dy_y = swap(dy, 1), swap(dy, 2)
    dy_top, dy_bottom = swap(dy_x[:half], 2), swap(dy_y[half:], 1)
    turn = [(s, (s + RING) % n_seq) for s in range(n_seq)]
    w_blocks = [w_in]
    for _ in range(outer - 1):
        w_blocks.append(lax.ppermute(w_blocks[-1], "seq", turn))

    writes = [write_proj] + [v[:, :state_dim] for v in projections[1:]]
    reads = [read_proj] + [v[:, state_dim:] for v in projections[1:]]
    cums = jnp.cumsum(jnp.stack(logs), axis=1)
    totals = cums[:, -1, :]
    cum_groups = [cums[j].reshape(rows, RING, heads).swapaxes(0, 1) for j in range(RING)]
    cum_rows = [cums[j].T.reshape(RING, heads, rows) for j in range(RING)]

    order = p ^ jnp.arange(RING)

    def decay_over(mask):
        return jnp.exp(jnp.sum(jnp.where(mask[..., None], totals, 0.0), axis=-2))

    later = order[None, :] > order[:, None]
    between = later[:, None, :] & later.T[None, :, :]
    grad_coef = jnp.where(later[:, :, None], decay_over(between), 0.0)
    grad_coef = jnp.concatenate([grad_coef, decay_over(later)[:, None]], axis=1)
    state_coef = jnp.where(later.T[:, :, None], decay_over(between.swapaxes(0, 1)), 0.0)
    state_coef = jnp.concatenate([state_coef, decay_over(later.T)[:, None]], axis=1)
    front_weight, end_weight = decay_over(later.T), decay_over(later)
    ring_log = jnp.sum(totals, axis=0)

    def my_heads(value):
        return lax.dynamic_slice_in_dim(value, p * heads, heads, value.ndim - 1)

    group = lambda g: (0, g)
    group3 = lambda g: (g, 0, 0)
    by_group = pl.BlockSpec((rows, part), group)
    top_spec = pl.BlockSpec((half, part), group)
    low_spec = pl.BlockSpec((half, part), lambda g: (1, g))
    proj_spec = whole((rows, state_dim))
    cum_spec = pl.BlockSpec((1, rows, heads), group3)
    cum_row_spec = pl.BlockSpec((1, heads, rows), group3)
    state_spec = pl.BlockSpec((1, state_dim, part), group3)
    state_shape = jax.ShapeDtypeStruct((RING, state_dim, part), bf16)
    block_bytes = rows * columns * 2

    ends, write_local, read_local = pl.pallas_call(
        functools.partial(own_kernel, heads),
        grid=(RING,),
        in_specs=[by_group, by_group, proj_spec, proj_spec, cum_spec, cum_row_spec],
        out_specs=[state_spec, proj_spec, proj_spec],
        out_shape=[state_shape] + [jax.ShapeDtypeStruct((rows, state_dim), f32)] * 2,
        scratch_shapes=[pltpu.VMEM((rows, rows), f32)],
        compiler_params=params(),
        cost_estimate=cost(2 * rows * columns * 600, 3 * block_bytes),
        name="own_tokens",
    )(x, dy, write_proj, read_proj, cum_groups[0], cum_rows[0])

    blocks = [(dy, dy), (dy_x, dy_x), (dy_y, dy_y), (dy_top, dy_bottom)]
    specs = [(top_spec, low_spec)] * 3 + [(top_spec, top_spec)]
    fronts = [
        pl.pallas_call(
            functools.partial(front_kernel, heads),
            grid=(RING,),
            in_specs=[*specs[j], proj_spec, cum_spec],
            out_specs=state_spec,
            out_shape=state_shape,
            compiler_params=params(),
            cost_estimate=cost(2 * rows * columns * 128, 2 * block_bytes),
            name="fronts",
        )(*blocks[j], reads[j], cum_groups[j])
        for j in range(RING)
    ]

    def wide(values):
        return jnp.repeat(values, width, axis=-1)

    def scan_along(own, log, way):
        span, span_log = own, log
        result, result_log = None, None
        d = 1
        while d < outer:
            got = along(span.astype(bf16), way * d).astype(f32)
            got_log = along(span_log, way * d)
            if result is None:
                result, result_log = got, got_log
            else:
                result = result + wide(jnp.exp(result_log)) * got
                result_log = result_log + got_log
            span = span + wide(jnp.exp(span_log)) * got
            span_log = span_log + got_log
            d *= 2
        return result.astype(bf16)

    my_log = my_heads(ring_log)[None]
    my_front_weight, my_end_weight = my_heads(front_weight), my_heads(end_weight)

    def mine(value):
        return lax.dynamic_index_in_dim(value, p, 0, False)

    front_sum = sum(
        wide(my_front_weight[j])[None] * mine(fronts[j]).astype(f32) for j in range(RING)
    )
    grad_part = scan_along(front_sum, my_log, -1)
    grad_parts = jnp.stack([grad_part] + [swap(grad_part, j) for j in range(1, RING)])
    grad_in = jnp.take(grad_parts, order, axis=0)

    my_ends = [mine(ends)] + [
        swap(lax.dynamic_index_in_dim(ends, p ^ j, 0, False), j) for j in range(1, RING)
    ]
    end_sum = sum(wide(my_end_weight[j])[None] * my_ends[j].astype(f32) for j in range(RING))
    state_part = scan_along(end_sum, my_log, 1)

    acts = []
    for j in range(RING):
        extra = j == 0
        out = pl.pallas_call(
            functools.partial(act_kernel, heads, extra),
            grid=(RING,),
            in_specs=[pl.BlockSpec(memory_space=pltpu.SMEM)]
            + [*specs[j], proj_spec, proj_spec, cum_spec, cum_row_spec]
            + [by_group] * extra
            + [state_spec] * (RING + 1),
            out_specs=[by_group] + [proj_spec] * extra,
            out_shape=[jax.ShapeDtypeStruct((rows, columns), bf16)]
            + [jax.ShapeDtypeStruct((rows, state_dim), f32)] * extra,
            compiler_params=params(),
            cost_estimate=cost(2 * rows * columns * 600, 5 * block_bytes),
            name="act_grad",
        )(
            grad_coef[j],
            *blocks[j],
            writes[j],
            reads[j],
            cum_groups[j],
            cum_rows[j],
            *([x] * extra),
            *fronts,
            grad_in,
        )
        acts.append(out[0])
        if extra:
            write_carry = out[1]
    act_grad = acts[0]

    pick = lambda g, q: (0, q[0])
    pick3 = lambda g, q: (q[0], 0, 0)
    fixed2 = lambda g, q: (0, 0)
    read_parts = pl.pallas_call(
        functools.partial(read_kernel, heads),
        grid_spec=pltpu.PrefetchScalarGridSpec(
            num_scalar_prefetch=1,
            grid=(1,),
            in_specs=[pl.BlockSpec(memory_space=pltpu.SMEM)]
            + [pl.BlockSpec((rows, part), pick)] * 3
            + [pl.BlockSpec((half, part), pick)] * 2
            + [pl.BlockSpec((1, rows, heads), pick3)] * RING
            + [pl.BlockSpec((state_dim, part), fixed2)] * (RING + 1),
            out_specs=pl.BlockSpec((RING, rows, state_dim), lambda g, q: (0, 0, 0)),
        ),
        out_shape=jax.ShapeDtypeStruct((RING, rows, state_dim), bf16),
        compiler_params=params(),
        cost_estimate=cost(2 * rows * columns * 128, 2 * block_bytes),
        name="read_carry",
    )(
        p.astype(jnp.int32)[None],
        my_heads(state_coef).reshape(RING * (RING + 1), heads),
        dy,
        dy_x,
        dy_y,
        dy_top,
        dy_bottom,
        *cum_groups,
        *my_ends,
        state_part,
    )
    read_carry = read_parts[0].astype(f32) + sum(
        swap(read_parts[j], j).astype(f32) for j in range(1, RING)
    )

    both = jnp.stack([write_local + write_carry, read_local + read_carry])
    if n_head == 2:
        both = both + lax.ppermute(both, "head", [(0, 1), (1, 0)])
    else:
        both = lax.psum(both, "head")

    depth = min(512, columns)
    w_rows = w_in.shape[0]
    tiles = [
        pl.pallas_call(
            product_kernel,
            grid=(columns // depth,),
            in_specs=[pl.BlockSpec((rows, depth), group)] * RING
            + [pl.BlockSpec((w_rows, depth), group)],
            out_specs=whole((RING, rows, w_rows)),
            out_shape=jax.ShapeDtypeStruct((RING, rows, w_rows), bf16),
            scratch_shapes=[pltpu.VMEM((RING, rows, w_rows), f32)],
            compiler_params=params(),
            cost_estimate=cost(2 * RING * rows * columns * w_rows, 5 * block_bytes),
            name="product",
        )(*acts, w)
        for w in w_blocks
    ]
    tiles = jnp.stack(tiles)
    share = outer // n_head
    side = lax.axis_index("head")
    if n_head == 2:
        def of(h):
            return jnp.take(tiles, (z - (h * share + jnp.arange(share))) % outer, axis=0)

        got = lax.ppermute(of(1 - side), "head", [(0, 1), (1, 0)])
        summed = (of(side).astype(f32) + got.astype(f32)).astype(bf16)
    else:
        tiles = jnp.take(tiles, (z - jnp.arange(outer)) % outer, axis=0)
        summed = lax.psum_scatter(tiles, "head", scatter_dimension=0, tiled=True)
    columns_of = jnp.stack([summed[:, 0]] + [swap(summed[:, j], j) for j in range(1, RING)])
    columns_of = jnp.take(columns_of, order, axis=0)
    input_grad = columns_of.transpose(2, 1, 0, 3).reshape(rows, share * RING * w_rows)
    return (input_grad, act_grad, both[0], both[1])


def solution(mesh):
    return jax.shard_map(
        local,
        mesh=mesh,
        in_specs=(
            P("seq", "head"),
            P("seq", "head"),
            P("seq", None),
            P("seq", None),
            P("seq", "head"),
            P("seq", "head"),
        ),
        out_specs=(P("seq", "head"), P("seq", "head"), P("seq", None), P("seq", None)),
        check_vma=False,
    )
```

```python
import functools

import jax
import jax.numpy as jnp
from jax import lax
from jax.experimental import pallas as pl
from jax.experimental.pallas import tpu as pltpu
from jax.sharding import PartitionSpec as P

RING = 4
NT = (((1,), (1,)), ((), ()))
TN = (((0,), (0,)), ((), ()))
NN = (((1,), (0,)), ((), ()))


def mm(a, b, dims):
    return lax.dot_general(a, b, dims, preferred_element_type=jnp.float32)


def mm_exact(a, b, dims):
    return lax.dot_general(
        a, b, dims, precision=lax.Precision.HIGHEST, preferred_element_type=jnp.float32
    )


def spread(columns, width):
    rows = columns.shape[0]
    return jnp.concatenate(
        [jnp.broadcast_to(columns[:, h : h + 1], (rows, width)) for h in range(columns.shape[1])],
        axis=1,
    )


def own_kernel(heads, x, dy, b, c, cum, cum_t, ends, write_local, read_local, total):
    g = pl.program_id(0)
    rows = x.shape[0]
    half = rows // 2
    width = x.shape[1] // heads

    @pl.when(g == 0)
    def _():
        total[...] = jnp.zeros_like(total)

    col = cum[0]
    mid = col[half - 1 : half, :]
    last = col[rows - 1 : rows, :]
    later = lax.broadcasted_iota(jnp.int32, (half, half), 1) >= lax.broadcasted_iota(
        jnp.int32, (half, half), 0
    )
    for i in range(2):
        lo = i * half
        acc = jnp.zeros((half, half), jnp.float32)
        for h in range(heads):
            span = slice(h * width, (h + 1) * width)
            log = cum_t[0, h : h + 1, lo : lo + half] - col[lo : lo + half, h : h + 1]
            decay = jnp.exp(jnp.where(later, log, -jnp.inf))
            acc += decay * mm(x[lo : lo + half, span], dy[lo : lo + half, span], NT)
        total[lo : lo + half, lo : lo + half] += acc
    xf = x[...].astype(jnp.float32)
    early = (xf[:half] * spread(jnp.exp(mid - col[:half]), width)).astype(jnp.bfloat16)
    late = (
        dy[half:, :].astype(jnp.float32) * spread(jnp.exp(col[half:] - mid), width)
    ).astype(jnp.bfloat16)
    total[:half, half:] += mm(early, late, NT)
    tailed = (xf * spread(jnp.exp(last - col), width)).astype(jnp.bfloat16)
    ends[0] = mm(b[...], tailed, TN).astype(ends.dtype)

    @pl.when(g == pl.num_programs(0) - 1)
    def _():
        write_local[...] = mm_exact(total[...], c[...].astype(jnp.float32), NN)
        read_local[...] = mm_exact(total[...], b[...].astype(jnp.float32), TN)


def front_kernel(heads, top, bottom, c, cum, fronts):
    half = top.shape[0]
    width = top.shape[1] // heads
    decay = jnp.exp(cum[0])
    first = (top[...].astype(jnp.float32) * spread(decay[:half], width)).astype(jnp.bfloat16)
    second = (bottom[...].astype(jnp.float32) * spread(decay[half:], width)).astype(jnp.bfloat16)
    fronts[0] = (mm(c[:half], first, TN) + mm(c[half:], second, TN)).astype(fronts.dtype)


def local_act_kernel(heads, top, bottom, b, c, cum, cum_t, act):
    half = top.shape[0]
    width = top.shape[1] // heads
    col = cum[0]
    mid = col[half - 1 : half, :]
    later = lax.broadcasted_iota(jnp.int32, (half, half), 1) >= lax.broadcasted_iota(
        jnp.int32, (half, half), 0
    )
    scores = mm(b[...], c[...], NT)
    late = (
        bottom[...].astype(jnp.float32) * spread(jnp.exp(col[half:] - mid), width)
    ).astype(jnp.bfloat16)
    cross = mm(scores[:half, half:].astype(jnp.bfloat16), late, NN)
    to_mid = jnp.exp(mid - col[:half])
    for i, dy in enumerate((top, bottom)):
        lo = i * half
        score = scores[lo : lo + half, lo : lo + half]
        for h in range(heads):
            span = slice(h * width, (h + 1) * width)
            log = cum_t[0, h : h + 1, lo : lo + half] - col[lo : lo + half, h : h + 1]
            decay = jnp.exp(jnp.where(later, log, -jnp.inf))
            out = mm((decay * score).astype(jnp.bfloat16), dy[:, span], NN)
            if i == 0:
                out += cross[:, span] * to_mid[:, h : h + 1]
            act[lo : lo + half, span] = out.astype(act.dtype)


def ring_kernel(heads, coef, *refs):
    fronts, outs = refs[:RING], refs[RING:]
    g = pl.program_id(0)
    width = fronts[0].shape[2] // heads
    for h in range(heads):
        span = slice(h * width, (h + 1) * width)
        parts = [front[0, :, span].astype(jnp.float32) for front in fronts]
        for j in range(RING):
            total = sum(
                parts[i] * coef[j * (RING + 1) + i, g * heads + h] for i in range(RING) if i != j
            )
            outs[j][0, :, span] = total.astype(outs[j].dtype)


def finish_kernel(heads, at, coef, *refs):
    locals_, refs = refs[:RING], refs[RING:]
    rings, refs = refs[:RING], refs[RING:]
    quarters, refs = refs[:RING], refs[RING:]
    writes, refs = refs[:RING], refs[RING:]
    cums, (x, acts, own, write) = refs[:RING], refs[RING:]
    g = pl.program_id(0)
    rows = own.shape[0]
    width = own.shape[1] // heads
    source = lax.bitwise_xor(at[0], g)
    carried = quarters[0][...].astype(jnp.float32)
    for j in range(1, RING):
        carried = jnp.where(source == j, quarters[j][...].astype(jnp.float32), carried)
    for j in range(RING):
        col = cums[j][0]
        tail = jnp.exp(col[rows - 1 : rows, :] - col)
        grads = jnp.concatenate(
            [
                carried[:, h * width : (h + 1) * width] * coef[j * (RING + 1) + RING, g * heads + h]
                for h in range(heads)
            ],
            axis=1,
        )
        grads = (grads + rings[j][0].astype(jnp.float32)).astype(jnp.bfloat16)
        wide_tail = spread(tail, width)
        out = mm(writes[j][...], grads, NN) * wide_tail + locals_[j][...].astype(jnp.float32)
        out = out.astype(acts.dtype)
        acts[j * rows : (j + 1) * rows, :] = out
        if j == 0:
            own[...] = out
            tailed = (x[...].astype(jnp.float32) * wide_tail).astype(jnp.bfloat16)

            @pl.when(g == 0)
            def _():
                write[...] = jnp.zeros_like(write)

            write[...] += mm(tailed, grads, NT)


def read_kernel(heads, quarter, coef, *refs):
    dys, refs = refs[: RING + 1], refs[RING + 1 :]
    cums, refs = refs[:RING], refs[RING:]
    ends, carried, out = refs[:RING], refs[RING], refs[RING + 1]
    rows = out.shape[1]
    width = carried.shape[1] // heads
    for j in range(RING):
        pieces = []
        for h in range(heads):
            span = slice(h * width, (h + 1) * width)
            piece = carried[:, span].astype(jnp.float32) * coef[j * (RING + 1) + RING, h]
            for i in range(RING):
                piece += ends[i][:, span].astype(jnp.float32) * coef[j * (RING + 1) + i, h]
            pieces.append(piece.astype(jnp.bfloat16))
        states = jnp.concatenate(pieces, axis=1)
        decay = spread(jnp.exp(cums[j][0]), width)
        if j < RING - 1:
            dy = (dys[j][...].astype(jnp.float32) * decay).astype(jnp.bfloat16)
            out[j] = mm(dy, states, NT).astype(out.dtype)
        else:
            half = rows // 2
            for i in range(2):
                at = slice(i * half, (i + 1) * half)
                dy = (dys[j + i][...].astype(jnp.float32) * decay[at]).astype(jnp.bfloat16)
                out[j, at] = mm(dy, states, NT).astype(out.dtype)


def place_kernel(outer, share, at, *refs):
    blocks, out = refs[:-1], refs[-1]
    p, z, side = at[0], at[1], at[2]
    width = blocks[0].shape[1]
    for k in range(outer):
        o = lax.rem(z + k, outer)
        first = lax.rem(o, share) * RING

        @pl.when(lax.div(o, share) == side)
        def _():
            for j in range(RING):
                column = pl.multiple_of((first + lax.bitwise_xor(p, j)) * width, width)
                out[:, pl.ds(column, width)] = blocks[k * RING + j][...]


def params():
    return pltpu.CompilerParams(vmem_limit_bytes=48 * 2**20)


def cost(flops, size):
    return pl.CostEstimate(flops=0, bytes_accessed=0, transcendentals=0)


def whole(shape):
    return pl.BlockSpec(shape, lambda g: (0,) * len(shape))


def local(x, dy, write_proj, read_proj, log_decay, w_in):
    rows, columns = x.shape
    half = rows // 2
    state_dim = write_proj.shape[1]
    n_heads = log_decay.shape[1]
    heads = n_heads // RING
    width = columns // n_heads
    part = heads * width
    n_seq, n_head = lax.axis_size("seq"), lax.axis_size("head")
    outer = n_seq // RING
    place = lax.axis_index("seq")
    p, z = place % RING, place // RING
    bf16, f32 = jnp.bfloat16, jnp.float32

    def swap(value, j):
        return lax.ppermute(value, "seq", [(s, s ^ j) for s in range(n_seq)])

    def along(value, d):
        return lax.ppermute(
            value, "seq", [(s, s + d * RING) for s in range(n_seq) if 0 <= s + d * RING < n_seq]
        )

    first = lax.reduce_precision(log_decay, 8, 7)
    second = lax.reduce_precision(log_decay - first, 8, 7)
    third = log_decay - first - second
    payload = jnp.concatenate(
        [write_proj, read_proj] + [v.astype(bf16) for v in (first, second, third)], axis=1
    )
    payloads = [swap(payload, j) for j in range(1, RING)]
    turn = [(s, (s - RING) % n_seq) for s in range(n_seq)]
    w_blocks = [w_in]

    def turn_w():
        w_blocks.append(lax.ppermute(w_blocks[-1], "seq", turn))

    turn_w()
    dy_x, dy_y = swap(dy, 1), swap(dy, 2)
    dy_x, dy_y, w_blocks[-1] = lax.optimization_barrier((dy_x, dy_y, w_blocks[-1]))
    turn_w()
    dy_top, dy_bottom = swap(dy_x[:half], 2), swap(dy_y[half:], 1)

    writes = [write_proj] + [v[:, :state_dim] for v in payloads]
    reads = [read_proj] + [v[:, state_dim : 2 * state_dim] for v in payloads]
    logs = [log_decay]
    for v in payloads:
        parts = v[:, 2 * state_dim :].astype(f32).reshape(rows, 3, n_heads)
        logs.append(parts[:, 0] + parts[:, 1] + parts[:, 2])
    cums = jnp.cumsum(jnp.stack(logs), axis=1)
    totals = cums[:, -1, :]
    cum_groups = [cums[j].reshape(rows, RING, heads).swapaxes(0, 1) for j in range(RING)]
    cum_rows = [cums[j].T.reshape(RING, heads, rows) for j in range(RING)]

    order = p ^ jnp.arange(RING)

    def decay_over(mask):
        return jnp.exp(jnp.sum(jnp.where(mask[..., None], totals, 0.0), axis=-2))

    later = order[None, :] > order[:, None]
    between = later[:, None, :] & later.T[None, :, :]
    grad_coef = jnp.where(later[:, :, None], decay_over(between), 0.0)
    grad_coef = jnp.concatenate([grad_coef, decay_over(later)[:, None]], axis=1)
    state_coef = jnp.where(later.T[:, :, None], decay_over(between.swapaxes(0, 1)), 0.0)
    state_coef = jnp.concatenate([state_coef, decay_over(later.T)[:, None]], axis=1)
    front_weight, end_weight = decay_over(later.T), decay_over(later)
    ring_log = jnp.sum(totals, axis=0)

    def my_heads(value):
        return lax.dynamic_slice_in_dim(value, p * heads, heads, value.ndim - 1)

    group = lambda g: (0, g)
    group3 = lambda g: (g, 0, 0)
    by_group = pl.BlockSpec((rows, part), group)
    top_spec = pl.BlockSpec((half, part), group)
    low_spec = pl.BlockSpec((half, part), lambda g: (1, g))
    proj_spec = whole((rows, state_dim))
    cum_spec = pl.BlockSpec((1, rows, heads), group3)
    cum_row_spec = pl.BlockSpec((1, heads, rows), group3)
    state_spec = pl.BlockSpec((1, state_dim, part), group3)
    state_shape = jax.ShapeDtypeStruct((RING, state_dim, part), bf16)
    block_bytes = rows * columns * 2

    ends, write_local, read_local = pl.pallas_call(
        functools.partial(own_kernel, heads),
        grid=(RING,),
        in_specs=[by_group, by_group, proj_spec, proj_spec, cum_spec, cum_row_spec],
        out_specs=[state_spec, proj_spec, proj_spec],
        out_shape=[state_shape] + [jax.ShapeDtypeStruct((rows, state_dim), f32)] * 2,
        scratch_shapes=[pltpu.VMEM((rows, rows), f32)],
        compiler_params=params(),
        cost_estimate=cost(2 * rows * columns * 600, 3 * block_bytes),
        name="own_tokens",
    )(x, dy, write_proj, read_proj, cum_groups[0], cum_rows[0])

    blocks = [(dy, dy), (dy_x, dy_x), (dy_y, dy_y), (dy_top, dy_bottom)]
    specs = [(top_spec, low_spec)] * 3 + [(top_spec, top_spec)]
    def local_act(j):
        return pl.pallas_call(
            functools.partial(local_act_kernel, heads),
            grid=(RING,),
            in_specs=[*specs[j], proj_spec, proj_spec, cum_spec, cum_row_spec],
            out_specs=by_group,
            out_shape=jax.ShapeDtypeStruct((rows, columns), bf16),
            compiler_params=params(),
            cost_estimate=cost(2 * rows * columns * 600, 5 * block_bytes),
            name="local_act",
        )(*blocks[j], writes[j], reads[j], cum_groups[j], cum_rows[j])

    local_acts = [local_act(j) for j in range(RING - 1)]
    *local_acts, dy_top, dy_bottom = lax.optimization_barrier((*local_acts, dy_top, dy_bottom))
    blocks[-1] = (dy_top, dy_bottom)
    local_acts.append(local_act(RING - 1))
    fronts = [
        pl.pallas_call(
            functools.partial(front_kernel, heads),
            grid=(RING,),
            in_specs=[*specs[j], proj_spec, cum_spec],
            out_specs=state_spec,
            out_shape=state_shape,
            compiler_params=params(),
            cost_estimate=cost(2 * rows * columns * 128, 2 * block_bytes),
            name="fronts",
        )(*blocks[j], reads[j], cum_groups[j])
        for j in range(RING)
    ]

    def wide(values):
        return jnp.repeat(values, width, axis=-1)

    def scan_along(own, log, way):
        span, span_log = own, log
        result, result_log = None, None
        d = 1
        while d < outer:
            first = lax.reduce_precision(span_log, 8, 7)
            second = lax.reduce_precision(span_log - first, 8, 7)
            tail = jnp.concatenate([first, second, span_log - first - second], axis=0)
            tail = jnp.pad(wide(tail), ((0, 13), (0, 0)))
            got = along(jnp.concatenate([span, tail], axis=0).astype(bf16), way * d).astype(f32)
            got_log = jnp.sum(got[state_dim : state_dim + 3, ::width], axis=0, keepdims=True)
            got = got[:state_dim]
            if result is None:
                result, result_log = got, got_log
            else:
                result = result + wide(jnp.exp(result_log)) * got
                result_log = result_log + got_log
            span = span + wide(jnp.exp(span_log)) * got
            span_log = span_log + got_log
            d *= 2
        return result.astype(bf16)

    my_log = my_heads(ring_log)[None]
    my_front_weight, my_end_weight = my_heads(front_weight), my_heads(end_weight)

    def mine(value):
        return lax.dynamic_index_in_dim(value, p, 0, False)

    front_sum = sum(
        wide(my_front_weight[j])[None] * mine(fronts[j]).astype(f32) for j in range(RING)
    )
    front_sum, w_blocks[-1] = lax.optimization_barrier((front_sum, w_blocks[-1]))
    while len(w_blocks) < outer:
        turn_w()
    grad_part = scan_along(front_sum, my_log, -1)
    my_ends = [mine(ends)] + [
        swap(lax.dynamic_index_in_dim(ends, p ^ j, 0, False), j) for j in range(1, RING)
    ]
    end_sum = sum(wide(my_end_weight[j])[None] * my_ends[j].astype(f32) for j in range(RING))
    end_sum, grad_part = lax.optimization_barrier((end_sum, grad_part))
    state_part = scan_along(end_sum, my_log, 1)

    grad_parts = [grad_part] + [swap(grad_part, j) for j in range(1, RING)]

    coef_flat = grad_coef.reshape(RING * (RING + 1), n_heads)
    ring_grads = pl.pallas_call(
        functools.partial(ring_kernel, heads),
        grid=(RING,),
        in_specs=[pl.BlockSpec(memory_space=pltpu.SMEM)] + [state_spec] * RING,
        out_specs=[state_spec] * RING,
        out_shape=[state_shape] * RING,
        compiler_params=params(),
        cost_estimate=cost(2 * rows * columns * 16, 4 * block_bytes),
        name="ring_grads",
    )(coef_flat, *fronts)
    acts, act_grad, write_carry = pl.pallas_call(
        functools.partial(finish_kernel, heads),
        grid=(RING,),
        in_specs=[pl.BlockSpec(memory_space=pltpu.SMEM)] * 2
        + [by_group] * RING
        + [state_spec] * RING
        + [whole((state_dim, part))] * RING
        + [proj_spec] * RING
        + [cum_spec] * RING
        + [by_group],
        out_specs=[pl.BlockSpec((RING * rows, part), group), by_group, proj_spec],
        out_shape=[
            jax.ShapeDtypeStruct((RING * rows, columns), bf16),
            jax.ShapeDtypeStruct((rows, columns), bf16),
            jax.ShapeDtypeStruct((rows, state_dim), f32),
        ],
        compiler_params=params(),
        cost_estimate=cost(2 * rows * columns * 600, 10 * block_bytes),
        name="finish_act",
    )(
        p.astype(jnp.int32)[None],
        coef_flat,
        *local_acts,
        *ring_grads,
        *grad_parts,
        *writes,
        *cum_groups,
        x,
    )

    pick = lambda g, q: (0, q[0])
    pick3 = lambda g, q: (q[0], 0, 0)
    fixed2 = lambda g, q: (0, 0)
    read_parts = pl.pallas_call(
        functools.partial(read_kernel, heads),
        grid_spec=pltpu.PrefetchScalarGridSpec(
            num_scalar_prefetch=1,
            grid=(1,),
            in_specs=[pl.BlockSpec(memory_space=pltpu.SMEM)]
            + [pl.BlockSpec((rows, part), pick)] * 3
            + [pl.BlockSpec((half, part), pick)] * 2
            + [pl.BlockSpec((1, rows, heads), pick3)] * RING
            + [pl.BlockSpec((state_dim, part), fixed2)] * (RING + 1),
            out_specs=pl.BlockSpec((RING, rows, state_dim), lambda g, q: (0, 0, 0)),
        ),
        out_shape=jax.ShapeDtypeStruct((RING, rows, state_dim), bf16),
        compiler_params=params(),
        cost_estimate=cost(2 * rows * columns * 128, 2 * block_bytes),
        name="read_carry",
    )(
        p.astype(jnp.int32)[None],
        my_heads(state_coef).reshape(RING * (RING + 1), heads),
        dy,
        dy_x,
        dy_y,
        dy_top,
        dy_bottom,
        *cum_groups,
        *my_ends,
        state_part,
    )
    read_carry = read_parts[0].astype(f32) + sum(
        swap(read_parts[j], j).astype(f32) for j in range(1, RING)
    )

    both = jnp.stack([write_local + write_carry, read_local + read_carry])
    if n_head == 2:
        both = both + lax.ppermute(both, "head", [(0, 1), (1, 0)])
    else:
        both = lax.psum(both, "head")

    w_rows = w_in.shape[0]
    share = outer // n_head
    side = lax.axis_index("head")
    tiles = [mm(acts, w, NT).astype(bf16) for w in w_blocks[:-1]]

    def over_head(tile):
        if n_head == 2:
            got = lax.ppermute(tile, "head", [(0, 1), (1, 0)])
            return (tile.astype(f32) + got.astype(f32)).astype(bf16)
        return lax.psum(tile.astype(f32), "head").astype(bf16)

    def to_owners(tile):
        return [tile[:rows]] + [swap(tile[j * rows : (j + 1) * rows], j) for j in range(1, RING)]

    early = over_head(jnp.concatenate(tiles, axis=1))
    early, w_blocks[-1] = lax.optimization_barrier((early, w_blocks[-1]))
    late = to_owners(over_head(mm(acts, w_blocks[-1], NT).astype(bf16)))
    early = to_owners(early)
    pieces = [
        early[j][:, k * w_rows : (k + 1) * w_rows] for k in range(outer - 1) for j in range(RING)
    ] + late
    if w_rows % 128 == 0:
        input_grad = pl.pallas_call(
            functools.partial(place_kernel, outer, share),
            in_specs=[pl.BlockSpec(memory_space=pltpu.SMEM)]
            + [pl.BlockSpec(memory_space=pltpu.VMEM)] * (outer * RING),
            out_specs=pl.BlockSpec(memory_space=pltpu.VMEM),
            out_shape=jax.ShapeDtypeStruct((rows, share * RING * w_rows), bf16),
            compiler_params=params(),
            name="place",
        )(jnp.stack([p, z, side]).astype(jnp.int32), *pieces)
    else:
        pieces = jnp.stack(pieces).reshape(outer, RING, rows, w_rows)
        pieces = jnp.take(pieces, (side * share + jnp.arange(share) - z) % outer, axis=0)
        pieces = jnp.take(pieces, order, axis=1)
        input_grad = pieces.transpose(2, 0, 1, 3).reshape(rows, share * RING * w_rows)
    return (input_grad, act_grad, both[0], both[1])


def solution(mesh):
    return jax.shard_map(
        local,
        mesh=mesh,
        in_specs=(
            P("seq", "head"),
            P("seq", "head"),
            P("seq", None),
            P("seq", None),
            P("seq", "head"),
            P("seq", "head"),
        ),
        out_specs=(P("seq", "head"), P("seq", "head"), P("seq", None), P("seq", None)),
        check_vma=False,
    )
```

```python
import functools

import jax
import jax.numpy as jnp
from jax import lax
from jax.experimental import pallas as pl
from jax.experimental.pallas import tpu as pltpu
from jax.sharding import PartitionSpec as P

RING = 4
LANES = 128
EXTRA = 16
NT = (((1,), (1,)), ((), ()))
TN = (((0,), (0,)), ((), ()))
NN = (((1,), (0,)), ((), ()))
bf16, f32 = jnp.bfloat16, jnp.float32


def mm(a, b, dims):
    return lax.dot_general(a, b, dims, preferred_element_type=f32)


def mm_exact(a, b, dims):
    return lax.dot_general(a, b, dims, precision=lax.Precision.HIGHEST, preferred_element_type=f32)


def spread(columns, width):
    rows = columns.shape[0]
    return jnp.concatenate(
        [jnp.broadcast_to(columns[:, h : h + 1], (rows, width)) for h in range(columns.shape[1])],
        axis=1,
    )


def iota(shape, axis):
    return lax.broadcasted_iota(jnp.int32, shape, axis)


def three_parts(value):
    first = value.astype(bf16).astype(f32)
    second = (value - first).astype(bf16).astype(f32)
    return first, second, value - first - second


def cumulate(n_heads, log_tiles, cum, cum_t):
    parts = jnp.concatenate([tile[...] for tile in log_tiles], axis=0)
    rows = parts.shape[0]
    source, head = iota((LANES, LANES), 0), iota((LANES, LANES), 1)
    pick = (source < 3 * n_heads) & (lax.rem(source, n_heads) == head)
    logs = mm(parts, pick.astype(f32).astype(bf16), NN)
    upto = (iota((rows, rows), 0) <= iota((rows, rows), 1)).astype(f32)
    cum[...] = mm_exact(upto, logs, TN)
    if cum_t is not None:
        cum_t[...] = mm_exact(logs, upto, TN)


def group_of(value, g, heads, axis):
    shift = lax.rem(LANES - g * heads, LANES)
    value = pltpu.roll(value, shift, axis)
    return value[:, :heads] if axis == 1 else value[:heads]


def diagonal(heads, half, lo, col, row, each):
    later = iota((half, half), 1) >= iota((half, half), 0)
    for h in range(heads):
        log = row[h : h + 1, lo : lo + half] - col[lo : lo + half, h : h + 1]
        each(h, jnp.exp(jnp.where(later, log, -jnp.inf)))


def own_kernel(n_heads, at, x, top, bottom, b, c, log_top, log_bottom, *refs):
    ends, (write_local, read_local, total, cum, cum_t) = refs[:RING], refs[RING:]
    g = pl.program_id(0)
    heads = n_heads // RING
    rows = x.shape[0]
    half = rows // 2
    width = x.shape[1] // heads

    @pl.when(g == 0)
    def _():
        total[...] = jnp.zeros_like(total)
        cumulate(n_heads, (log_top, log_bottom), cum, cum_t)

    col, row = group_of(cum[...], g, heads, 1), group_of(cum_t[...], g, heads, 0)
    mid, last = col[half - 1 : half, :], col[rows - 1 : rows, :]
    for i, dy in enumerate((top, bottom)):
        lo = i * half
        parts = []

        def add(h, decay):
            span = slice(h * width, (h + 1) * width)
            parts.append(decay * mm(x[lo : lo + half, span], dy[:, span], NT))

        diagonal(heads, half, lo, col, row, add)
        total[lo : lo + half, lo : lo + half] += sum(parts)
    xf = x[...].astype(f32)
    early = (xf[:half] * spread(jnp.exp(mid - col[:half]), width)).astype(bf16)
    late = (bottom[...].astype(f32) * spread(jnp.exp(col[half:] - mid), width)).astype(bf16)
    total[:half, half:] += mm(early, late, NT)
    tailed = (xf * spread(jnp.exp(last - col), width)).astype(bf16)
    mine = mm(b[...], tailed, TN).astype(bf16)
    for j in range(RING):

        @pl.when(lax.bitwise_xor(at[0], g) == j)
        def _():
            ends[j][...] = mine

    @pl.when(g == pl.num_programs(0) - 1)
    def _():
        write_local[...] = mm_exact(total[...], c[...].astype(f32), NN)
        read_local[...] = mm_exact(total[...], b[...].astype(f32), TN)


def block_kernel(n_heads, top, bottom, *refs):
    tiles, (act, fronts, log_row, cum_out, cum_t) = refs[:6], refs[6:]
    b = jnp.concatenate([tiles[0][...], tiles[1][...]], axis=0)
    c = jnp.concatenate([tiles[2][...], tiles[3][...]], axis=0)
    g = pl.program_id(0)
    heads = n_heads // RING
    half = top.shape[0]
    rows = 2 * half
    width = top.shape[1] // heads

    @pl.when(g == 0)
    def _():
        cumulate(n_heads, tiles[4:], cum_out, cum_t)

    col, row = group_of(cum_out[...], g, heads, 1), group_of(cum_t[...], g, heads, 0)
    mid, last = col[half - 1 : half, :], col[rows - 1 : rows, :]
    log_row[...] = spread(last, width)
    scores = mm(b, c, NT)
    late_f = bottom[...].astype(f32) * spread(jnp.exp(col[half:] - mid), width)
    late = late_f.astype(bf16)
    first = (top[...].astype(f32) * spread(jnp.exp(col[:half]), width)).astype(bf16)
    second = (late_f * spread(jnp.exp(mid), width)).astype(bf16)
    fronts[0] = (mm(c[:half], first, TN) + mm(c[half:], second, TN)).astype(bf16)
    cross = mm(scores[:half, half:].astype(bf16), late, NN)
    to_mid = jnp.exp(mid - col[:half])
    for i, dy in enumerate((top, bottom)):
        lo = i * half
        score = scores[lo : lo + half, lo : lo + half]

        def put(h, decay):
            span = slice(h * width, (h + 1) * width)
            out = mm((decay * score).astype(bf16), dy[:, span], NN)
            if i == 0:
                out += cross[:, span] * to_mid[:, h : h + 1]
            act[lo : lo + half, span] = out.astype(act.dtype)

        diagonal(heads, half, lo, col, row, put)


def log_over(p, logs, wanted):
    total = jnp.zeros_like(logs[0])
    for k in range(RING):
        total += jnp.where(wanted(lax.bitwise_xor(p, k)), logs[k], 0.0)
    return total


def combine_kernel(way, at, *refs):
    parts, logs, out = refs[:RING], [r[...] for r in refs[RING : 2 * RING]], refs[2 * RING]
    p = at[0]
    n = out.shape[0] - EXTRA
    total = 0.0
    for j in range(RING):
        own = lax.bitwise_xor(p, j)
        if way == 1:
            weight = jnp.exp(log_over(p, logs, lambda k: k > own))
        else:
            weight = jnp.exp(log_over(p, logs, lambda k: k < own))
        part = parts[j][0] if len(parts[j].shape) == 3 else parts[j][...]
        total += part.astype(f32) * weight
    out[:n] = total.astype(bf16)
    write_log(out, sum(logs))


def write_log(out, log):
    n, width = out.shape
    row = iota((EXTRA, width), 0)
    rows = jnp.zeros((EXTRA, width), f32)
    for i, part in enumerate(three_parts(log)):
        rows = jnp.where(row == i, part, rows)
    out[n - EXTRA :] = rows.astype(bf16)


def log_of(message):
    n = message.shape[0] - EXTRA
    tail = message[n:].astype(f32)
    return tail[0:1] + tail[1:2] + tail[2:3]


def merge_kernel(near, far, out):
    n = near.shape[0] - EXTRA
    log = log_of(near)
    out[:n] = (near[:n].astype(f32) + far[:n].astype(f32) * jnp.exp(log)).astype(bf16)
    write_log(out, log + log_of(far))


def ring_kernel(at, *refs):
    fronts, logs, outs = refs[:RING], [r[...] for r in refs[RING : 2 * RING]], refs[2 * RING :]
    p = at[0]
    for j in range(RING):
        own = lax.bitwise_xor(p, j)
        total = 0.0
        for i in range(RING):
            if i != j:
                there = lax.bitwise_xor(p, i)
                weight = jnp.exp(log_over(p, logs, lambda k: (k > own) & (k < there)))
                total += fronts[i][0].astype(f32) * jnp.where(there > own, weight, 0.0)
        outs[j][0] = total.astype(bf16)


def finish_kernel(n_heads, n_w, at, *refs):
    locals_, refs = refs[:RING], refs[RING:]
    rings, refs = refs[:RING], refs[RING:]
    quarters, refs = refs[:RING], refs[RING:]
    logs, refs = [r[...] for r in refs[:RING]], refs[RING:]
    tops, refs = refs[:RING], refs[RING:]
    bottoms, refs = refs[:RING], refs[RING:]
    cums, refs = refs[:RING], refs[RING:]
    w, refs = refs[:n_w], refs[n_w:]
    x, acts, own, write, tiles, total = refs
    g, p = pl.program_id(0), at[0]
    heads = n_heads // RING
    rows = own.shape[0]
    width = own.shape[1] // heads
    n = quarters[0].shape[0] - EXTRA
    source = lax.bitwise_xor(p, g)
    carried = quarters[0][:n].astype(f32)
    for j in range(1, RING):
        carried = jnp.where(source == j, quarters[j][:n].astype(f32), carried)

    @pl.when(g == 0)
    def _():
        write[...] = jnp.zeros_like(write)
        total[...] = jnp.zeros_like(total)

    for j in range(RING):
        col = group_of(cums[j][...], g, heads, 1)
        tail = spread(jnp.exp(col[rows - 1 : rows, :] - col), width)
        place = lax.bitwise_xor(p, j)
        weight = jnp.exp(log_over(p, logs, lambda k: k > place))
        grads = (carried * weight + rings[j][0].astype(f32)).astype(bf16)
        b = jnp.concatenate([tops[j][...], bottoms[j][...]], axis=0)
        out = mm(b, grads, NN) * tail + locals_[j][...].astype(f32)
        out = out.astype(acts.dtype)
        acts[j * rows : (j + 1) * rows, :] = out
        if j == 0:
            own[...] = out
            write[...] += mm((x[...].astype(f32) * tail).astype(bf16), grads, NT)
    for k in range(n_w):
        n_rows = w[k].shape[0]
        total[:, k * n_rows : (k + 1) * n_rows] += mm(acts[...], w[k][...], NT)

    @pl.when(g == pl.num_programs(0) - 1)
    def _():
        tiles[...] = total[...].astype(tiles.dtype)


def read_kernel(n_heads, at, *refs):
    tops, refs = refs[:RING], refs[RING:]
    bottoms, refs = refs[:RING], refs[RING:]
    cums, refs = refs[:RING], refs[RING:]
    logs, refs = [r[...] for r in refs[:RING]], refs[RING:]
    ends, (carried, *outs) = refs[:RING], refs[RING:]
    p = at[0]
    heads = n_heads // RING
    half = tops[0].shape[0]
    n = carried.shape[0] - EXTRA
    width = carried.shape[1] // heads
    for j in range(RING):
        own = lax.bitwise_xor(p, j)
        total = carried[:n].astype(f32) * jnp.exp(log_over(p, logs, lambda k: k < own))
        for i in range(RING):
            if i != j:
                there = lax.bitwise_xor(p, i)
                weight = jnp.exp(log_over(p, logs, lambda k: (k < own) & (k > there)))
                total += ends[i][...].astype(f32) * jnp.where(there < own, weight, 0.0)
        states = total.astype(bf16)
        decay = spread(jnp.exp(group_of(cums[j][...], p, heads, 1)), width)
        for i, dy in enumerate((tops[j], bottoms[j])):
            at_rows = slice(i * half, (i + 1) * half)
            scaled = (dy[...].astype(f32) * decay[at_rows]).astype(bf16)
            outs[j][at_rows] = mm(scaled, states, NT).astype(bf16)


def place_kernel(outer, share, at, *refs):
    blocks, out = refs[:-1], refs[-1]
    p, z, side = at[0], at[1], at[2]
    width = out.shape[1] // (share * RING)
    for k in range(outer):
        o = lax.rem(z + k, outer)
        first = lax.rem(o, share) * RING

        @pl.when(lax.div(o, share) == side)
        def _():
            for j in range(RING):
                column = pl.multiple_of((first + lax.bitwise_xor(p, j)) * width, width)
                if k < outer - 1:
                    out[:, pl.ds(column, width)] = blocks[j][:, k * width : (k + 1) * width]
                else:
                    out[:, pl.ds(column, width)] = blocks[RING + j][...]


def call(kernel, name, grid, in_specs, out_specs, out_shape, scratch=(), prefetch=1):
    return pl.pallas_call(
        kernel,
        grid_spec=pltpu.PrefetchScalarGridSpec(
            num_scalar_prefetch=prefetch,
            grid=grid,
            in_specs=in_specs,
            out_specs=out_specs,
            scratch_shapes=list(scratch),
        ),
        out_shape=out_shape,
        compiler_params=pltpu.CompilerParams(vmem_limit_bytes=56 * 2**20),
        cost_estimate=pl.CostEstimate(flops=0, bytes_accessed=0, transcendentals=0),
        name=name,
    )


def local(x, dy, write_proj, read_proj, log_decay, w_in):
    rows, columns = x.shape
    half = rows // 2
    state_dim = write_proj.shape[1]
    n_heads = log_decay.shape[1]
    heads = n_heads // RING
    width = columns // n_heads
    part = heads * width
    w_rows = w_in.shape[0]
    n_seq, n_head = lax.axis_size("seq"), lax.axis_size("head")
    outer = n_seq // RING
    place = lax.axis_index("seq")
    side = lax.axis_index("head")
    p, z = place % RING, place // RING
    at = p.astype(jnp.int32)[None]

    def swap(value, j):
        return lax.ppermute(value, "seq", [(s, s ^ j) for s in range(n_seq)])

    def along(value, d):
        return lax.ppermute(
            value, "seq", [(s, s + d * RING) for s in range(n_seq) if 0 <= s + d * RING < n_seq]
        )

    w_blocks = [w_in]

    def turn_w():
        turn = [(s, (s - RING) % n_seq) for s in range(n_seq)]
        w_blocks.append(lax.ppermute(w_blocks[-1], "seq", turn))

    turn_w()

    first = lax.reduce_precision(log_decay, 8, 7)
    second = lax.reduce_precision(log_decay - first, 8, 7)
    third = log_decay - first - second
    fill = jnp.zeros((rows, LANES - 3 * n_heads), bf16)
    beside = [write_proj, read_proj] + [v.astype(bf16) for v in (first, second, third)] + [fill]
    own_top = jnp.concatenate([v[:half] for v in [dy] + beside], axis=1)
    own_bottom = jnp.concatenate([v[half:] for v in [dy] + beside], axis=1)
    x_top, y_bottom = swap(own_top, 1), swap(own_bottom, 2)
    x_bottom, y_top = swap(own_bottom, 1), swap(own_top, 2)
    x_top, x_bottom, y_top, y_bottom = lax.optimization_barrier((x_top, x_bottom, y_top, y_bottom))
    blocks = [
        (own_top, own_bottom),
        (x_top, x_bottom),
        (y_top, y_bottom),
        (swap(x_top, 2), swap(y_bottom, 1)),
    ]

    half_spec = pl.BlockSpec((half, part), lambda g, q: (0, g))
    first_tile = columns // LANES

    def tile_spec(i):
        return pl.BlockSpec((half, LANES), lambda g, q: (0, first_tile + i))

    def const(*shape):
        return pl.BlockSpec(shape, lambda g, q: (0,) * len(shape))

    by_group = pl.BlockSpec((rows, part), lambda g, q: (0, g))
    state_spec = pl.BlockSpec((1, state_dim, part), lambda g, q: (g, 0, 0))
    log_spec = pl.BlockSpec((1, part), lambda g, q: (0, g))
    cum_spec = const(rows, LANES)
    proj_spec = const(rows, state_dim)
    message_spec = const(state_dim + EXTRA, part)
    shape = jax.ShapeDtypeStruct
    state_shape = shape((RING, state_dim, part), bf16)
    log_shape = shape((1, columns), f32)
    cum_shape = shape((rows, LANES), f32)
    message_shape = shape((state_dim + EXTRA, part), bf16)
    cum_scratch, cum_t_scratch = pltpu.VMEM((rows, LANES), f32), pltpu.VMEM((LANES, rows), f32)

    *ends, write_local, read_local = call(
        functools.partial(own_kernel, n_heads),
        "own_tokens",
        (RING,),
        [by_group, half_spec, half_spec, proj_spec, proj_spec, tile_spec(2), tile_spec(2)],
        [const(state_dim, part)] * RING + [proj_spec] * 2,
        [shape((state_dim, part), bf16)] * RING + [shape((rows, state_dim), f32)] * 2,
        [pltpu.VMEM((rows, rows), f32), cum_scratch, cum_t_scratch],
    )(at, x, own_top, own_bottom, write_proj, read_proj, own_top, own_bottom)

    def block(j):
        top, bottom = blocks[j]
        return call(
            functools.partial(lambda *refs: block_kernel(n_heads, *refs[1:])),
            "tokens",
            (RING,),
            [half_spec, half_spec] + [tile_spec(i) for i in range(3) for _ in range(2)],
            [by_group, state_spec, log_spec, cum_spec],
            [shape((rows, columns), bf16), state_shape, log_shape, cum_shape],
            [cum_t_scratch],
        )(at, top, bottom, *([top, bottom] * 3))

    results = [block(0)]
    logs = [results[0][2]]
    logs[0], read_local, w_blocks[-1] = lax.optimization_barrier(
        (logs[0], read_local, w_blocks[-1])
    )
    results += [block(j) for j in range(1, RING - 1)]
    logs += [v[2] for v in results[1:]]
    logs, blocks[-1] = lax.optimization_barrier((logs, blocks[-1]))
    results.append(block(RING - 1))
    logs.append(results[-1][2])
    local_acts, fronts, _, cums = zip(*results)

    mine3 = pl.BlockSpec((1, state_dim, part), lambda g, q: (q[0], 0, 0))
    mine_log = pl.BlockSpec((1, part), lambda g, q: (0, q[0]))

    def combine(parts, way):
        return call(
            functools.partial(combine_kernel, way),
            "message",
            (1,),
            [mine3 if v.ndim == 3 else const(*v.shape) for v in parts] + [mine_log] * RING,
            message_spec,
            message_shape,
        )(at, *parts, *logs)

    def merge(near, far):
        return call(
            lambda q, *refs: merge_kernel(*refs),
            "merge",
            (1,),
            [message_spec] * 2,
            message_spec,
            message_shape,
        )(at, near, far)

    fronts = list(fronts)
    while len(w_blocks) < min(3, outer):
        turn_w()
    fronts[-1], w_blocks[-1] = lax.optimization_barrier((fronts[-1], w_blocks[-1]))
    while len(w_blocks) < outer:
        turn_w()

    def scan_along(span, way, after=None):
        result, d = None, 1
        while d < outer:
            got = along(span, way * d)
            if after is not None:
                got = after(got)
            result = got if result is None else merge(result, got)
            if 2 * d < outer:
                span = merge(span, got)
            d *= 2
        return result

    grad_part = scan_along(combine(fronts, -1), -1)
    grad_parts = [grad_part] + [swap(grad_part, j) for j in range(1, RING)]

    ring_grads = call(
        ring_kernel,
        "ring_grads",
        (RING,),
        [state_spec] * RING + [log_spec] * RING,
        [state_spec] * RING,
        [state_shape] * RING,
    )(at, *fronts, *logs)

    n_w = outer - 1
    tall = pl.BlockSpec((RING * rows, part), lambda g, q: (0, g))
    w_spec = pl.BlockSpec((w_rows, part), lambda g, q: (0, g))
    acts, act_grad, write_carry, tiles = call(
        functools.partial(finish_kernel, n_heads, n_w),
        "finish",
        (RING,),
        [by_group] * RING
        + [state_spec] * RING
        + [message_spec] * RING
        + [log_spec] * RING
        + [tile_spec(0)] * (2 * RING)
        + [cum_spec] * RING
        + [w_spec] * n_w
        + [by_group],
        [tall, by_group, proj_spec, const(RING * rows, n_w * w_rows)],
        [
            shape((RING * rows, columns), bf16),
            shape((rows, columns), bf16),
            shape((rows, state_dim), f32),
            shape((RING * rows, n_w * w_rows), bf16),
        ],
        [pltpu.VMEM((RING * rows, n_w * w_rows), f32)],
    )(
        at,
        *local_acts,
        *ring_grads,
        *grad_parts,
        *logs,
        *[top for top, _ in blocks],
        *[bottom for _, bottom in blocks],
        *cums,
        *w_blocks[:n_w],
        x,
    )

    def over_head(tile):
        if n_head == 2:
            got = lax.ppermute(tile, "head", [(0, 1), (1, 0)])
            return (tile.astype(f32) + got.astype(f32)).astype(bf16)
        return lax.psum(tile.astype(f32), "head").astype(bf16)

    def to_owners(tile):
        return [tile[:rows]] + [swap(tile[j * rows : (j + 1) * rows], j) for j in range(1, RING)]

    share = outer // n_head
    tiles, w_blocks[-1] = lax.optimization_barrier((tiles, w_blocks[-1]))
    early = over_head(tiles)
    late_tile = mm(acts, w_blocks[-1], NT).astype(bf16)

    held = [tiles, late_tile]

    def after(got):
        held[0], got = lax.optimization_barrier((held[0], got))
        held[0] = held[1]
        return got

    my_ends = [ends[0]] + [swap(ends[j], j) for j in range(1, RING)]
    state_part = scan_along(combine(my_ends, 1), 1, after)
    mine_half = pl.BlockSpec((half, part), lambda g, q: (0, q[0]))
    read_parts = call(
        functools.partial(read_kernel, n_heads),
        "read_carry",
        (1,),
        [mine_half] * (2 * RING)
        + [cum_spec] * RING
        + [mine_log] * RING
        + [const(state_dim, part)] * RING
        + [message_spec],
        [proj_spec] * RING,
        [shape((rows, state_dim), bf16)] * RING,
    )(
        at,
        *[top for top, _ in blocks],
        *[bottom for _, bottom in blocks],
        *cums,
        *logs,
        *my_ends,
        state_part,
    )

    late = over_head(late_tile)
    late, read_parts = lax.optimization_barrier((late, read_parts))
    late = to_owners(late)
    early = to_owners(early)
    read_carry = read_parts[0].astype(f32) + sum(
        swap(read_parts[j], j).astype(f32) for j in range(1, RING)
    )
    both = jnp.stack([write_local + write_carry, read_local + read_carry])
    if n_head == 2:
        both = both + lax.ppermute(both, "head", [(0, 1), (1, 0)])
    else:
        both = lax.psum(both, "head")

    if w_rows % LANES == 0:
        input_grad = pl.pallas_call(
            functools.partial(place_kernel, outer, share),
            in_specs=[pl.BlockSpec(memory_space=pltpu.SMEM)]
            + [pl.BlockSpec(memory_space=pltpu.VMEM)] * (2 * RING),
            out_specs=pl.BlockSpec(memory_space=pltpu.VMEM),
            out_shape=shape((rows, share * RING * w_rows), bf16),
            compiler_params=pltpu.CompilerParams(vmem_limit_bytes=32 * 2**20),
            name="place",
        )(jnp.stack([p, z, side]).astype(jnp.int32), *early, *late)
    else:
        order = p ^ jnp.arange(RING)
        pieces = jnp.concatenate([jnp.stack(early), jnp.stack(late)], axis=2)
        pieces = jnp.take(pieces.reshape(RING, rows, outer, w_rows), order, axis=0)
        pieces = jnp.take(pieces, (side * share + jnp.arange(share) - z) % outer, axis=2)
        input_grad = pieces.transpose(1, 2, 0, 3).reshape(rows, share * RING * w_rows)
    return (input_grad, act_grad, both[0], both[1])


def solution(mesh):
    return jax.shard_map(
        local,
        mesh=mesh,
        in_specs=(
            P("seq", "head"),
            P("seq", "head"),
            P("seq", None),
            P("seq", None),
            P("seq", "head"),
            P("seq", "head"),
        ),
        out_specs=(P("seq", "head"), P("seq", "head"), P("seq", None), P("seq", None)),
        check_vma=False,
    )
```

```python
import functools

import jax
import jax.numpy as jnp
from jax import lax
from jax.experimental import pallas as pl
from jax.experimental.pallas import tpu as pltpu
from jax.sharding import PartitionSpec as P

RING = 4
LANES = 128
EXTRA = 16
NT = (((1,), (1,)), ((), ()))
TN = (((0,), (0,)), ((), ()))
NN = (((1,), (0,)), ((), ()))
bf16, f32 = jnp.bfloat16, jnp.float32


def mm(a, b, dims):
    return lax.dot_general(a, b, dims, preferred_element_type=f32)


def mm_exact(a, b, dims):
    return lax.dot_general(a, b, dims, precision=lax.Precision.HIGHEST, preferred_element_type=f32)


def spread(columns, width):
    rows = columns.shape[0]
    return jnp.concatenate(
        [jnp.broadcast_to(columns[:, h : h + 1], (rows, width)) for h in range(columns.shape[1])],
        axis=1,
    )


def iota(shape, axis):
    return lax.broadcasted_iota(jnp.int32, shape, axis)


def three_parts(value):
    first = value.astype(bf16).astype(f32)
    second = (value - first).astype(bf16).astype(f32)
    return first, second, value - first - second


def cumulate(n_heads, log_tiles, cum, cum_t):
    parts = jnp.concatenate([tile[...] for tile in log_tiles], axis=0)
    rows = parts.shape[0]
    source, head = iota((LANES, LANES), 0), iota((LANES, LANES), 1)
    pick = (source < 3 * n_heads) & (lax.rem(source, n_heads) == head)
    logs = mm(parts, pick.astype(f32).astype(bf16), NN)
    upto = (iota((rows, rows), 0) <= iota((rows, rows), 1)).astype(f32)
    cum[...] = mm_exact(upto, logs, TN)
    if cum_t is not None:
        cum_t[...] = mm_exact(logs, upto, TN)


def group_of(value, g, heads, axis):
    shift = lax.rem(LANES - g * heads, LANES)
    value = pltpu.roll(value, shift, axis)
    return value[:, :heads] if axis == 1 else value[:heads]


def diagonal(heads, half, lo, col, row, each):
    later = iota((half, half), 1) >= iota((half, half), 0)
    for h in range(heads):
        log = row[h : h + 1, lo : lo + half] - col[lo : lo + half, h : h + 1]
        each(h, jnp.exp(jnp.where(later, log, -jnp.inf)))


def own_logs(log_decay):
    rows, n_heads = log_decay.shape
    return jnp.concatenate([log_decay[...], jnp.zeros((rows, LANES - n_heads), f32)], axis=1)


def edge_kernel(n_heads, at, x, dy, b, c, log_decay, *refs):
    messages, cum = refs[:RING], refs[RING]
    g = pl.program_id(0)
    heads = n_heads // RING
    rows = x.shape[0]
    width = x.shape[1] // heads
    n = b.shape[1]

    @pl.when(g == 0)
    def _():
        upto = (iota((rows, rows), 0) <= iota((rows, rows), 1)).astype(f32)
        cum[...] = mm_exact(upto, own_logs(log_decay), TN)

    col = group_of(cum[...], g, heads, 1)
    last = col[rows - 1 : rows, :]
    tailed = (x[...].astype(f32) * spread(jnp.exp(last - col), width)).astype(bf16)
    decayed = (dy[...].astype(f32) * spread(jnp.exp(col), width)).astype(bf16)
    ends = mm(b[...], tailed, TN).astype(bf16)
    fronts = mm(c[...], decayed, TN).astype(bf16)
    log = spread(last, width)
    for j in range(RING):

        @pl.when(lax.bitwise_xor(at[0], g) == j)
        def _():
            messages[j][:n] = ends
            messages[j][n : 2 * n] = fronts
            write_log(messages[j], log)


def pack_kernel(n_heads, dy, b, c, log_decay, out):
    rows, columns = dy.shape
    parts = [v.astype(bf16) for v in three_parts(log_decay[...])]
    fill = jnp.zeros((rows, LANES - 3 * n_heads), bf16)
    out[:, :columns] = dy[...]
    out[:, columns : columns + LANES] = b[...]
    out[:, columns + LANES : columns + 2 * LANES] = c[...]
    out[:, columns + 2 * LANES :] = jnp.concatenate(parts + [fill], axis=1)


def own_kernel(n_heads, x, dy, b, c, log_decay, write_local, read_local, total, cum, cum_t):
    g = pl.program_id(0)
    heads = n_heads // RING
    rows = x.shape[0]
    half = rows // 2
    width = x.shape[1] // heads

    @pl.when(g == 0)
    def _():
        total[...] = jnp.zeros_like(total)
        logs = own_logs(log_decay)
        upto = (iota((rows, rows), 0) <= iota((rows, rows), 1)).astype(f32)
        cum[...] = mm_exact(upto, logs, TN)
        cum_t[...] = mm_exact(logs, upto, TN)

    col, row = group_of(cum[...], g, heads, 1), group_of(cum_t[...], g, heads, 0)
    mid = col[half - 1 : half, :]
    for i in range(2):
        lo = i * half
        parts = []

        def add(h, decay):
            span = slice(h * width, (h + 1) * width)
            parts.append(decay * mm(x[lo : lo + half, span], dy[lo : lo + half, span], NT))

        diagonal(heads, half, lo, col, row, add)
        total[lo : lo + half, lo : lo + half] += sum(parts)
    early = (x[:half].astype(f32) * spread(jnp.exp(mid - col[:half]), width)).astype(bf16)
    late = (dy[half:].astype(f32) * spread(jnp.exp(col[half:] - mid), width)).astype(bf16)
    total[:half, half:] += mm(early, late, NT)

    @pl.when(g == pl.num_programs(0) - 1)
    def _():
        write_local[...] = mm_exact(total[...], c[...].astype(f32), NN)
        read_local[...] = mm_exact(total[...], b[...].astype(f32), TN)


def block_kernel(n_heads, top, bottom, *refs):
    tiles, (act, fronts, log_row, cum_out, cum_t) = refs[:6], refs[6:]
    b = jnp.concatenate([tiles[0][...], tiles[1][...]], axis=0)
    c = jnp.concatenate([tiles[2][...], tiles[3][...]], axis=0)
    g = pl.program_id(0)
    heads = n_heads // RING
    half = top.shape[0]
    rows = 2 * half
    width = top.shape[1] // heads

    @pl.when(g == 0)
    def _():
        cumulate(n_heads, tiles[4:], cum_out, cum_t)

    col, row = group_of(cum_out[...], g, heads, 1), group_of(cum_t[...], g, heads, 0)
    mid, last = col[half - 1 : half, :], col[rows - 1 : rows, :]
    log_row[...] = spread(last, width)
    scores = mm(b, c, NT)
    late_f = bottom[...].astype(f32) * spread(jnp.exp(col[half:] - mid), width)
    late = late_f.astype(bf16)
    first = (top[...].astype(f32) * spread(jnp.exp(col[:half]), width)).astype(bf16)
    second = (late_f * spread(jnp.exp(mid), width)).astype(bf16)
    fronts[0] = (mm(c[:half], first, TN) + mm(c[half:], second, TN)).astype(bf16)
    cross = mm(scores[:half, half:].astype(bf16), late, NN)
    to_mid = jnp.exp(mid - col[:half])
    for i, dy in enumerate((top, bottom)):
        lo = i * half
        score = scores[lo : lo + half, lo : lo + half]

        def put(h, decay):
            span = slice(h * width, (h + 1) * width)
            out = mm((decay * score).astype(bf16), dy[:, span], NN)
            if i == 0:
                out += cross[:, span] * to_mid[:, h : h + 1]
            act[lo : lo + half, span] = out.astype(act.dtype)

        diagonal(heads, half, lo, col, row, put)


def log_over(p, logs, wanted):
    total = jnp.zeros_like(logs[0])
    for k in range(RING):
        total += jnp.where(wanted(lax.bitwise_xor(p, k)), logs[k], 0.0)
    return total


def combine_kernel(at, *refs):
    parts, (state_out, grad_out) = refs[:RING], refs[RING:]
    n = state_out.shape[0] - EXTRA
    logs = [log_of(part) for part in parts]
    p = at[0]
    state, grad = 0.0, 0.0
    for j in range(RING):
        own = lax.bitwise_xor(p, j)
        state += parts[j][:n].astype(f32) * jnp.exp(log_over(p, logs, lambda k: k > own))
        grad += parts[j][n : 2 * n].astype(f32) * jnp.exp(log_over(p, logs, lambda k: k < own))
    for out, value in ((state_out, state), (grad_out, grad)):
        out[:n] = value.astype(bf16)
        write_log(out, sum(logs))


def write_log(out, log):
    n, width = out.shape
    row = iota((EXTRA, width), 0)
    rows = jnp.zeros((EXTRA, width), f32)
    for i, part in enumerate(three_parts(log)):
        rows = jnp.where(row == i, part, rows)
    out[n - EXTRA :] = rows.astype(bf16)


def log_of(message):
    n = message.shape[0] - EXTRA
    tail = message[n:].astype(f32)
    return tail[0:1] + tail[1:2] + tail[2:3]


def merge_kernel(*refs):
    for near, far, out in ((*refs[:2], refs[4]), (*refs[2:4], refs[5])):
        n = near.shape[0] - EXTRA
        log = log_of(near)
        out[:n] = (near[:n].astype(f32) + far[:n].astype(f32) * jnp.exp(log)).astype(bf16)
        write_log(out, log + log_of(far))


def ring_kernel(at, *refs):
    fronts, logs, outs = refs[:RING], [r[...] for r in refs[RING : 2 * RING]], refs[2 * RING :]
    p = at[0]
    for j in range(RING):
        own = lax.bitwise_xor(p, j)
        total = 0.0
        for i in range(RING):
            if i != j:
                there = lax.bitwise_xor(p, i)
                weight = jnp.exp(log_over(p, logs, lambda k: (k > own) & (k < there)))
                total += fronts[i][0].astype(f32) * jnp.where(there > own, weight, 0.0)
        outs[j][0] = total.astype(bf16)


def finish_kernel(n_heads, n_w, outer, share, at, *refs):
    locals_, refs = refs[:RING], refs[RING:]
    rings, refs = refs[:RING], refs[RING:]
    quarters, refs = refs[:RING], refs[RING:]
    logs, refs = [r[...] for r in refs[:RING]], refs[RING:]
    tops, refs = refs[:RING], refs[RING:]
    bottoms, refs = refs[:RING], refs[RING:]
    cums, refs = refs[:RING], refs[RING:]
    w, refs = refs[:n_w], refs[n_w:]
    x, acts, own, write, *tiles, total = refs
    g, p = pl.program_id(0), at[0]
    heads = n_heads // RING
    rows = own.shape[0]
    width = own.shape[1] // heads
    n = quarters[0].shape[0] - EXTRA
    source = lax.bitwise_xor(p, g)
    carried = quarters[0][:n].astype(f32)
    for j in range(1, RING):
        carried = jnp.where(source == j, quarters[j][:n].astype(f32), carried)

    @pl.when(g == 0)
    def _():
        write[...] = jnp.zeros_like(write)
        total[...] = jnp.zeros_like(total)

    for j in range(RING):
        col = group_of(cums[j][...], g, heads, 1)
        tail = spread(jnp.exp(col[rows - 1 : rows, :] - col), width)
        place = lax.bitwise_xor(p, j)
        weight = jnp.exp(log_over(p, logs, lambda k: k > place))
        grads = (carried * weight + rings[j][0].astype(f32)).astype(bf16)
        b = jnp.concatenate([tops[j][...], bottoms[j][...]], axis=0)
        out = mm(b, grads, NN) * tail + locals_[j][...].astype(f32)
        out = out.astype(acts.dtype)
        acts[j * rows : (j + 1) * rows, :] = out
        if j == 0:
            own[...] = out
            write[...] += mm((x[...].astype(f32) * tail).astype(bf16), grads, NT)
    for k in range(n_w):
        n_rows = w[k].shape[0]
        total[:, k * n_rows : (k + 1) * n_rows] += mm(acts[...], w[k][...], NT)

    @pl.when(g == pl.num_programs(0) - 1)
    def _():
        if len(tiles) == 1:
            for k in range(n_w):
                put_tile(tiles[0], lax.rem(at[1] + k, outer), total, k, n_rows)
        else:
            for tile in tiles:
                tile[...] = jnp.zeros_like(tile)
            for k in range(n_w):
                o = lax.rem(at[1] + k, outer)
                for tile, side in zip(tiles, (at[2], 1 - at[2])):

                    @pl.when(lax.div(o, share) == side)
                    def _():
                        put_tile(tile, lax.rem(o, share), total, k, n_rows)


def put_tile(tile, slot, total, k, n_rows):
    rows = total.shape[0] // RING
    for j in range(RING):
        part = total[j * rows : (j + 1) * rows, k * n_rows : (k + 1) * n_rows]
        tile[j, slot] = part.astype(tile.dtype)


def read_kernel(n_heads, at, *refs):
    tops, refs = refs[:RING], refs[RING:]
    bottoms, refs = refs[:RING], refs[RING:]
    cums, refs = refs[:RING], refs[RING:]
    parts, (carried, *outs) = refs[:RING], refs[RING:]
    logs = [log_of(part) for part in parts]
    p = at[0]
    heads = n_heads // RING
    half = tops[0].shape[0]
    n = carried.shape[0] - EXTRA
    width = carried.shape[1] // heads
    for j in range(RING):
        own = lax.bitwise_xor(p, j)
        total = carried[:n].astype(f32) * jnp.exp(log_over(p, logs, lambda k: k < own))
        for i in range(RING):
            if i != j:
                there = lax.bitwise_xor(p, i)
                weight = jnp.exp(log_over(p, logs, lambda k: (k < own) & (k > there)))
                total += parts[i][:n].astype(f32) * jnp.where(there < own, weight, 0.0)
        states = total.astype(bf16)
        decay = spread(jnp.exp(group_of(cums[j][...], p, heads, 1)), width)
        for i, dy in enumerate((tops[j], bottoms[j])):
            at_rows = slice(i * half, (i + 1) * half)
            scaled = (dy[...].astype(f32) * decay[at_rows]).astype(bf16)
            outs[j][at_rows] = mm(scaled, states, NT).astype(bf16)


def place_kernel(outer, share, at, *refs):
    blocks, late, out = refs[:RING], refs[RING:-1], refs[-1]
    p, z, side = at[0], at[1], at[2]
    width = out.shape[1] // (share * RING)
    last = lax.rem(z + outer - 1, outer)
    for slot in range(share):
        for j in range(RING):
            column = pl.multiple_of((slot * RING + lax.bitwise_xor(p, j)) * width, width)

            @pl.when(side * share + slot == last)
            def _():
                out[:, pl.ds(column, width)] = late[j][...]

            @pl.when(side * share + slot != last)
            def _():
                out[:, pl.ds(column, width)] = blocks[j][slot]


def call(kernel, name, grid, in_specs, out_specs, out_shape, scratch=(), prefetch=1):
    return pl.pallas_call(
        kernel,
        grid_spec=pltpu.PrefetchScalarGridSpec(
            num_scalar_prefetch=prefetch,
            grid=grid,
            in_specs=in_specs,
            out_specs=out_specs,
            scratch_shapes=list(scratch),
        ),
        out_shape=out_shape,
        compiler_params=pltpu.CompilerParams(vmem_limit_bytes=56 * 2**20),
        cost_estimate=pl.CostEstimate(flops=0, bytes_accessed=0, transcendentals=0),
        name=name,
    )


def local(x, dy, write_proj, read_proj, log_decay, w_in):
    rows, columns = x.shape
    half = rows // 2
    state_dim = write_proj.shape[1]
    n_heads = log_decay.shape[1]
    heads = n_heads // RING
    width = columns // n_heads
    part = heads * width
    w_rows = w_in.shape[0]
    n_seq, n_head = lax.axis_size("seq"), lax.axis_size("head")
    outer = n_seq // RING
    place = lax.axis_index("seq")
    side = lax.axis_index("head")
    p, z = place % RING, place // RING
    at = jnp.stack([p, z, side]).astype(jnp.int32)

    def swap(value, j):
        return lax.ppermute(value, "seq", [(s, s ^ j) for s in range(n_seq)])

    def along(value, d):
        return lax.ppermute(
            value, "seq", [(s, s + d * RING) for s in range(n_seq) if 0 <= s + d * RING < n_seq]
        )

    w_blocks = [w_in]

    def turn_w():
        turn = [(s, (s - RING) % n_seq) for s in range(n_seq)]
        w_blocks.append(lax.ppermute(w_blocks[-1], "seq", turn))

    turn_w()

    def const(*shape):
        return pl.BlockSpec(shape, lambda g, q: (0,) * len(shape))

    by_group = pl.BlockSpec((rows, part), lambda g, q: (0, g))
    state_spec = pl.BlockSpec((1, state_dim, part), lambda g, q: (g, 0, 0))
    log_spec = pl.BlockSpec((1, part), lambda g, q: (0, g))
    cum_spec = const(rows, LANES)
    proj_spec = const(rows, state_dim)
    message_spec = const(state_dim + EXTRA, part)
    shape = jax.ShapeDtypeStruct
    state_shape = shape((RING, state_dim, part), bf16)
    log_shape = shape((1, columns), f32)
    cum_shape = shape((rows, LANES), f32)
    message_shape = shape((state_dim + EXTRA, part), bf16)
    cum_scratch, cum_t_scratch = pltpu.VMEM((rows, LANES), f32), pltpu.VMEM((LANES, rows), f32)

    log_in_spec = const(rows, n_heads)
    own_specs = [by_group, by_group, proj_spec, proj_spec, log_in_spec]
    part_spec = const(2 * state_dim + EXTRA, part)
    parts = call(
        functools.partial(edge_kernel, n_heads),
        "edges",
        (RING,),
        own_specs,
        [part_spec] * RING,
        [shape((2 * state_dim + EXTRA, part), bf16)] * RING,
        [cum_scratch],
    )(at, x, dy, write_proj, read_proj, log_decay)
    parts = [parts[0]] + [swap(parts[j], j) for j in range(1, RING)]

    write_local, read_local = call(
        functools.partial(lambda *refs: own_kernel(n_heads, *refs[1:])),
        "own_tokens",
        (RING,),
        own_specs,
        [proj_spec] * 2,
        [shape((rows, state_dim), f32)] * 2,
        [pltpu.VMEM((rows, rows), f32), cum_scratch, cum_t_scratch],
    )(at, x, dy, write_proj, read_proj, log_decay)

    packed = call(
        functools.partial(lambda *refs: pack_kernel(n_heads, *refs[1:])),
        "pack",
        (1,),
        [const(rows, columns), proj_spec, proj_spec, log_in_spec],
        const(rows, columns + 3 * LANES),
        shape((rows, columns + 3 * LANES), bf16),
    )(at, dy, write_proj, read_proj, log_decay)

    def halves(width, column):
        upper = pl.BlockSpec((half, width), lambda g, q: (0, column(g, q)))
        lower = pl.BlockSpec((half, width), lambda g, q: (1, column(g, q)))
        return [(upper, lower)] * (RING - 1) + [(upper, upper)]

    half_specs = halves(part, lambda g, q: g)
    mine_specs = halves(part, lambda g, q: q[0])
    tile_specs = [halves(LANES, lambda g, q, i=i: columns // LANES + i) for i in range(3)]

    def block(j, top, bottom):
        return call(
            functools.partial(lambda *refs: block_kernel(n_heads, *refs[1:])),
            "tokens",
            (RING,),
            [*half_specs[j]] + [spec for specs in tile_specs for spec in specs[j]],
            [by_group, state_spec, log_spec, cum_spec],
            [shape((rows, columns), bf16), state_shape, log_shape, cum_shape],
            [cum_t_scratch],
        )(at, top, bottom, *([top, bottom] * 3))

    results = [block(0, packed, packed)]
    logs = [results[0][2]]
    packed, parts, logs, read_local = lax.optimization_barrier((packed, parts, logs, read_local))
    from_x, from_y = lax.optimization_barrier((swap(packed, 1), swap(packed, 2)))

    def combine():
        return call(
            combine_kernel,
            "messages",
            (1,),
            [part_spec] * RING,
            [message_spec] * 2,
            [message_shape] * 2,
        )(at, *parts)

    def merge(*pairs):
        return call(
            lambda q, *refs: merge_kernel(*refs),
            "merge",
            (1,),
            [message_spec] * 4,
            [message_spec] * 2,
            [message_shape] * 2,
        )(at, *pairs)

    state_span, grad_span = combine()
    d = 1
    while d < outer:
        state_got, grad_got = along(state_span, d), along(grad_span, -d)
        if d == 1:
            state_part, grad_part = state_got, grad_got
        else:
            state_part, grad_part = merge(state_part, state_got, grad_part, grad_got)
        if 2 * d < outer:
            state_span, grad_span = merge(state_span, state_got, grad_span, grad_got)
        d *= 2
    state_got, grad_got, w_blocks[-1] = lax.optimization_barrier(
        (state_got, grad_got, w_blocks[-1])
    )
    turn_w()
    grad_parts = [grad_part] + [swap(grad_part, j) for j in range(1, RING)]

    blocks = [(packed, packed), (from_x, from_x), (from_y, from_y)]
    blocks.append((swap(from_x[:half], 2), swap(from_y[half:], 1)))
    results += [block(j, *blocks[j]) for j in range(1, RING - 1)]
    logs += [v[2] for v in results[1:]]
    logs, blocks[-1] = lax.optimization_barrier((logs, blocks[-1]))
    results.append(block(RING - 1, *blocks[-1]))
    logs.append(results[-1][2])
    local_acts, fronts, _, cums = zip(*results)
    fronts = list(fronts)
    if outer > 2:
        fronts[-1], w_blocks[-1] = lax.optimization_barrier((fronts[-1], w_blocks[-1]))
    while len(w_blocks) < outer:
        turn_w()

    ring_grads = call(
        ring_kernel,
        "ring_grads",
        (RING,),
        [state_spec] * RING + [log_spec] * RING,
        [state_spec] * RING,
        [state_shape] * RING,
    )(at, *fronts, *logs)

    two = n_head == 2 and w_rows % LANES == 0
    share = outer // n_head
    n_w = outer - 1 if two else outer
    tall = pl.BlockSpec((RING * rows, part), lambda g, q: (0, g))
    w_spec = pl.BlockSpec((w_rows, part), lambda g, q: (0, g))
    tile_shapes = [(RING, share, rows, w_rows)] * 2 if two else [(RING, outer, rows, w_rows)]
    acts, act_grad, write_carry, *tiles = call(
        functools.partial(finish_kernel, n_heads, n_w, outer, share),
        "finish",
        (RING,),
        [by_group] * RING
        + [state_spec] * RING
        + [message_spec] * RING
        + [log_spec] * RING
        + [spec[0] for spec in tile_specs[0]]
        + [spec[1] for spec in tile_specs[0]]
        + [cum_spec] * RING
        + [w_spec] * n_w
        + [by_group],
        [tall, by_group, proj_spec] + [const(*v) for v in tile_shapes],
        [
            shape((RING * rows, columns), bf16),
            shape((rows, columns), bf16),
            shape((rows, state_dim), f32),
        ]
        + [shape(v, bf16) for v in tile_shapes],
        [pltpu.VMEM((RING * rows, n_w * w_rows), f32)],
    )(
        at,
        *local_acts,
        *ring_grads,
        *grad_parts,
        *logs,
        *[top for top, _ in blocks],
        *[bottom for _, bottom in blocks],
        *cums,
        *w_blocks[:n_w],
        x,
    )

    read_parts = call(
        functools.partial(read_kernel, n_heads),
        "read_carry",
        (1,),
        [spec[0] for spec in mine_specs]
        + [spec[1] for spec in mine_specs]
        + [cum_spec] * RING + [part_spec] * RING + [message_spec],
        [proj_spec] * RING,
        [shape((rows, state_dim), bf16)] * RING,
    )(
        at,
        *[top for top, _ in blocks],
        *[bottom for _, bottom in blocks],
        *cums,
        *parts,
        state_part,
    )
    read_carry = read_parts[0].astype(f32) + sum(
        swap(read_parts[j], j).astype(f32) for j in range(1, RING)
    )
    both = jnp.stack([write_local + write_carry, read_local + read_carry])
    if n_head == 2:
        both = both + lax.ppermute(both, "head", [(0, 1), (1, 0)])
    else:
        both = lax.psum(both, "head")

    def to_owners(tile):
        return [tile[0]] + [swap(tile[j], j) for j in range(1, RING)]

    if two:
        mine, theirs = tiles
        got = lax.ppermute(theirs, "head", [(0, 1), (1, 0)])
        early = (mine.astype(f32) + got.astype(f32)).astype(bf16)
        _, w_last = lax.optimization_barrier((early, w_blocks[-1]))
        tile = mm(acts, w_last, NT).astype(bf16)

        def owner(s):
            return (s // RING + outer - 1) % outer // share

        both_axes = ("seq", "head")
        got = lax.ppermute(
            tile, both_axes, [(2 * s + 1 - owner(s), 2 * s + owner(s)) for s in range(n_seq)]
        )
        tile = (tile.astype(f32) + got.astype(f32)).astype(bf16).reshape(RING, rows, w_rows)
        late = [tile[0]] + [
            lax.ppermute(
                tile[j],
                both_axes,
                [(2 * s + owner(s), 2 * (s ^ j) + owner(s)) for s in range(n_seq)],
            )
            for j in range(1, RING)
        ]
        early = to_owners(early)
        input_grad = pl.pallas_call(
            functools.partial(place_kernel, outer, share),
            in_specs=[pl.BlockSpec(memory_space=pltpu.SMEM)]
            + [pl.BlockSpec(memory_space=pltpu.VMEM)] * (2 * RING),
            out_specs=pl.BlockSpec(memory_space=pltpu.VMEM),
            out_shape=shape((rows, share * RING * w_rows), bf16),
            compiler_params=pltpu.CompilerParams(vmem_limit_bytes=32 * 2**20),
            name="place",
        )(at, *early, *late)
    else:
        summed = lax.psum_scatter(tiles[0], "head", scatter_dimension=1, tiled=True)
        pieces = jnp.take(jnp.stack(to_owners(summed)), p ^ jnp.arange(RING), axis=0)
        input_grad = pieces.transpose(2, 1, 0, 3).reshape(rows, share * RING * w_rows)
    return (input_grad, act_grad, both[0], both[1])


def solution(mesh):
    return jax.shard_map(
        local,
        mesh=mesh,
        in_specs=(
            P("seq", "head"),
            P("seq", "head"),
            P("seq", None),
            P("seq", None),
            P("seq", "head"),
            P("seq", "head"),
        ),
        out_specs=(P("seq", "head"), P("seq", "head"), P("seq", None), P("seq", None)),
        check_vma=False,
    )
```

```python
import functools

import jax
import jax.numpy as jnp
from jax import lax
from jax.experimental import pallas as pl
from jax.experimental.pallas import tpu as pltpu
from jax.sharding import PartitionSpec as P

RING = 4
LANES = 128
EXTRA = 16
NT = (((1,), (1,)), ((), ()))
TN = (((0,), (0,)), ((), ()))
NN = (((1,), (0,)), ((), ()))
bf16, f32 = jnp.bfloat16, jnp.float32


def mm(a, b, dims):
    return lax.dot_general(a, b, dims, preferred_element_type=f32)


def mm_exact(a, b, dims):
    return lax.dot_general(a, b, dims, precision=lax.Precision.HIGHEST, preferred_element_type=f32)


def spread(columns, width):
    rows = columns.shape[0]
    return jnp.concatenate(
        [jnp.broadcast_to(columns[:, h : h + 1], (rows, width)) for h in range(columns.shape[1])],
        axis=1,
    )


def iota(shape, axis):
    return lax.broadcasted_iota(jnp.int32, shape, axis)


def three_parts(value):
    first = value.astype(bf16).astype(f32)
    second = (value - first).astype(bf16).astype(f32)
    return first, second, value - first - second


def cumulate(n_heads, log_tiles, cum, cum_t):
    parts = jnp.concatenate([tile[...] for tile in log_tiles], axis=0)
    rows = parts.shape[0]
    source, head = iota((LANES, LANES), 0), iota((LANES, LANES), 1)
    pick = (source < 3 * n_heads) & (lax.rem(source, n_heads) == head)
    logs = mm(parts, pick.astype(f32).astype(bf16), NN)
    upto = (iota((rows, rows), 0) <= iota((rows, rows), 1)).astype(f32)
    cum[...] = mm_exact(upto, logs, TN)
    if cum_t is not None:
        cum_t[...] = mm_exact(logs, upto, TN)


def group_of(value, g, heads, axis):
    shift = lax.rem(LANES - g * heads, LANES)
    value = pltpu.roll(value, shift, axis)
    return value[:, :heads] if axis == 1 else value[:heads]


def diagonal(heads, half, lo, col, row, each):
    later = iota((half, half), 1) >= iota((half, half), 0)
    for h in range(heads):
        log = row[h : h + 1, lo : lo + half] - col[lo : lo + half, h : h + 1]
        each(h, jnp.exp(jnp.where(later, log, -jnp.inf)))


def cumulate_own(log_t, cum, cum_t):
    n_heads, rows = log_t.shape
    logs = jnp.concatenate([log_t[...], jnp.zeros((LANES - n_heads, rows), f32)], axis=0)
    upto = (iota((rows, rows), 0) <= iota((rows, rows), 1)).astype(f32)
    cum[...] = mm_exact(upto, logs, (((0,), (1,)), ((), ())))
    if cum_t is not None:
        cum_t[...] = mm_exact(logs, upto, NN)


def edge_kernel(n_heads, at, x, dy, b, c, log_t, *refs):
    messages, cum = refs[:RING], refs[RING]
    g = pl.program_id(0)
    heads = n_heads // RING
    rows = x.shape[0]
    width = x.shape[1] // heads
    n = b.shape[1]

    @pl.when(g == 0)
    def _():
        cumulate_own(log_t, cum, None)

    col = group_of(cum[...], g, heads, 1)
    last = col[rows - 1 : rows, :]
    tailed = (x[...].astype(f32) * spread(jnp.exp(last - col), width)).astype(bf16)
    decayed = (dy[...].astype(f32) * spread(jnp.exp(col), width)).astype(bf16)
    ends = mm(b[...], tailed, TN).astype(bf16)
    fronts = mm(c[...], decayed, TN).astype(bf16)
    log = spread(last, width)
    for j in range(RING):

        @pl.when(lax.bitwise_xor(at[0], g) == j)
        def _():
            messages[j][:n] = ends
            messages[j][n : 2 * n] = fronts
            write_log(messages[j], log)


def pack_kernel(n_heads, dy, b, c, log_t, out):
    rows, columns = dy.shape
    fill = jnp.zeros((LANES - 3 * n_heads, rows), f32)
    logs = jnp.concatenate([*three_parts(log_t[...]), fill], axis=0)
    out[:, :columns] = dy[...]
    out[:, columns : columns + LANES] = b[...]
    out[:, columns + LANES : columns + 2 * LANES] = c[...]
    out[:, columns + 2 * LANES :] = logs.T.astype(bf16)


def own_kernel(n_heads, x, dy, b, c, log_t, write_local, read_local, total, cum, cum_t):
    g = pl.program_id(0)
    heads = n_heads // RING
    rows = x.shape[0]
    half = rows // 2
    width = x.shape[1] // heads

    @pl.when(g == 0)
    def _():
        total[...] = jnp.zeros_like(total)
        cumulate_own(log_t, cum, cum_t)

    col, row = group_of(cum[...], g, heads, 1), group_of(cum_t[...], g, heads, 0)
    mid = col[half - 1 : half, :]
    for i in range(2):
        lo = i * half
        parts = []

        def add(h, decay):
            span = slice(h * width, (h + 1) * width)
            parts.append(decay * mm(x[lo : lo + half, span], dy[lo : lo + half, span], NT))

        diagonal(heads, half, lo, col, row, add)
        total[lo : lo + half, lo : lo + half] += sum(parts)
    early = (x[:half].astype(f32) * spread(jnp.exp(mid - col[:half]), width)).astype(bf16)
    late = (dy[half:].astype(f32) * spread(jnp.exp(col[half:] - mid), width)).astype(bf16)
    total[:half, half:] += mm(early, late, NT)

    @pl.when(g == pl.num_programs(0) - 1)
    def _():
        write_local[...] = mm_exact(total[...], c[...].astype(f32), NN)
        read_local[...] = mm_exact(total[...], b[...].astype(f32), TN)


def block_kernel(n_heads, top, bottom, *refs):
    tiles, (act, fronts, log_row, cum_out, cum_t) = refs[:6], refs[6:]
    b = jnp.concatenate([tiles[0][...], tiles[1][...]], axis=0)
    c = jnp.concatenate([tiles[2][...], tiles[3][...]], axis=0)
    g = pl.program_id(0)
    heads = n_heads // RING
    half = top.shape[0]
    rows = 2 * half
    width = top.shape[1] // heads

    @pl.when(g == 0)
    def _():
        cumulate(n_heads, tiles[4:], cum_out, cum_t)

    col, row = group_of(cum_out[...], g, heads, 1), group_of(cum_t[...], g, heads, 0)
    mid, last = col[half - 1 : half, :], col[rows - 1 : rows, :]
    log_row[...] = spread(last, width)
    scores = mm(b, c, NT)
    late_f = bottom[...].astype(f32) * spread(jnp.exp(col[half:] - mid), width)
    late = late_f.astype(bf16)
    first = (top[...].astype(f32) * spread(jnp.exp(col[:half]), width)).astype(bf16)
    second = (late_f * spread(jnp.exp(mid), width)).astype(bf16)
    fronts[0] = (mm(c[:half], first, TN) + mm(c[half:], second, TN)).astype(bf16)
    cross = mm(scores[:half, half:].astype(bf16), late, NN)
    to_mid = jnp.exp(mid - col[:half])
    for i, dy in enumerate((top, bottom)):
        lo = i * half
        score = scores[lo : lo + half, lo : lo + half]

        def put(h, decay):
            span = slice(h * width, (h + 1) * width)
            out = mm((decay * score).astype(bf16), dy[:, span], NN)
            if i == 0:
                out += cross[:, span] * to_mid[:, h : h + 1]
            act[lo : lo + half, span] = out.astype(act.dtype)

        diagonal(heads, half, lo, col, row, put)


def log_over(p, logs, wanted):
    total = jnp.zeros_like(logs[0])
    for k in range(RING):
        total += jnp.where(wanted(lax.bitwise_xor(p, k)), logs[k], 0.0)
    return total


def combine_kernel(at, *refs):
    parts, (state_out, grad_out) = refs[:RING], refs[RING:]
    n = state_out.shape[0] - EXTRA
    logs = [log_of(part) for part in parts]
    p = at[0]
    state, grad = 0.0, 0.0
    for j in range(RING):
        own = lax.bitwise_xor(p, j)
        state += parts[j][:n].astype(f32) * jnp.exp(log_over(p, logs, lambda k: k > own))
        grad += parts[j][n : 2 * n].astype(f32) * jnp.exp(log_over(p, logs, lambda k: k < own))
    for out, value in ((state_out, state), (grad_out, grad)):
        out[:n] = value.astype(bf16)
        write_log(out, sum(logs))


def write_log(out, log):
    n, width = out.shape
    row = iota((EXTRA, width), 0)
    rows = jnp.zeros((EXTRA, width), f32)
    for i, part in enumerate(three_parts(log)):
        rows = jnp.where(row == i, part, rows)
    out[n - EXTRA :] = rows.astype(bf16)


def log_of(message):
    n = message.shape[0] - EXTRA
    tail = message[n:].astype(f32)
    return tail[0:1] + tail[1:2] + tail[2:3]


def merge_kernel(*refs):
    refs[6][...] = jnp.zeros_like(refs[6])
    for near, far, out in ((*refs[:2], refs[4]), (*refs[2:4], refs[5])):
        n = near.shape[0] - EXTRA
        log = log_of(near)
        out[:n] = (near[:n].astype(f32) + far[:n].astype(f32) * jnp.exp(log)).astype(bf16)
        write_log(out, log + log_of(far))


def ring_kernel(at, *refs):
    fronts, logs, outs = refs[:RING], [r[...] for r in refs[RING : 2 * RING]], refs[2 * RING :]
    p = at[0]
    for j in range(RING):
        own = lax.bitwise_xor(p, j)
        total = 0.0
        for i in range(RING):
            if i != j:
                there = lax.bitwise_xor(p, i)
                weight = jnp.exp(log_over(p, logs, lambda k: (k > own) & (k < there)))
                total += fronts[i][0].astype(f32) * jnp.where(there > own, weight, 0.0)
        outs[j][0] = total.astype(bf16)


def finish_kernel(n_heads, n_w, n_pieces, outer, share, at, *refs):
    locals_, refs = refs[:RING], refs[RING:]
    rings, refs = refs[:RING], refs[RING:]
    quarters, refs = refs[:RING], refs[RING:]
    logs, refs = [r[...] for r in refs[:RING]], refs[RING:]
    tops, refs = refs[:RING], refs[RING:]
    bottoms, refs = refs[:RING], refs[RING:]
    cums, refs = refs[:RING], refs[RING:]
    w, refs = refs[:n_pieces], refs[n_pieces:]
    x, acts, own, write, *tiles, total = refs
    late = tiles.pop() if len(tiles) == 3 else None
    g, p = pl.program_id(0), at[0]
    heads = n_heads // RING
    rows = own.shape[0]
    width = own.shape[1] // heads
    n = quarters[0].shape[0] - EXTRA
    source = lax.bitwise_xor(p, g)
    carried = quarters[0][:n].astype(f32)
    for j in range(1, RING):
        carried = jnp.where(source == j, quarters[j][:n].astype(f32), carried)

    @pl.when(g == 0)
    def _():
        write[...] = jnp.zeros_like(write)
        total[...] = jnp.zeros_like(total)

    for j in range(RING):
        col = group_of(cums[j][...], g, heads, 1)
        tail = spread(jnp.exp(col[rows - 1 : rows, :] - col), width)
        place = lax.bitwise_xor(p, j)
        weight = jnp.exp(log_over(p, logs, lambda k: k > place))
        grads = (carried * weight + rings[j][0].astype(f32)).astype(bf16)
        b = jnp.concatenate([tops[j][...], bottoms[j][...]], axis=0)
        out = mm(b, grads, NN) * tail + locals_[j][...].astype(f32)
        out = out.astype(acts.dtype)
        acts[j * rows : (j + 1) * rows, :] = out
        if j == 0:
            own[...] = out
            write[...] += mm((x[...].astype(f32) * tail).astype(bf16), grads, NT)
    n_rows, column = w[0].shape[0], 0
    for piece in w:
        total[:, column : column + piece.shape[0]] += mm(acts[...], piece[...], NT)
        column += piece.shape[0]

    @pl.when(g == pl.num_programs(0) - 1)
    def _():
        if len(tiles) == 1:
            for k in range(n_w):
                put_tile(tiles[0], lax.rem(at[1] + k, outer), total, k, n_rows)
        else:
            late[...] = total[:, n_w * n_rows :].astype(late.dtype)
            for tile in tiles:
                tile[...] = jnp.zeros_like(tile)
            for k in range(n_w):
                o = lax.rem(at[1] + k, outer)
                for tile, side in zip(tiles, (at[2], 1 - at[2])):

                    @pl.when(lax.div(o, share) == side)
                    def _():
                        put_tile(tile, lax.rem(o, share), total, k, n_rows)


def put_tile(tile, slot, total, k, n_rows):
    rows = total.shape[0] // RING
    for j in range(RING):
        part = total[j * rows : (j + 1) * rows, k * n_rows : (k + 1) * n_rows]
        tile[j, slot] = part.astype(tile.dtype)


def read_kernel(n_heads, at, *refs):
    tops, refs = refs[:RING], refs[RING:]
    bottoms, refs = refs[:RING], refs[RING:]
    cums, refs = refs[:RING], refs[RING:]
    parts, (carried, *outs) = refs[:RING], refs[RING:]
    logs = [log_of(part) for part in parts]
    p = at[0]
    heads = n_heads // RING
    half = tops[0].shape[0]
    n = carried.shape[0] - EXTRA
    width = carried.shape[1] // heads
    for j in range(RING):
        own = lax.bitwise_xor(p, j)
        total = carried[:n].astype(f32) * jnp.exp(log_over(p, logs, lambda k: k < own))
        for i in range(RING):
            if i != j:
                there = lax.bitwise_xor(p, i)
                weight = jnp.exp(log_over(p, logs, lambda k: (k < own) & (k > there)))
                total += parts[i][:n].astype(f32) * jnp.where(there < own, weight, 0.0)
        states = total.astype(bf16)
        decay = spread(jnp.exp(group_of(cums[j][...], p, heads, 1)), width)
        for i, dy in enumerate((tops[j], bottoms[j])):
            at_rows = slice(i * half, (i + 1) * half)
            scaled = (dy[...].astype(f32) * decay[at_rows]).astype(bf16)
            outs[j][at_rows] = mm(scaled, states, NT).astype(bf16)


def place_kernel(outer, share, at, *refs):
    blocks, late, out = refs[:RING], refs[RING:-1], refs[-1]
    p, z, side = at[0], at[1], at[2]
    width = out.shape[1] // (share * RING)
    last = lax.rem(z + outer - 1, outer)
    for slot in range(share):
        for j in range(RING):
            column = pl.multiple_of((slot * RING + lax.bitwise_xor(p, j)) * width, width)

            @pl.when(side * share + slot == last)
            def _():
                out[:, pl.ds(column, width)] = late[j][...]

            @pl.when(side * share + slot != last)
            def _():
                out[:, pl.ds(column, width)] = blocks[j][slot]


def call(kernel, name, grid, in_specs, out_specs, out_shape, scratch=(), after=(), flops=0):
    n_in, n_after = len(in_specs), len(after)

    def body(at, *refs):
        kernel(at, *refs[:n_in], *refs[n_in + n_after :])

    fn = pl.pallas_call(
        body,
        grid_spec=pltpu.PrefetchScalarGridSpec(
            num_scalar_prefetch=1,
            grid=grid,
            in_specs=list(in_specs) + [pl.BlockSpec(memory_space=pl.ANY)] * n_after,
            out_specs=out_specs,
            scratch_shapes=list(scratch),
        ),
        out_shape=out_shape,
        compiler_params=pltpu.CompilerParams(vmem_limit_bytes=56 * 2**20),
        cost_estimate=pl.CostEstimate(flops=flops, bytes_accessed=0, transcendentals=0),
        name=name,
    )
    return lambda *operands: fn(*operands, *after)


def local(x, dy, write_proj, read_proj, log_decay, w_in):
    rows, columns = x.shape
    half = rows // 2
    state_dim = write_proj.shape[1]
    n_heads = log_decay.shape[1]
    heads = n_heads // RING
    width = columns // n_heads
    part = heads * width
    w_rows = w_in.shape[0]
    n_seq, n_head = lax.axis_size("seq"), lax.axis_size("head")
    outer = n_seq // RING
    place = lax.axis_index("seq")
    side = lax.axis_index("head")
    p, z = place % RING, place // RING
    at = jnp.stack([p, z, side]).astype(jnp.int32)

    def swap(value, j):
        return lax.ppermute(value, "seq", [(s, s ^ j) for s in range(n_seq)])

    def along(value, d):
        return lax.ppermute(
            value, "seq", [(s, s + d * RING) for s in range(n_seq) if 0 <= s + d * RING < n_seq]
        )

    two = n_head == 2 and w_rows % (2 * LANES) == 0 and outer > 2
    share = outer // n_head

    def turn(value):
        return lax.ppermute(value, "seq", [(s, (s - RING) % n_seq) for s in range(n_seq)])

    w_first = turn(w_in)

    def const(*shape):
        return pl.BlockSpec(shape, lambda g, q: (0,) * len(shape))

    by_group = pl.BlockSpec((rows, part), lambda g, q: (0, g))
    state_spec = pl.BlockSpec((1, state_dim, part), lambda g, q: (g, 0, 0))
    log_spec = pl.BlockSpec((1, part), lambda g, q: (0, g))
    cum_spec = const(rows, LANES)
    proj_spec = const(rows, state_dim)
    message_spec = const(state_dim + EXTRA, part)
    shape = jax.ShapeDtypeStruct
    state_shape = shape((RING, state_dim, part), bf16)
    log_shape = shape((1, columns), f32)
    cum_shape = shape((rows, LANES), f32)
    message_shape = shape((state_dim + EXTRA, part), bf16)
    cum_scratch, cum_t_scratch = pltpu.VMEM((rows, LANES), f32), pltpu.VMEM((LANES, rows), f32)

    log_in_spec = const(n_heads, rows)
    log_t = log_decay.T
    own_specs = [by_group, by_group, proj_spec, proj_spec, log_in_spec]
    part_spec = const(2 * state_dim + EXTRA, part)
    parts = call(
        functools.partial(edge_kernel, n_heads),
        "edges",
        (RING,),
        own_specs,
        [part_spec] * RING,
        [shape((2 * state_dim + EXTRA, part), bf16)] * RING,
        [cum_scratch],
    )(at, x, dy, write_proj, read_proj, log_t)
    parts = [parts[0]] + [swap(parts[j], j) for j in range(1, RING)]

    write_local, read_local = call(
        functools.partial(lambda *refs: own_kernel(n_heads, *refs[1:])),
        "own_tokens",
        (RING,),
        own_specs,
        [proj_spec] * 2,
        [shape((rows, state_dim), f32)] * 2,
        [pltpu.VMEM((rows, rows), f32), cum_scratch, cum_t_scratch],
    )(at, x, dy, write_proj, read_proj, log_t)

    packed = call(
        functools.partial(lambda *refs: pack_kernel(n_heads, *refs[1:])),
        "pack",
        (1,),
        [const(rows, columns), proj_spec, proj_spec, log_in_spec],
        const(rows, columns + 3 * LANES),
        shape((rows, columns + 3 * LANES), bf16),
    )(at, dy, write_proj, read_proj, log_t)

    def halves(width, column):
        upper = pl.BlockSpec((half, width), lambda g, q: (0, column(g, q)))
        lower = pl.BlockSpec((half, width), lambda g, q: (1, column(g, q)))
        return [(upper, lower)] * (RING - 1) + [(upper, upper)]

    half_specs = halves(part, lambda g, q: g)
    mine_specs = halves(part, lambda g, q: q[0])
    tile_specs = [halves(LANES, lambda g, q, i=i: columns // LANES + i) for i in range(3)]

    def block(j, top, bottom, after=()):
        return call(
            functools.partial(lambda *refs: block_kernel(n_heads, *refs[1:])),
            "tokens",
            (RING,),
            [*half_specs[j]] + [spec for specs in tile_specs for spec in specs[j]],
            [by_group, state_spec, log_spec, cum_spec],
            [shape((rows, columns), bf16), state_shape, log_shape, cum_shape],
            [cum_t_scratch],
            after,
            flops=2 * rows * rows * columns * 16 if j else 0,
        )(at, top, bottom, *([top, bottom] * 3))

    results = [block(0, packed, packed)]
    logs = [results[0][2]]
    packed, parts, logs, read_local, w_first = lax.optimization_barrier(
        (packed, parts, logs, read_local, w_first)
    )
    from_x, from_y = lax.optimization_barrier((swap(packed, 1), swap(packed, 2)))

    def combine():
        return call(
            combine_kernel,
            "messages",
            (1,),
            [part_spec] * RING,
            [message_spec] * 2,
            [message_shape] * 2,
            after=[w_first],
        )(at, *parts)

    def merge(*pairs):
        return call(
            lambda q, *refs: merge_kernel(*refs),
            "merge",
            (1,),
            [message_spec] * 4,
            [message_spec] * 2 + [const(8, LANES)],
            [message_shape] * 2 + [shape((8, LANES), f32)],
        )(at, *pairs)

    n_halves = 2 if two else 1
    w_rest = []
    state_span, grad_span = combine()

    def go_on(mark):
        i, n_rows = len(w_rest), w_rows // n_halves
        if i < n_halves:
            piece = call(
                lambda at, ref, out: out.__setitem__(Ellipsis, ref[...]),
                "half",
                (RING,),
                [pl.BlockSpec((n_rows, part), lambda g, q: (i, g))],
                pl.BlockSpec((n_rows, part), lambda g, q: (0, g)),
                shape((n_rows, columns), bf16),
                after=[mark],
            )(at, w_first)
            w_rest.append(turn(piece))

    d = 1
    while d < outer:
        state_got, grad_got = along(state_span, d), along(grad_span, -d)
        if d == 1:
            state_part, grad_part = state_got, grad_got
        else:
            state_part, grad_part, mark = merge(state_part, state_got, grad_part, grad_got)
            go_on(mark)
        if 2 * d < outer:
            state_span, grad_span, mark = merge(state_span, state_got, grad_span, grad_got)
            go_on(mark)
        d *= 2
    blocks = [(packed, packed), (from_x, from_x), (from_y, from_y)]
    blocks.append((swap(from_x[:half], 2), swap(from_y[half:], 1)))
    results.append(block(1, *blocks[1], after=[grad_part, w_rest[0]]))
    results += [block(j, *blocks[j]) for j in range(2, RING - 1)]
    logs += [v[2] for v in results[1:]]
    logs, blocks[-1] = lax.optimization_barrier((logs, blocks[-1]))
    results.append(block(RING - 1, *blocks[-1]))
    logs.append(results[-1][2])
    logs, grad_part = lax.optimization_barrier((logs, grad_part))
    grad_parts = [grad_part] + [swap(grad_part, j) for j in range(1, RING)]
    local_acts, fronts, _, cums = zip(*results)
    w_last = [turn(v) for v in w_rest]
    w_pieces = [w_in, w_first, *w_rest, *w_last[:1]]
    if not two:
        while len(w_pieces) < outer:
            w_pieces.append(turn(w_pieces[-1]))

    ring_grads = call(
        ring_kernel,
        "ring_grads",
        (RING,),
        [state_spec] * RING + [log_spec] * RING,
        [state_spec] * RING,
        [state_shape] * RING,
    )(at, *fronts, *logs)

    n_w = outer - 1 if two else outer
    tall = pl.BlockSpec((RING * rows, part), lambda g, q: (0, g))
    tile_shapes = [(RING, outer, rows, w_rows)]
    if two:
        tile_shapes = [(RING, share, rows, w_rows)] * 2 + [(RING * rows, w_rows // 2)]
    w_total = sum(v.shape[0] for v in w_pieces)
    acts, act_grad, write_carry, *tiles = call(
        functools.partial(finish_kernel, n_heads, n_w, len(w_pieces), outer, share),
        "finish",
        (RING,),
        [by_group] * RING
        + [state_spec] * RING
        + [message_spec] * RING
        + [log_spec] * RING
        + [spec[0] for spec in tile_specs[0]]
        + [spec[1] for spec in tile_specs[0]]
        + [cum_spec] * RING
        + [pl.BlockSpec((v.shape[0], part), lambda g, q: (0, g)) for v in w_pieces]
        + [by_group],
        [tall, by_group, proj_spec] + [const(*v) for v in tile_shapes],
        [
            shape((RING * rows, columns), bf16),
            shape((rows, columns), bf16),
            shape((rows, state_dim), f32),
        ]
        + [shape(v, bf16) for v in tile_shapes],
        [pltpu.VMEM((RING * rows, w_total), f32)],
        flops=2 * RING * rows * columns * w_total,
    )(
        at,
        *local_acts,
        *ring_grads,
        *grad_parts,
        *logs,
        *[top for top, _ in blocks],
        *[bottom for _, bottom in blocks],
        *cums,
        *w_pieces,
        x,
    )

    def to_owners(tile):
        return [tile[0]] + [swap(tile[j], j) for j in range(1, RING)]

    if two:
        mine, theirs, late = tiles
        got = lax.ppermute(theirs, "head", [(0, 1), (1, 0)])
        early = (mine.astype(f32) + got.astype(f32)).astype(bf16)
        early_sent = to_owners(early)
        late_b = mm(acts, w_last[1], NT).astype(bf16)
        late = jnp.concatenate([late, late_b], axis=1)

        def owner(s):
            return (s // RING + outer - 1) % outer // share

        both_axes = ("seq", "head")
        got = lax.ppermute(
            late, both_axes, [(2 * s + 1 - owner(s), 2 * s + owner(s)) for s in range(n_seq)]
        )
        late = (late.astype(f32) + got.astype(f32)).astype(bf16).reshape(RING, rows, w_rows)
        late, early_sent = lax.optimization_barrier((late, early_sent))
    read_parts = call(
        functools.partial(read_kernel, n_heads),
        "read_carry",
        (1,),
        [spec[0] for spec in mine_specs]
        + [spec[1] for spec in mine_specs]
        + [cum_spec] * RING + [part_spec] * RING + [message_spec],
        [proj_spec] * RING,
        [shape((rows, state_dim), bf16)] * RING,
        after=[late_b] if two else [],
    )(
        at,
        *[top for top, _ in blocks],
        *[bottom for _, bottom in blocks],
        *cums,
        *parts,
        state_part,
    )
    if two:
        late, read_parts = lax.optimization_barrier((late, read_parts))
    read_carry = read_parts[0].astype(f32) + sum(
        swap(read_parts[j], j).astype(f32) for j in range(1, RING)
    )
    both = jnp.stack([write_local + write_carry, read_local + read_carry])
    if n_head == 2:
        both = both + lax.ppermute(both, "head", [(0, 1), (1, 0)])
    else:
        both = lax.psum(both, "head")

    if two:
        late = [late[0]] + [
            lax.ppermute(
                late[j],
                both_axes,
                [(2 * s + owner(s), 2 * (s ^ j) + owner(s)) for s in range(n_seq)],
            )
            for j in range(1, RING)
        ]
        input_grad = pl.pallas_call(
            functools.partial(place_kernel, outer, share),
            in_specs=[pl.BlockSpec(memory_space=pltpu.SMEM)]
            + [pl.BlockSpec(memory_space=pltpu.VMEM)] * (2 * RING),
            out_specs=pl.BlockSpec(memory_space=pltpu.VMEM),
            out_shape=shape((rows, share * RING * w_rows), bf16),
            compiler_params=pltpu.CompilerParams(vmem_limit_bytes=32 * 2**20),
            name="place",
        )(at, *early_sent, *late)
    else:
        summed = lax.psum_scatter(tiles[0], "head", scatter_dimension=1, tiled=True)
        pieces = jnp.take(jnp.stack(to_owners(summed)), p ^ jnp.arange(RING), axis=0)
        input_grad = pieces.transpose(2, 1, 0, 3).reshape(rows, share * RING * w_rows)
    return (input_grad, act_grad, both[0], both[1])


def solution(mesh):
    return jax.shard_map(
        local,
        mesh=mesh,
        in_specs=(
            P("seq", "head"),
            P("seq", "head"),
            P("seq", None),
            P("seq", None),
            P("seq", "head"),
            P("seq", "head"),
        ),
        out_specs=(P("seq", "head"), P("seq", "head"), P("seq", None), P("seq", None)),
        check_vma=False,
    )
```

```python
import functools

import jax
import jax.numpy as jnp
from jax import lax
from jax.experimental import pallas as pl
from jax.experimental.pallas import tpu as pltpu
from jax.sharding import PartitionSpec as P

RING = 4
LANES = 128
EXTRA = 16
NT = (((1,), (1,)), ((), ()))
TN = (((0,), (0,)), ((), ()))
NN = (((1,), (0,)), ((), ()))
bf16, f32 = jnp.bfloat16, jnp.float32


def mm(a, b, dims):
    return lax.dot_general(a, b, dims, preferred_element_type=f32)


def mm_exact(a, b, dims):
    return lax.dot_general(a, b, dims, precision=lax.Precision.HIGHEST, preferred_element_type=f32)


def spread(columns, width):
    rows = columns.shape[0]
    return jnp.concatenate(
        [jnp.broadcast_to(columns[:, h : h + 1], (rows, width)) for h in range(columns.shape[1])],
        axis=1,
    )


def iota(shape, axis):
    return lax.broadcasted_iota(jnp.int32, shape, axis)


def three_parts(value):
    first = value.astype(bf16).astype(f32)
    second = (value - first).astype(bf16).astype(f32)
    return first, second, value - first - second


def cumulate(n_heads, log_tiles, cum, cum_t):
    parts = jnp.concatenate([tile[...] for tile in log_tiles], axis=0)
    rows = parts.shape[0]
    source, head = iota((LANES, LANES), 0), iota((LANES, LANES), 1)
    pick = (source < 3 * n_heads) & (lax.rem(source, n_heads) == head)
    logs = mm(parts, pick.astype(f32).astype(bf16), NN)
    upto = (iota((rows, rows), 0) <= iota((rows, rows), 1)).astype(f32)
    cum[...] = mm_exact(upto, logs, TN)
    if cum_t is not None:
        cum_t[...] = mm_exact(logs, upto, TN)


def group_of(value, g, heads, axis):
    shift = lax.rem(LANES - g * heads, LANES)
    value = pltpu.roll(value, shift, axis)
    return value[:, :heads] if axis == 1 else value[:heads]


def diagonal(heads, half, lo, col, row, each):
    later = iota((half, half), 1) >= iota((half, half), 0)
    for h in range(heads):
        log = row[h : h + 1, lo : lo + half] - col[lo : lo + half, h : h + 1]
        each(h, jnp.exp(jnp.where(later, log, -jnp.inf)))


def cumulate_own(log_t, cum, cum_t):
    n_heads, rows = log_t.shape
    logs = jnp.concatenate([log_t[...], jnp.zeros((LANES - n_heads, rows), f32)], axis=0)
    upto = (iota((rows, rows), 0) <= iota((rows, rows), 1)).astype(f32)
    cum[...] = mm_exact(upto, logs, (((0,), (1,)), ((), ())))
    if cum_t is not None:
        cum_t[...] = mm_exact(logs, upto, NN)


def edge_kernel(n_heads, at, x, dy, b, c, log_t, *refs):
    messages, cum = refs[:RING], refs[RING]
    g = pl.program_id(0)
    heads = n_heads // RING
    rows = x.shape[0]
    width = x.shape[1] // heads
    n = b.shape[1]

    @pl.when(g == 0)
    def _():
        cumulate_own(log_t, cum, None)

    col = group_of(cum[...], g, heads, 1)
    last = col[rows - 1 : rows, :]
    tailed = (x[...].astype(f32) * spread(jnp.exp(last - col), width)).astype(bf16)
    decayed = (dy[...].astype(f32) * spread(jnp.exp(col), width)).astype(bf16)
    ends = mm(b[...], tailed, TN).astype(bf16)
    fronts = mm(c[...], decayed, TN).astype(bf16)
    log = spread(last, width)
    for j in range(RING):

        @pl.when(lax.bitwise_xor(at[0], g) == j)
        def _():
            messages[j][:n] = ends
            messages[j][n : 2 * n] = fronts
            write_log(messages[j], log)


def pack_kernel(n_heads, dy, b, c, log_t, out):
    rows, columns = dy.shape
    fill = jnp.zeros((LANES - 3 * n_heads, rows), f32)
    logs = jnp.concatenate([*three_parts(log_t[...]), fill], axis=0)
    out[:, :columns] = dy[...]
    out[:, columns : columns + LANES] = b[...]
    out[:, columns + LANES : columns + 2 * LANES] = c[...]
    out[:, columns + 2 * LANES :] = logs.T.astype(bf16)


def own_kernel(n_heads, x, dy, b, c, log_t, write_local, read_local, total, cum, cum_t):
    g = pl.program_id(0)
    heads = n_heads // RING
    rows = x.shape[0]
    half = rows // 2
    width = x.shape[1] // heads

    @pl.when(g == 0)
    def _():
        total[...] = jnp.zeros_like(total)
        cumulate_own(log_t, cum, cum_t)

    col, row = group_of(cum[...], g, heads, 1), group_of(cum_t[...], g, heads, 0)
    mid = col[half - 1 : half, :]
    for i in range(2):
        lo = i * half
        parts = []

        def add(h, decay):
            span = slice(h * width, (h + 1) * width)
            parts.append(decay * mm(x[lo : lo + half, span], dy[lo : lo + half, span], NT))

        diagonal(heads, half, lo, col, row, add)
        total[lo : lo + half, lo : lo + half] += sum(parts)
    early = (x[:half].astype(f32) * spread(jnp.exp(mid - col[:half]), width)).astype(bf16)
    late = (dy[half:].astype(f32) * spread(jnp.exp(col[half:] - mid), width)).astype(bf16)
    total[:half, half:] += mm(early, late, NT)

    @pl.when(g == pl.num_programs(0) - 1)
    def _():
        write_local[...] = mm_exact(total[...], c[...].astype(f32), NN)
        read_local[...] = mm_exact(total[...], b[...].astype(f32), TN)


def block_kernel(n_heads, top, bottom, *refs):
    tiles, (act, fronts, log_row, cum_out, cum_t) = refs[:6], refs[6:]
    b = jnp.concatenate([tiles[0][...], tiles[1][...]], axis=0)
    c = jnp.concatenate([tiles[2][...], tiles[3][...]], axis=0)
    g = pl.program_id(0)
    heads = n_heads // RING
    half = top.shape[0]
    rows = 2 * half
    width = top.shape[1] // heads

    @pl.when(g == 0)
    def _():
        cumulate(n_heads, tiles[4:], cum_out, cum_t)

    col, row = group_of(cum_out[...], g, heads, 1), group_of(cum_t[...], g, heads, 0)
    mid, last = col[half - 1 : half, :], col[rows - 1 : rows, :]
    log_row[...] = spread(last, width)
    scores = mm(b, c, NT)
    late_f = bottom[...].astype(f32) * spread(jnp.exp(col[half:] - mid), width)
    late = late_f.astype(bf16)
    first = (top[...].astype(f32) * spread(jnp.exp(col[:half]), width)).astype(bf16)
    second = (late_f * spread(jnp.exp(mid), width)).astype(bf16)
    fronts[0] = (mm(c[:half], first, TN) + mm(c[half:], second, TN)).astype(bf16)
    cross = mm(scores[:half, half:].astype(bf16), late, NN)
    to_mid = jnp.exp(mid - col[:half])
    for i, dy in enumerate((top, bottom)):
        lo = i * half
        score = scores[lo : lo + half, lo : lo + half]

        def put(h, decay):
            span = slice(h * width, (h + 1) * width)
            out = mm((decay * score).astype(bf16), dy[:, span], NN)
            if i == 0:
                out += cross[:, span] * to_mid[:, h : h + 1]
            act[lo : lo + half, span] = out.astype(act.dtype)

        diagonal(heads, half, lo, col, row, put)


def log_over(p, logs, wanted):
    total = jnp.zeros_like(logs[0])
    for k in range(RING):
        total += jnp.where(wanted(lax.bitwise_xor(p, k)), logs[k], 0.0)
    return total


def combine_kernel(at, *refs):
    parts, (state_out, grad_out) = refs[:RING], refs[RING:]
    n = state_out.shape[0] - EXTRA
    logs = [log_of(part) for part in parts]
    p = at[0]
    state, grad = 0.0, 0.0
    for j in range(RING):
        own = lax.bitwise_xor(p, j)
        state += parts[j][:n].astype(f32) * jnp.exp(log_over(p, logs, lambda k: k > own))
        grad += parts[j][n : 2 * n].astype(f32) * jnp.exp(log_over(p, logs, lambda k: k < own))
    for out, value in ((state_out, state), (grad_out, grad)):
        out[:n] = value.astype(bf16)
        write_log(out, sum(logs))


def write_log(out, log):
    n, width = out.shape
    row = iota((EXTRA, width), 0)
    rows = jnp.zeros((EXTRA, width), f32)
    for i, part in enumerate(three_parts(log)):
        rows = jnp.where(row == i, part, rows)
    out[n - EXTRA :] = rows.astype(bf16)


def log_of(message):
    n = message.shape[0] - EXTRA
    tail = message[n:].astype(f32)
    return tail[0:1] + tail[1:2] + tail[2:3]


def merge_kernel(*refs):
    for near, far, out in ((*refs[:2], refs[4]), (*refs[2:4], refs[5])):
        n = near.shape[0] - EXTRA
        log = log_of(near)
        out[:n] = (near[:n].astype(f32) + far[:n].astype(f32) * jnp.exp(log)).astype(bf16)
        write_log(out, log + log_of(far))


def ring_kernel(at, *refs):
    fronts, logs, outs = refs[:RING], [r[...] for r in refs[RING : 2 * RING]], refs[2 * RING :]
    p = at[0]
    for j in range(RING):
        own = lax.bitwise_xor(p, j)
        total = 0.0
        for i in range(RING):
            if i != j:
                there = lax.bitwise_xor(p, i)
                weight = jnp.exp(log_over(p, logs, lambda k: (k > own) & (k < there)))
                total += fronts[i][0].astype(f32) * jnp.where(there > own, weight, 0.0)
        outs[j][0] = total.astype(bf16)


def finish_kernel(n_heads, n_w, n_pieces, outer, share, at, *refs):
    locals_, refs = refs[:RING], refs[RING:]
    rings, refs = refs[:RING], refs[RING:]
    quarters, refs = refs[:RING], refs[RING:]
    logs, refs = [r[...] for r in refs[:RING]], refs[RING:]
    tops, refs = refs[:RING], refs[RING:]
    bottoms, refs = refs[:RING], refs[RING:]
    cums, refs = refs[:RING], refs[RING:]
    w, refs = refs[:n_pieces], refs[n_pieces:]
    x, acts, own, write, *tiles, total = refs
    g, p = pl.program_id(0), at[0]
    heads = n_heads // RING
    rows = own.shape[0]
    width = own.shape[1] // heads
    n = quarters[0].shape[0] - EXTRA
    source = lax.bitwise_xor(p, g)
    carried = quarters[0][:n].astype(f32)
    for j in range(1, RING):
        carried = jnp.where(source == j, quarters[j][:n].astype(f32), carried)

    @pl.when(g == 0)
    def _():
        write[...] = jnp.zeros_like(write)
        total[...] = jnp.zeros_like(total)

    for j in range(RING):
        col = group_of(cums[j][...], g, heads, 1)
        tail = spread(jnp.exp(col[rows - 1 : rows, :] - col), width)
        place = lax.bitwise_xor(p, j)
        weight = jnp.exp(log_over(p, logs, lambda k: k > place))
        grads = (carried * weight + rings[j][0].astype(f32)).astype(bf16)
        b = jnp.concatenate([tops[j][...], bottoms[j][...]], axis=0)
        out = mm(b, grads, NN) * tail + locals_[j][...].astype(f32)
        out = out.astype(acts.dtype)
        acts[j * rows : (j + 1) * rows, :] = out
        if j == 0:
            own[...] = out
            write[...] += mm((x[...].astype(f32) * tail).astype(bf16), grads, NT)
    n_rows, column = w[0].shape[0], 0
    for piece in w:
        total[:, column : column + piece.shape[0]] += mm(acts[...], piece[...], NT)
        column += piece.shape[0]

    @pl.when(g == pl.num_programs(0) - 1)
    def _():
        if len(tiles) == 1:
            for k in range(n_w):
                put_tile(tiles[0], lax.rem(at[1] + k, outer), total, k, n_rows)
        else:
            for tile in tiles:
                tile[...] = jnp.zeros_like(tile)
            for k in range(n_w):
                o = lax.rem(at[1] + k, outer)
                for tile, side in zip(tiles, (at[2], 1 - at[2])):

                    @pl.when(lax.div(o, share) == side)
                    def _():
                        put_tile(tile, lax.rem(o, share), total, k, n_rows)


def put_tile(tile, slot, total, k, n_rows):
    rows = total.shape[0] // RING
    for j in range(RING):
        part = total[j * rows : (j + 1) * rows, k * n_rows : (k + 1) * n_rows]
        tile[j, slot] = part.astype(tile.dtype)


def read_kernel(n_heads, at, *refs):
    tops, refs = refs[:RING], refs[RING:]
    bottoms, refs = refs[:RING], refs[RING:]
    cums, refs = refs[:RING], refs[RING:]
    parts, (carried, *outs) = refs[:RING], refs[RING:]
    logs = [log_of(part) for part in parts]
    p = at[0]
    heads = n_heads // RING
    half = tops[0].shape[0]
    n = carried.shape[0] - EXTRA
    width = carried.shape[1] // heads
    for j in range(RING):
        own = lax.bitwise_xor(p, j)
        total = carried[:n].astype(f32) * jnp.exp(log_over(p, logs, lambda k: k < own))
        for i in range(RING):
            if i != j:
                there = lax.bitwise_xor(p, i)
                weight = jnp.exp(log_over(p, logs, lambda k: (k < own) & (k > there)))
                total += parts[i][:n].astype(f32) * jnp.where(there < own, weight, 0.0)
        states = total.astype(bf16)
        decay = spread(jnp.exp(group_of(cums[j][...], p, heads, 1)), width)
        for i, dy in enumerate((tops[j], bottoms[j])):
            at_rows = slice(i * half, (i + 1) * half)
            scaled = (dy[...].astype(f32) * decay[at_rows]).astype(bf16)
            outs[j][at_rows] = mm(scaled, states, NT).astype(bf16)


def place_kernel(outer, share, at, *refs):
    blocks, late, out = refs[:RING], refs[RING:-1], refs[-1]
    p, z, side = at[0], at[1], at[2]
    width = out.shape[1] // (share * RING)
    last = lax.rem(z + outer - 1, outer)
    for slot in range(share):
        for j in range(RING):
            column = pl.multiple_of((slot * RING + lax.bitwise_xor(p, j)) * width, width)

            @pl.when(side * share + slot == last)
            def _():
                out[:, pl.ds(column, width)] = late[j][...]

            @pl.when(side * share + slot != last)
            def _():
                out[:, pl.ds(column, width)] = blocks[j][slot]


def call(kernel, name, grid, in_specs, out_specs, out_shape, scratch=(), after=(), flops=0):
    n_in, n_after = len(in_specs), len(after)

    def body(at, *refs):
        kernel(at, *refs[:n_in], *refs[n_in + n_after :])

    fn = pl.pallas_call(
        body,
        grid_spec=pltpu.PrefetchScalarGridSpec(
            num_scalar_prefetch=1,
            grid=grid,
            in_specs=list(in_specs) + [pl.BlockSpec(memory_space=pl.ANY)] * n_after,
            out_specs=out_specs,
            scratch_shapes=list(scratch),
        ),
        out_shape=out_shape,
        compiler_params=pltpu.CompilerParams(vmem_limit_bytes=56 * 2**20),
        cost_estimate=pl.CostEstimate(flops=flops, bytes_accessed=0, transcendentals=0),
        name=name,
    )
    return lambda *operands: fn(*operands, *after)


def local(x, dy, write_proj, read_proj, log_decay, w_in):
    rows, columns = x.shape
    half = rows // 2
    state_dim = write_proj.shape[1]
    n_heads = log_decay.shape[1]
    heads = n_heads // RING
    width = columns // n_heads
    part = heads * width
    w_rows = w_in.shape[0]
    n_seq, n_head = lax.axis_size("seq"), lax.axis_size("head")
    outer = n_seq // RING
    place = lax.axis_index("seq")
    side = lax.axis_index("head")
    p, z = place % RING, place // RING
    at = jnp.stack([p, z, side]).astype(jnp.int32)

    def swap(value, j):
        return lax.ppermute(value, "seq", [(s, s ^ j) for s in range(n_seq)])

    def along(value, d):
        return lax.ppermute(
            value, "seq", [(s, s + d * RING) for s in range(n_seq) if 0 <= s + d * RING < n_seq]
        )

    two = n_head == 2 and w_rows % LANES == 0 and outer == 4
    share = outer // n_head

    def turn(value):
        return lax.ppermute(value, "seq", [(s, (s - RING) % n_seq) for s in range(n_seq)])

    w_first = turn(w_in)

    def const(*shape):
        return pl.BlockSpec(shape, lambda g, q: (0,) * len(shape))

    by_group = pl.BlockSpec((rows, part), lambda g, q: (0, g))
    state_spec = pl.BlockSpec((1, state_dim, part), lambda g, q: (g, 0, 0))
    log_spec = pl.BlockSpec((1, part), lambda g, q: (0, g))
    cum_spec = const(rows, LANES)
    proj_spec = const(rows, state_dim)
    message_spec = const(state_dim + EXTRA, part)
    shape = jax.ShapeDtypeStruct
    state_shape = shape((RING, state_dim, part), bf16)
    log_shape = shape((1, columns), f32)
    cum_shape = shape((rows, LANES), f32)
    message_shape = shape((state_dim + EXTRA, part), bf16)
    cum_scratch, cum_t_scratch = pltpu.VMEM((rows, LANES), f32), pltpu.VMEM((LANES, rows), f32)

    log_in_spec = const(n_heads, rows)
    log_t = log_decay.T
    own_specs = [by_group, by_group, proj_spec, proj_spec, log_in_spec]
    part_spec = const(2 * state_dim + EXTRA, part)
    parts = call(
        functools.partial(edge_kernel, n_heads),
        "edges",
        (RING,),
        own_specs,
        [part_spec] * RING,
        [shape((2 * state_dim + EXTRA, part), bf16)] * RING,
        [cum_scratch],
    )(at, x, dy, write_proj, read_proj, log_t)

    write_local, read_local = call(
        functools.partial(lambda *refs: own_kernel(n_heads, *refs[1:])),
        "own_tokens",
        (RING,),
        own_specs,
        [proj_spec] * 2,
        [shape((rows, state_dim), f32)] * 2,
        [pltpu.VMEM((rows, rows), f32), cum_scratch, cum_t_scratch],
    )(at, x, dy, write_proj, read_proj, log_t)

    packed = call(
        functools.partial(lambda *refs: pack_kernel(n_heads, *refs[1:])),
        "pack",
        (1,),
        [const(rows, columns), proj_spec, proj_spec, log_in_spec],
        const(rows, columns + 3 * LANES),
        shape((rows, columns + 3 * LANES), bf16),
    )(at, dy, write_proj, read_proj, log_t)

    def halves(width, column):
        upper = pl.BlockSpec((half, width), lambda g, q: (0, column(g, q)))
        lower = pl.BlockSpec((half, width), lambda g, q: (1, column(g, q)))
        return [(upper, lower)] * (RING - 1) + [(upper, upper)]

    half_specs = halves(part, lambda g, q: g)
    mine_specs = halves(part, lambda g, q: q[0])
    tile_specs = [halves(LANES, lambda g, q, i=i: columns // LANES + i) for i in range(3)]

    def block(j, top, bottom, after=()):
        return call(
            functools.partial(lambda *refs: block_kernel(n_heads, *refs[1:])),
            "tokens",
            (RING,),
            [*half_specs[j]] + [spec for specs in tile_specs for spec in specs[j]],
            [by_group, state_spec, log_spec, cum_spec],
            [shape((rows, columns), bf16), state_shape, log_shape, cum_shape],
            [cum_t_scratch],
            after,
            flops=2 * rows * rows * columns * 16 if j else 0,
        )(at, top, bottom, *([top, bottom] * 3))

    results = [block(0, packed, packed)]
    from_x, from_y = swap(packed, 1), swap(packed, 2)
    results.append(block(1, from_x, from_x, after=[w_first, read_local]))
    results.append(block(2, from_y, from_y))
    from_x, from_y, parts = lax.optimization_barrier((from_x, from_y, parts))
    parts = [parts[0]] + [swap(parts[j], j) for j in range(1, RING)]
    logs = [v[2] for v in results]
    from_x, from_y, logs, parts = lax.optimization_barrier((from_x, from_y, logs, parts))
    blocks = [(packed, packed), (from_x, from_x), (from_y, from_y)]
    blocks.append((swap(from_x[:half], 2), swap(from_y[half:], 1)))
    results.append(block(RING - 1, *blocks[-1]))
    logs.append(results[-1][2])
    local_acts, fronts, _, cums = zip(*results)

    def combine():
        return call(
            combine_kernel,
            "messages",
            (1,),
            [part_spec] * RING,
            [message_spec] * 2,
            [message_shape] * 2,
        )(at, *parts)

    def merge(*pairs, after=()):
        return call(
            lambda q, *refs: merge_kernel(*refs),
            "merge",
            (1,),
            [message_spec] * 4,
            [message_spec] * 2,
            [message_shape] * 2,
            after=after,
        )(at, *pairs)

    w_pieces = [w_in, w_first]
    while len(w_pieces) < outer - 1:
        w_pieces.append(turn(w_pieces[-1]))
    state_span, grad_span = combine()
    d = 1
    while d < outer:
        state_got, grad_got = along(state_span, d), along(grad_span, -d)
        if d == 1:
            state_part, grad_part = state_got, grad_got
        else:
            after = [logs[-1]] if 2 * d >= outer else []
            state_part, grad_part = merge(
                state_part, state_got, grad_part, grad_got, after=after
            )
        if 2 * d < outer:
            state_span, grad_span = merge(state_span, state_got, grad_span, grad_got)
        d *= 2
    grad_part, w_last = lax.optimization_barrier((grad_part, w_pieces[-1]))
    w_last = turn(w_last)
    if not two:
        w_pieces.append(w_last)
    grad_parts = [grad_part] + [swap(grad_part, j) for j in range(1, RING)]

    ring_grads = call(
        ring_kernel,
        "ring_grads",
        (RING,),
        [state_spec] * RING + [log_spec] * RING,
        [state_spec] * RING,
        [state_shape] * RING,
    )(at, *fronts, *logs)

    n_w = outer - 1 if two else outer
    tall = pl.BlockSpec((RING * rows, part), lambda g, q: (0, g))
    tile_shapes = [(RING, outer, rows, w_rows)]
    if two:
        tile_shapes = [(RING, share, rows, w_rows)] * 2
    w_total = sum(v.shape[0] for v in w_pieces)
    acts, act_grad, write_carry, *tiles = call(
        functools.partial(finish_kernel, n_heads, n_w, len(w_pieces), outer, share),
        "finish",
        (RING,),
        [by_group] * RING
        + [state_spec] * RING
        + [message_spec] * RING
        + [log_spec] * RING
        + [spec[0] for spec in tile_specs[0]]
        + [spec[1] for spec in tile_specs[0]]
        + [cum_spec] * RING
        + [pl.BlockSpec((v.shape[0], part), lambda g, q: (0, g)) for v in w_pieces]
        + [by_group],
        [tall, by_group, proj_spec] + [const(*v) for v in tile_shapes],
        [
            shape((RING * rows, columns), bf16),
            shape((rows, columns), bf16),
            shape((rows, state_dim), f32),
        ]
        + [shape(v, bf16) for v in tile_shapes],
        [pltpu.VMEM((RING * rows, w_total), f32)],
        flops=2 * RING * rows * columns * w_total,
    )(
        at,
        *local_acts,
        *ring_grads,
        *grad_parts,
        *logs,
        *[top for top, _ in blocks],
        *[bottom for _, bottom in blocks],
        *cums,
        *w_pieces,
        x,
    )

    def to_owners(tile):
        return [tile[0]] + [swap(tile[j], j) for j in range(1, RING)]

    read_parts = call(
        functools.partial(read_kernel, n_heads),
        "read_carry",
        (1,),
        [spec[0] for spec in mine_specs]
        + [spec[1] for spec in mine_specs]
        + [cum_spec] * RING + [part_spec] * RING + [message_spec],
        [proj_spec] * RING,
        [shape((rows, state_dim), bf16)] * RING,
        after=[write_carry],
    )(
        at,
        *[top for top, _ in blocks],
        *[bottom for _, bottom in blocks],
        *cums,
        *parts,
        state_part,
    )
    read_got = [swap(read_parts[j], j) for j in range(1, RING)]
    if two:
        mine, theirs = tiles
        got = lax.ppermute(theirs, "head", [(0, 1), (1, 0)])
        early = (mine.astype(f32) + got.astype(f32)).astype(bf16)
        early, read_own, w_last = lax.optimization_barrier((early, read_parts[0], w_last))
        late = mm(acts, w_last, NT).astype(bf16)

        def owner(s):
            return (s // RING + outer - 1) % outer // share

        both_axes = ("seq", "head")
        got = lax.ppermute(
            late, both_axes, [(2 * s + 1 - owner(s), 2 * s + owner(s)) for s in range(n_seq)]
        )
        early_sent = to_owners(early)
        got, read_got, early_sent = lax.optimization_barrier((got, read_got, early_sent))
        late = (late.astype(f32) + got.astype(f32)).astype(bf16).reshape(RING, rows, w_rows)
        late = [late[0]] + [
            lax.ppermute(
                late[j],
                both_axes,
                [(2 * s + owner(s), 2 * (s ^ j) + owner(s)) for s in range(n_seq)],
            )
            for j in range(1, RING)
        ]
        input_grad = pl.pallas_call(
            functools.partial(place_kernel, outer, share),
            in_specs=[pl.BlockSpec(memory_space=pltpu.SMEM)]
            + [pl.BlockSpec(memory_space=pltpu.VMEM)] * (2 * RING),
            out_specs=pl.BlockSpec(memory_space=pltpu.VMEM),
            out_shape=shape((rows, share * RING * w_rows), bf16),
            compiler_params=pltpu.CompilerParams(vmem_limit_bytes=32 * 2**20),
            name="place",
        )(at, *early_sent, *late)
    else:
        summed = lax.psum_scatter(tiles[0], "head", scatter_dimension=1, tiled=True)
        pieces = jnp.take(jnp.stack(to_owners(summed)), p ^ jnp.arange(RING), axis=0)
        input_grad = pieces.transpose(2, 1, 0, 3).reshape(rows, share * RING * w_rows)
    read_carry = read_parts[0].astype(f32) + sum(v.astype(f32) for v in read_got)
    both = jnp.stack([write_local + write_carry, read_local + read_carry])
    if n_head == 2:
        both = both + lax.ppermute(both, "head", [(0, 1), (1, 0)])
    else:
        both = lax.psum(both, "head")
    return (input_grad, act_grad, both[0], both[1])


def solution(mesh):
    return jax.shard_map(
        local,
        mesh=mesh,
        in_specs=(
            P("seq", "head"),
            P("seq", "head"),
            P("seq", None),
            P("seq", None),
            P("seq", "head"),
            P("seq", "head"),
        ),
        out_specs=(P("seq", "head"), P("seq", "head"), P("seq", None), P("seq", None)),
        check_vma=False,
    )
```

```python
import functools

import jax
import jax.numpy as jnp
from jax import lax
from jax.experimental import pallas as pl
from jax.experimental.pallas import tpu as pltpu
from jax.sharding import PartitionSpec as P

RING = 4
LANES = 128
EXTRA = 16
NT = (((1,), (1,)), ((), ()))
TN = (((0,), (0,)), ((), ()))
NN = (((1,), (0,)), ((), ()))
bf16, f32 = jnp.bfloat16, jnp.float32


def mm(a, b, dims):
    return lax.dot_general(a, b, dims, preferred_element_type=f32)


def mm_exact(a, b, dims):
    return lax.dot_general(a, b, dims, precision=lax.Precision.HIGHEST, preferred_element_type=f32)


def spread(columns, width):
    rows = columns.shape[0]
    return jnp.concatenate(
        [jnp.broadcast_to(columns[:, h : h + 1], (rows, width)) for h in range(columns.shape[1])],
        axis=1,
    )


def iota(shape, axis):
    return lax.broadcasted_iota(jnp.int32, shape, axis)


def three_parts(value):
    first = value.astype(bf16).astype(f32)
    second = (value - first).astype(bf16).astype(f32)
    return first, second, value - first - second


def cumulate(n_heads, log_tiles, cum, cum_t):
    parts = jnp.concatenate([tile[...] for tile in log_tiles], axis=0)
    rows = parts.shape[0]
    source, head = iota((LANES, LANES), 0), iota((LANES, LANES), 1)
    pick = (source < 3 * n_heads) & (lax.rem(source, n_heads) == head)
    logs = mm(parts, pick.astype(f32).astype(bf16), NN)
    upto = (iota((rows, rows), 0) <= iota((rows, rows), 1)).astype(f32)
    cum[...] = mm_exact(upto, logs, TN)
    if cum_t is not None:
        cum_t[...] = mm_exact(logs, upto, TN)


def group_of(value, g, heads, axis):
    shift = lax.rem(LANES - g * heads, LANES)
    value = pltpu.roll(value, shift, axis)
    return value[:, :heads] if axis == 1 else value[:heads]


def diagonal(heads, half, lo, col, row, each):
    later = iota((half, half), 1) >= iota((half, half), 0)
    for h in range(heads):
        log = row[h : h + 1, lo : lo + half] - col[lo : lo + half, h : h + 1]
        each(h, jnp.exp(jnp.where(later, log, -jnp.inf)))


def cumulate_own(log_t, cum, cum_t):
    n_heads, rows = log_t.shape
    logs = jnp.concatenate([log_t[...], jnp.zeros((LANES - n_heads, rows), f32)], axis=0)
    upto = (iota((rows, rows), 0) <= iota((rows, rows), 1)).astype(f32)
    cum[...] = mm_exact(upto, logs, (((0,), (1,)), ((), ())))
    if cum_t is not None:
        cum_t[...] = mm_exact(logs, upto, NN)


def edge_kernel(n_heads, at, x, dy, b, c, log_t, *refs):
    messages, cum = refs[:RING], refs[RING]
    g = pl.program_id(0)
    heads = n_heads // RING
    rows = x.shape[0]
    width = x.shape[1] // heads
    n = b.shape[1]

    @pl.when(g == 0)
    def _():
        cumulate_own(log_t, cum, None)

    col = group_of(cum[...], g, heads, 1)
    last = col[rows - 1 : rows, :]
    tailed = (x[...].astype(f32) * spread(jnp.exp(last - col), width)).astype(bf16)
    decayed = (dy[...].astype(f32) * spread(jnp.exp(col), width)).astype(bf16)
    ends = mm(b[...], tailed, TN).astype(bf16)
    fronts = mm(c[...], decayed, TN).astype(bf16)
    log = spread(last, width)
    for j in range(RING):

        @pl.when(lax.bitwise_xor(at[0], g) == j)
        def _():
            messages[j][:n] = ends
            messages[j][n : 2 * n] = fronts
            write_log(messages[j], log)


def pack_kernel(n_heads, dy, b, c, log_t, out):
    rows, columns = dy.shape
    fill = jnp.zeros((LANES - 3 * n_heads, rows), f32)
    logs = jnp.concatenate([*three_parts(log_t[...]), fill], axis=0)
    out[:, :columns] = dy[...]
    out[:, columns : columns + LANES] = b[...]
    out[:, columns + LANES : columns + 2 * LANES] = c[...]
    out[:, columns + 2 * LANES :] = logs.T.astype(bf16)


def own_kernel(n_heads, x, dy, b, c, log_t, write_local, read_local, total, cum, cum_t):
    g = pl.program_id(0)
    heads = n_heads // RING
    rows = x.shape[0]
    half = rows // 2
    width = x.shape[1] // heads

    @pl.when(g == 0)
    def _():
        total[...] = jnp.zeros_like(total)
        cumulate_own(log_t, cum, cum_t)

    col, row = group_of(cum[...], g, heads, 1), group_of(cum_t[...], g, heads, 0)
    mid = col[half - 1 : half, :]
    for i in range(2):
        lo = i * half
        parts = []

        def add(h, decay):
            span = slice(h * width, (h + 1) * width)
            parts.append(decay * mm(x[lo : lo + half, span], dy[lo : lo + half, span], NT))

        diagonal(heads, half, lo, col, row, add)
        total[lo : lo + half, lo : lo + half] += sum(parts)
    early = (x[:half].astype(f32) * spread(jnp.exp(mid - col[:half]), width)).astype(bf16)
    late = (dy[half:].astype(f32) * spread(jnp.exp(col[half:] - mid), width)).astype(bf16)
    total[:half, half:] += mm(early, late, NT)

    @pl.when(g == pl.num_programs(0) - 1)
    def _():
        write_local[...] = mm_exact(total[...], c[...].astype(f32), NN)
        read_local[...] = mm_exact(total[...], b[...].astype(f32), TN)


def block_kernel(n_heads, top, bottom, *refs):
    tiles, (act, fronts, log_row, cum_out, cum_t) = refs[:6], refs[6:]
    b = jnp.concatenate([tiles[0][...], tiles[1][...]], axis=0)
    c = jnp.concatenate([tiles[2][...], tiles[3][...]], axis=0)
    g = pl.program_id(0)
    heads = n_heads // RING
    half = top.shape[0]
    rows = 2 * half
    width = top.shape[1] // heads

    @pl.when(g == 0)
    def _():
        cumulate(n_heads, tiles[4:], cum_out, cum_t)

    col, row = group_of(cum_out[...], g, heads, 1), group_of(cum_t[...], g, heads, 0)
    mid, last = col[half - 1 : half, :], col[rows - 1 : rows, :]
    log_row[...] = spread(last, width)
    scores = mm(b, c, NT)
    late_f = bottom[...].astype(f32) * spread(jnp.exp(col[half:] - mid), width)
    late = late_f.astype(bf16)
    first = (top[...].astype(f32) * spread(jnp.exp(col[:half]), width)).astype(bf16)
    second = (late_f * spread(jnp.exp(mid), width)).astype(bf16)
    fronts[0] = (mm(c[:half], first, TN) + mm(c[half:], second, TN)).astype(bf16)
    cross = mm(scores[:half, half:].astype(bf16), late, NN)
    to_mid = jnp.exp(mid - col[:half])
    for i, dy in enumerate((top, bottom)):
        lo = i * half
        score = scores[lo : lo + half, lo : lo + half]

        def put(h, decay):
            span = slice(h * width, (h + 1) * width)
            out = mm((decay * score).astype(bf16), dy[:, span], NN)
            if i == 0:
                out += cross[:, span] * to_mid[:, h : h + 1]
            act[lo : lo + half, span] = out.astype(act.dtype)

        diagonal(heads, half, lo, col, row, put)


def log_over(p, logs, wanted):
    total = jnp.zeros_like(logs[0])
    for k in range(RING):
        total += jnp.where(wanted(lax.bitwise_xor(p, k)), logs[k], 0.0)
    return total


def combine_kernel(at, *refs):
    parts, (state_out, grad_out) = refs[:RING], refs[RING:]
    n = state_out.shape[0] - EXTRA
    logs = [log_of(part) for part in parts]
    p = at[0]
    state, grad = 0.0, 0.0
    for j in range(RING):
        own = lax.bitwise_xor(p, j)
        state += parts[j][:n].astype(f32) * jnp.exp(log_over(p, logs, lambda k: k > own))
        grad += parts[j][n : 2 * n].astype(f32) * jnp.exp(log_over(p, logs, lambda k: k < own))
    for out, value in ((state_out, state), (grad_out, grad)):
        out[:n] = value.astype(bf16)
        write_log(out, sum(logs))


def write_log(out, log):
    n, width = out.shape
    row = iota((EXTRA, width), 0)
    rows = jnp.zeros((EXTRA, width), f32)
    for i, part in enumerate(three_parts(log)):
        rows = jnp.where(row == i, part, rows)
    out[n - EXTRA :] = rows.astype(bf16)


def log_of(message):
    n = message.shape[0] - EXTRA
    tail = message[n:].astype(f32)
    return tail[0:1] + tail[1:2] + tail[2:3]


def merge_kernel(*refs):
    for near, far, out in ((*refs[:2], refs[4]), (*refs[2:4], refs[5])):
        n = near.shape[0] - EXTRA
        log = log_of(near)
        out[:n] = (near[:n].astype(f32) + far[:n].astype(f32) * jnp.exp(log)).astype(bf16)
        write_log(out, log + log_of(far))


def ring_kernel(at, *refs):
    fronts, logs, outs = refs[:RING], [r[...] for r in refs[RING : 2 * RING]], refs[2 * RING :]
    p = at[0]
    for j in range(RING):
        own = lax.bitwise_xor(p, j)
        total = 0.0
        for i in range(RING):
            if i != j:
                there = lax.bitwise_xor(p, i)
                weight = jnp.exp(log_over(p, logs, lambda k: (k > own) & (k < there)))
                total += fronts[i][0].astype(f32) * jnp.where(there > own, weight, 0.0)
        outs[j][0] = total.astype(bf16)


def finish_kernel(n_heads, n_w, n_pieces, outer, share, at, *refs):
    locals_, refs = refs[:RING], refs[RING:]
    rings, refs = refs[:RING], refs[RING:]
    quarters, refs = refs[:RING], refs[RING:]
    logs, refs = [r[...] for r in refs[:RING]], refs[RING:]
    tops, refs = refs[:RING], refs[RING:]
    bottoms, refs = refs[:RING], refs[RING:]
    cums, refs = refs[:RING], refs[RING:]
    w, refs = refs[:n_pieces], refs[n_pieces:]
    x, acts, own, write, *tiles, total = refs
    g, p = pl.program_id(0), at[0]
    heads = n_heads // RING
    rows = own.shape[0]
    width = own.shape[1] // heads
    n = quarters[0].shape[0] - EXTRA
    source = lax.bitwise_xor(p, g)
    carried = quarters[0][:n].astype(f32)
    for j in range(1, RING):
        carried = jnp.where(source == j, quarters[j][:n].astype(f32), carried)

    @pl.when(g == 0)
    def _():
        write[...] = jnp.zeros_like(write)
        total[...] = jnp.zeros_like(total)

    for j in range(RING):
        col = group_of(cums[j][...], g, heads, 1)
        tail = spread(jnp.exp(col[rows - 1 : rows, :] - col), width)
        place = lax.bitwise_xor(p, j)
        weight = jnp.exp(log_over(p, logs, lambda k: k > place))
        grads = (carried * weight + rings[j][0].astype(f32)).astype(bf16)
        b = jnp.concatenate([tops[j][...], bottoms[j][...]], axis=0)
        out = mm(b, grads, NN) * tail + locals_[j][...].astype(f32)
        out = out.astype(acts.dtype)
        acts[j * rows : (j + 1) * rows, :] = out
        if j == 0:
            own[...] = out
            write[...] += mm((x[...].astype(f32) * tail).astype(bf16), grads, NT)
    n_rows, column = w[0].shape[0], 0
    for piece in w:
        total[:, column : column + piece.shape[0]] += mm(acts[...], piece[...], NT)
        column += piece.shape[0]

    @pl.when(g == pl.num_programs(0) - 1)
    def _():
        if len(tiles) == 1:
            for k in range(n_w):
                put_tile(tiles[0], lax.rem(at[1] + k, outer), total, k, n_rows)
        else:
            for tile in tiles:
                tile[...] = jnp.zeros_like(tile)
            for k in range(n_w):
                o = lax.rem(at[1] + k, outer)
                for tile, side in zip(tiles, (at[2], 1 - at[2])):

                    @pl.when(lax.div(o, share) == side)
                    def _():
                        put_tile(tile, lax.rem(o, share), total, k, n_rows)


def put_tile(tile, slot, total, k, n_rows):
    rows = total.shape[0] // RING
    for j in range(RING):
        part = total[j * rows : (j + 1) * rows, k * n_rows : (k + 1) * n_rows]
        tile[j, slot] = part.astype(tile.dtype)


def product_kernel(at, acts, w, out, total):
    g = pl.program_id(0)

    @pl.when(g == 0)
    def _():
        total[...] = jnp.zeros_like(total)

    total[...] += mm(acts[...], w[...], NT)

    @pl.when(g == pl.num_programs(0) - 1)
    def _():
        out[...] = total[...].astype(out.dtype)


def read_kernel(n_heads, at, *refs):
    tops, refs = refs[:RING], refs[RING:]
    bottoms, refs = refs[:RING], refs[RING:]
    cums, refs = refs[:RING], refs[RING:]
    parts, (carried, *outs) = refs[:RING], refs[RING:]
    logs = [log_of(part) for part in parts]
    p = at[0]
    heads = n_heads // RING
    half = tops[0].shape[0]
    n = carried.shape[0] - EXTRA
    width = carried.shape[1] // heads
    for j in range(RING):
        own = lax.bitwise_xor(p, j)
        total = carried[:n].astype(f32) * jnp.exp(log_over(p, logs, lambda k: k < own))
        for i in range(RING):
            if i != j:
                there = lax.bitwise_xor(p, i)
                weight = jnp.exp(log_over(p, logs, lambda k: (k < own) & (k > there)))
                total += parts[i][:n].astype(f32) * jnp.where(there < own, weight, 0.0)
        states = total.astype(bf16)
        decay = spread(jnp.exp(group_of(cums[j][...], p, heads, 1)), width)
        for i, dy in enumerate((tops[j], bottoms[j])):
            at_rows = slice(i * half, (i + 1) * half)
            scaled = (dy[...].astype(f32) * decay[at_rows]).astype(bf16)
            outs[j][at_rows] = mm(scaled, states, NT).astype(bf16)


def place_kernel(outer, share, at, *refs):
    blocks, late, out = refs[:RING], refs[RING:-1], refs[-1]
    p, z, side = at[0], at[1], at[2]
    width = out.shape[1] // (share * RING)
    last = lax.rem(z + outer - 1, outer)
    for slot in range(share):
        for j in range(RING):
            column = pl.multiple_of((slot * RING + lax.bitwise_xor(p, j)) * width, width)

            @pl.when(side * share + slot == last)
            def _():
                out[:, pl.ds(column, width)] = late[j][...]

            @pl.when(side * share + slot != last)
            def _():
                out[:, pl.ds(column, width)] = blocks[j][slot]


def call(kernel, name, grid, in_specs, out_specs, out_shape, scratch=(), after=(), flops=0):
    n_in, n_after = len(in_specs), len(after)

    def body(at, *refs):
        kernel(at, *refs[:n_in], *refs[n_in + n_after :])

    fn = pl.pallas_call(
        body,
        grid_spec=pltpu.PrefetchScalarGridSpec(
            num_scalar_prefetch=1,
            grid=grid,
            in_specs=list(in_specs) + [pl.BlockSpec(memory_space=pl.ANY)] * n_after,
            out_specs=out_specs,
            scratch_shapes=list(scratch),
        ),
        out_shape=out_shape,
        compiler_params=pltpu.CompilerParams(vmem_limit_bytes=56 * 2**20),
        cost_estimate=pl.CostEstimate(flops=flops, bytes_accessed=0, transcendentals=0),
        name=name,
    )
    return lambda *operands: fn(*operands, *after)


def local(x, dy, write_proj, read_proj, log_decay, w_in):
    rows, columns = x.shape
    half = rows // 2
    state_dim = write_proj.shape[1]
    n_heads = log_decay.shape[1]
    heads = n_heads // RING
    width = columns // n_heads
    part = heads * width
    w_rows = w_in.shape[0]
    n_seq, n_head = lax.axis_size("seq"), lax.axis_size("head")
    outer = n_seq // RING
    place = lax.axis_index("seq")
    side = lax.axis_index("head")
    p, z = place % RING, place // RING
    at = jnp.stack([p, z, side]).astype(jnp.int32)

    def swap(value, j):
        return lax.ppermute(value, "seq", [(s, s ^ j) for s in range(n_seq)])

    def along(value, d):
        return lax.ppermute(
            value, "seq", [(s, s + d * RING) for s in range(n_seq) if 0 <= s + d * RING < n_seq]
        )

    two = n_head == 2 and w_rows % LANES == 0 and outer == 4
    share = outer // n_head

    def turn(value):
        return lax.ppermute(value, "seq", [(s, (s - RING) % n_seq) for s in range(n_seq)])

    w_first = turn(w_in)

    def const(*shape):
        return pl.BlockSpec(shape, lambda g, q: (0,) * len(shape))

    by_group = pl.BlockSpec((rows, part), lambda g, q: (0, g))
    state_spec = pl.BlockSpec((1, state_dim, part), lambda g, q: (g, 0, 0))
    log_spec = pl.BlockSpec((1, part), lambda g, q: (0, g))
    cum_spec = const(rows, LANES)
    proj_spec = const(rows, state_dim)
    message_spec = const(state_dim + EXTRA, part)
    shape = jax.ShapeDtypeStruct
    state_shape = shape((RING, state_dim, part), bf16)
    log_shape = shape((1, columns), f32)
    cum_shape = shape((rows, LANES), f32)
    message_shape = shape((state_dim + EXTRA, part), bf16)
    cum_scratch, cum_t_scratch = pltpu.VMEM((rows, LANES), f32), pltpu.VMEM((LANES, rows), f32)

    log_in_spec = const(n_heads, rows)
    log_t = log_decay.T
    own_specs = [by_group, by_group, proj_spec, proj_spec, log_in_spec]
    part_spec = const(2 * state_dim + EXTRA, part)
    parts = call(
        functools.partial(edge_kernel, n_heads),
        "edges",
        (RING,),
        own_specs,
        [part_spec] * RING,
        [shape((2 * state_dim + EXTRA, part), bf16)] * RING,
        [cum_scratch],
    )(at, x, dy, write_proj, read_proj, log_t)

    write_local, read_local = call(
        functools.partial(lambda *refs: own_kernel(n_heads, *refs[1:])),
        "own_tokens",
        (RING,),
        own_specs,
        [proj_spec] * 2,
        [shape((rows, state_dim), f32)] * 2,
        [pltpu.VMEM((rows, rows), f32), cum_scratch, cum_t_scratch],
    )(at, x, dy, write_proj, read_proj, log_t)

    packed = call(
        functools.partial(lambda *refs: pack_kernel(n_heads, *refs[1:])),
        "pack",
        (1,),
        [const(rows, columns), proj_spec, proj_spec, log_in_spec],
        const(rows, columns + 3 * LANES),
        shape((rows, columns + 3 * LANES), bf16),
    )(at, dy, write_proj, read_proj, log_t)

    def halves(width, column):
        upper = pl.BlockSpec((half, width), lambda g, q: (0, column(g, q)))
        lower = pl.BlockSpec((half, width), lambda g, q: (1, column(g, q)))
        return [(upper, lower)] * (RING - 1) + [(upper, upper)]

    half_specs = halves(part, lambda g, q: g)
    mine_specs = halves(part, lambda g, q: q[0])
    tile_specs = [halves(LANES, lambda g, q, i=i: columns // LANES + i) for i in range(3)]

    def block(j, top, bottom, after=()):
        return call(
            functools.partial(lambda *refs: block_kernel(n_heads, *refs[1:])),
            "tokens",
            (RING,),
            [*half_specs[j]] + [spec for specs in tile_specs for spec in specs[j]],
            [by_group, state_spec, log_spec, cum_spec],
            [shape((rows, columns), bf16), state_shape, log_shape, cum_shape],
            [cum_t_scratch],
            after,
        )(at, top, bottom, *([top, bottom] * 3))

    parts = [parts[0]] + [swap(parts[j], j) for j in range(1, RING)]
    results = [block(0, packed, packed)]
    logs = [results[0][2]]
    packed, parts, logs, read_local, w_first = lax.optimization_barrier(
        (packed, parts, logs, read_local, w_first)
    )
    from_x, from_y = lax.optimization_barrier((swap(packed, 1), swap(packed, 2)))

    def combine():
        return call(
            combine_kernel,
            "messages",
            (1,),
            [part_spec] * RING,
            [message_spec] * 2,
            [message_shape] * 2,
        )(at, *parts)

    def merge(*pairs, after=()):
        return call(
            lambda q, *refs: merge_kernel(*refs),
            "merge",
            (1,),
            [message_spec] * 4,
            [message_spec] * 2,
            [message_shape] * 2,
            after=after,
        )(at, *pairs)

    state_span, grad_span = combine()
    d = 1
    while d < outer:
        state_got, grad_got = along(state_span, d), along(grad_span, -d)
        if 2 * d >= outer:
            w_pieces = [w_in, w_first]
            while len(w_pieces) < outer - 1:
                w_pieces.append(turn(w_pieces[-1]))
            blocks = [(packed, packed), (from_x, from_x), (from_y, from_y)]
            blocks.append((swap(from_x[:half], 2), swap(from_y[half:], 1)))
            results.append(block(1, *blocks[1]))
            results.append(block(2, *blocks[2], after=[w_pieces[-1]]))
            logs += [v[2] for v in results[1:]]
        if d == 1:
            state_part, grad_part = state_got, grad_got
        else:
            state_part, grad_part = merge(
                state_part, state_got, grad_part, grad_got, after=logs[1:]
            )
        if 2 * d < outer:
            state_span, grad_span = merge(state_span, state_got, grad_span, grad_got)
            if 4 * d >= outer:
                state_span, grad_span, w_first = lax.optimization_barrier(
                    (state_span, grad_span, w_first)
                )
        d *= 2
    grad_part, w_last = lax.optimization_barrier((grad_part, w_pieces[-1]))
    w_last = turn(w_last)
    if not two:
        w_pieces.append(w_last)
    grad_parts = [grad_part] + [swap(grad_part, j) for j in range(1, RING)]
    results.append(block(RING - 1, *blocks[-1]))
    logs.append(results[-1][2])
    local_acts, fronts, _, cums = zip(*results)

    ring_grads = call(
        ring_kernel,
        "ring_grads",
        (RING,),
        [state_spec] * RING + [log_spec] * RING,
        [state_spec] * RING,
        [state_shape] * RING,
    )(at, *fronts, *logs)

    n_w = outer - 1 if two else outer
    tall = pl.BlockSpec((RING * rows, part), lambda g, q: (0, g))
    tile_shapes = [(RING, outer, rows, w_rows)]
    if two:
        tile_shapes = [(RING, share, rows, w_rows)] * 2
    w_total = sum(v.shape[0] for v in w_pieces)
    acts, act_grad, write_carry, *tiles = call(
        functools.partial(finish_kernel, n_heads, n_w, len(w_pieces), outer, share),
        "finish",
        (RING,),
        [by_group] * RING
        + [state_spec] * RING
        + [message_spec] * RING
        + [log_spec] * RING
        + [spec[0] for spec in tile_specs[0]]
        + [spec[1] for spec in tile_specs[0]]
        + [cum_spec] * RING
        + [pl.BlockSpec((v.shape[0], part), lambda g, q: (0, g)) for v in w_pieces]
        + [by_group],
        [tall, by_group, proj_spec] + [const(*v) for v in tile_shapes],
        [
            shape((RING * rows, columns), bf16),
            shape((rows, columns), bf16),
            shape((rows, state_dim), f32),
        ]
        + [shape(v, bf16) for v in tile_shapes],
        [pltpu.VMEM((RING * rows, w_total), f32)],
    )(
        at,
        *local_acts,
        *ring_grads,
        *grad_parts,
        *logs,
        *[top for top, _ in blocks],
        *[bottom for _, bottom in blocks],
        *cums,
        *w_pieces,
        x,
    )

    def to_owners(tile):
        return [tile[0]] + [swap(tile[j], j) for j in range(1, RING)]

    read_parts = call(
        functools.partial(read_kernel, n_heads),
        "read_carry",
        (1,),
        [spec[0] for spec in mine_specs]
        + [spec[1] for spec in mine_specs]
        + [cum_spec] * RING + [part_spec] * RING + [message_spec],
        [proj_spec] * RING,
        [shape((rows, state_dim), bf16)] * RING,
        after=[write_carry],
    )(
        at,
        *[top for top, _ in blocks],
        *[bottom for _, bottom in blocks],
        *cums,
        *parts,
        state_part,
    )
    if two:
        mine, theirs = tiles
        got = lax.ppermute(theirs, "head", [(0, 1), (1, 0)])
        early = (mine.astype(f32) + got.astype(f32)).astype(bf16)
        late = call(
            product_kernel,
            "late_product",
            (RING,),
            [tall, pl.BlockSpec((w_rows, part), lambda g, q: (0, g))],
            const(RING * rows, w_rows),
            shape((RING * rows, w_rows), bf16),
            [pltpu.VMEM((RING * rows, w_rows), f32)],
            after=[early, read_parts[0]],
        )(at, acts, w_last)

        def owner(s):
            return (s // RING + outer - 1) % outer // share

        both_axes = ("seq", "head")
        got = lax.ppermute(
            late, both_axes, [(2 * s + 1 - owner(s), 2 * s + owner(s)) for s in range(n_seq)]
        )
        early_sent = to_owners(early)
        got, early_sent = lax.optimization_barrier((got, early_sent))
        late = (late.astype(f32) + got.astype(f32)).astype(bf16).reshape(RING, rows, w_rows)
        late = [late[0]] + [
            lax.ppermute(
                late[j],
                both_axes,
                [(2 * s + owner(s), 2 * (s ^ j) + owner(s)) for s in range(n_seq)],
            )
            for j in range(1, RING)
        ]
        input_grad = pl.pallas_call(
            functools.partial(place_kernel, outer, share),
            in_specs=[pl.BlockSpec(memory_space=pltpu.SMEM)]
            + [pl.BlockSpec(memory_space=pltpu.VMEM)] * (2 * RING),
            out_specs=pl.BlockSpec(memory_space=pltpu.VMEM),
            out_shape=shape((rows, share * RING * w_rows), bf16),
            compiler_params=pltpu.CompilerParams(vmem_limit_bytes=32 * 2**20),
            name="place",
        )(at, *early_sent, *late)
    else:
        summed = lax.psum_scatter(tiles[0], "head", scatter_dimension=1, tiled=True)
        pieces = jnp.take(jnp.stack(to_owners(summed)), p ^ jnp.arange(RING), axis=0)
        input_grad = pieces.transpose(2, 1, 0, 3).reshape(rows, share * RING * w_rows)
    read_got = [swap(read_parts[j], j) for j in range(1, RING)]
    read_carry = read_parts[0].astype(f32) + sum(v.astype(f32) for v in read_got)
    both = jnp.stack([write_local + write_carry, read_local + read_carry])
    if n_head == 2:
        both = both + lax.ppermute(both, "head", [(0, 1), (1, 0)])
    else:
        both = lax.psum(both, "head")
    return (input_grad, act_grad, both[0], both[1])


def solution(mesh):
    return jax.shard_map(
        local,
        mesh=mesh,
        in_specs=(
            P("seq", "head"),
            P("seq", "head"),
            P("seq", None),
            P("seq", None),
            P("seq", "head"),
            P("seq", "head"),
        ),
        out_specs=(P("seq", "head"), P("seq", "head"), P("seq", None), P("seq", None)),
        check_vma=False,
    )
```

```python
import functools

import jax
import jax.numpy as jnp
from jax import lax
from jax.experimental import pallas as pl
from jax.experimental.pallas import tpu as pltpu
from jax.sharding import PartitionSpec as P

RING = 4
LANES = 128
EXTRA = 16
NT = (((1,), (1,)), ((), ()))
TN = (((0,), (0,)), ((), ()))
NN = (((1,), (0,)), ((), ()))
bf16, f32 = jnp.bfloat16, jnp.float32


def mm(a, b, dims):
    return lax.dot_general(a, b, dims, preferred_element_type=f32)


def mm_exact(a, b, dims):
    return lax.dot_general(a, b, dims, precision=lax.Precision.HIGHEST, preferred_element_type=f32)


def spread(columns, width):
    rows = columns.shape[0]
    return jnp.concatenate(
        [jnp.broadcast_to(columns[:, h : h + 1], (rows, width)) for h in range(columns.shape[1])],
        axis=1,
    )


def iota(shape, axis):
    return lax.broadcasted_iota(jnp.int32, shape, axis)


def three_parts(value):
    first = value.astype(bf16).astype(f32)
    second = (value - first).astype(bf16).astype(f32)
    return first, second, value - first - second


def cumulate(n_heads, log_tiles, cum, cum_t):
    parts = jnp.concatenate([tile[...] for tile in log_tiles], axis=0)
    rows = parts.shape[0]
    source, head = iota((LANES, LANES), 0), iota((LANES, LANES), 1)
    pick = (source < 3 * n_heads) & (lax.rem(source, n_heads) == head)
    logs = mm(parts, pick.astype(f32).astype(bf16), NN)
    upto = (iota((rows, rows), 0) <= iota((rows, rows), 1)).astype(f32)
    cum[...] = mm_exact(upto, logs, TN)
    if cum_t is not None:
        cum_t[...] = mm_exact(logs, upto, TN)


def group_of(value, g, heads, axis):
    shift = lax.rem(LANES - g * heads, LANES)
    value = pltpu.roll(value, shift, axis)
    return value[:, :heads] if axis == 1 else value[:heads]


def diagonal(heads, half, lo, col, row, each):
    later = iota((half, half), 1) >= iota((half, half), 0)
    for h in range(heads):
        log = row[h : h + 1, lo : lo + half] - col[lo : lo + half, h : h + 1]
        each(h, jnp.exp(jnp.where(later, log, -jnp.inf)))


def cumulate_own(log_t, cum, cum_t):
    n_heads, rows = log_t.shape
    logs = jnp.concatenate([log_t[...], jnp.zeros((LANES - n_heads, rows), f32)], axis=0)
    upto = (iota((rows, rows), 0) <= iota((rows, rows), 1)).astype(f32)
    cum[...] = mm_exact(upto, logs, (((0,), (1,)), ((), ())))
    if cum_t is not None:
        cum_t[...] = mm_exact(logs, upto, NN)


def edge_kernel(n_heads, at, x, dy, b, c, log_t, *refs):
    messages, cum = refs[:RING], refs[RING]
    g = pl.program_id(0)
    heads = n_heads // RING
    rows = x.shape[0]
    width = x.shape[1] // heads
    n = b.shape[1]

    @pl.when(g == 0)
    def _():
        cumulate_own(log_t, cum, None)

    col = group_of(cum[...], g, heads, 1)
    last = col[rows - 1 : rows, :]
    tailed = (x[...].astype(f32) * spread(jnp.exp(last - col), width)).astype(bf16)
    decayed = (dy[...].astype(f32) * spread(jnp.exp(col), width)).astype(bf16)
    ends = mm(b[...], tailed, TN).astype(bf16)
    fronts = mm(c[...], decayed, TN).astype(bf16)
    log = spread(last, width)
    for j in range(RING):

        @pl.when(lax.bitwise_xor(at[0], g) == j)
        def _():
            messages[j][:n] = ends
            messages[j][n : 2 * n] = fronts
            write_log(messages[j], log)


def pack_kernel(n_heads, dy, b, c, log_t, out):
    rows, columns = dy.shape
    fill = jnp.zeros((LANES - 3 * n_heads, rows), f32)
    logs = jnp.concatenate([*three_parts(log_t[...]), fill], axis=0)
    out[:, :columns] = dy[...]
    out[:, columns : columns + LANES] = b[...]
    out[:, columns + LANES : columns + 2 * LANES] = c[...]
    out[:, columns + 2 * LANES :] = logs.T.astype(bf16)


def own_kernel(n_heads, x, dy, b, c, log_t, write_local, read_local, total, cum, cum_t):
    g = pl.program_id(0)
    heads = n_heads // RING
    rows = x.shape[0]
    half = rows // 2
    width = x.shape[1] // heads

    @pl.when(g == 0)
    def _():
        total[...] = jnp.zeros_like(total)
        cumulate_own(log_t, cum, cum_t)

    col, row = group_of(cum[...], g, heads, 1), group_of(cum_t[...], g, heads, 0)
    mid = col[half - 1 : half, :]
    for i in range(2):
        lo = i * half
        parts = []

        def add(h, decay):
            span = slice(h * width, (h + 1) * width)
            parts.append(decay * mm(x[lo : lo + half, span], dy[lo : lo + half, span], NT))

        diagonal(heads, half, lo, col, row, add)
        total[lo : lo + half, lo : lo + half] += sum(parts)
    early = (x[:half].astype(f32) * spread(jnp.exp(mid - col[:half]), width)).astype(bf16)
    late = (dy[half:].astype(f32) * spread(jnp.exp(col[half:] - mid), width)).astype(bf16)
    total[:half, half:] += mm(early, late, NT)

    @pl.when(g == pl.num_programs(0) - 1)
    def _():
        write_local[...] = mm_exact(total[...], c[...].astype(f32), NN)
        read_local[...] = mm_exact(total[...], b[...].astype(f32), TN)


def block_kernel(n_heads, top, bottom, *refs):
    tiles, (act, fronts, log_row, cum_out, cum_t) = refs[:6], refs[6:]
    b = jnp.concatenate([tiles[0][...], tiles[1][...]], axis=0)
    c = jnp.concatenate([tiles[2][...], tiles[3][...]], axis=0)
    g = pl.program_id(0)
    heads = n_heads // RING
    half = top.shape[0]
    rows = 2 * half
    width = top.shape[1] // heads

    @pl.when(g == 0)
    def _():
        cumulate(n_heads, tiles[4:], cum_out, cum_t)

    col, row = group_of(cum_out[...], g, heads, 1), group_of(cum_t[...], g, heads, 0)
    mid, last = col[half - 1 : half, :], col[rows - 1 : rows, :]
    log_row[...] = spread(last, width)
    scores = mm(b, c, NT)
    late_f = bottom[...].astype(f32) * spread(jnp.exp(col[half:] - mid), width)
    late = late_f.astype(bf16)
    first = (top[...].astype(f32) * spread(jnp.exp(col[:half]), width)).astype(bf16)
    second = (late_f * spread(jnp.exp(mid), width)).astype(bf16)
    fronts[0] = (mm(c[:half], first, TN) + mm(c[half:], second, TN)).astype(bf16)
    cross = mm(scores[:half, half:].astype(bf16), late, NN)
    to_mid = jnp.exp(mid - col[:half])
    for i, dy in enumerate((top, bottom)):
        lo = i * half
        score = scores[lo : lo + half, lo : lo + half]

        def put(h, decay):
            span = slice(h * width, (h + 1) * width)
            out = mm((decay * score).astype(bf16), dy[:, span], NN)
            if i == 0:
                out += cross[:, span] * to_mid[:, h : h + 1]
            act[lo : lo + half, span] = out.astype(act.dtype)

        diagonal(heads, half, lo, col, row, put)


def log_over(p, logs, wanted):
    total = jnp.zeros_like(logs[0])
    for k in range(RING):
        total += jnp.where(wanted(lax.bitwise_xor(p, k)), logs[k], 0.0)
    return total


def combine_kernel(at, *refs):
    parts, (state_out, grad_out) = refs[:RING], refs[RING:]
    n = state_out.shape[0] - EXTRA
    logs = [log_of(part) for part in parts]
    p = at[0]
    state, grad = 0.0, 0.0
    for j in range(RING):
        own = lax.bitwise_xor(p, j)
        state += parts[j][:n].astype(f32) * jnp.exp(log_over(p, logs, lambda k: k > own))
        grad += parts[j][n : 2 * n].astype(f32) * jnp.exp(log_over(p, logs, lambda k: k < own))
    for out, value in ((state_out, state), (grad_out, grad)):
        out[:n] = value.astype(bf16)
        write_log(out, sum(logs))


def write_log(out, log):
    n, width = out.shape
    row = iota((EXTRA, width), 0)
    rows = jnp.zeros((EXTRA, width), f32)
    for i, part in enumerate(three_parts(log)):
        rows = jnp.where(row == i, part, rows)
    out[n - EXTRA :] = rows.astype(bf16)


def log_of(message):
    n = message.shape[0] - EXTRA
    tail = message[n:].astype(f32)
    return tail[0:1] + tail[1:2] + tail[2:3]


def merge_kernel(*refs):
    for near, far, out in ((*refs[:2], refs[4]), (*refs[2:4], refs[5])):
        n = near.shape[0] - EXTRA
        log = log_of(near)
        out[:n] = (near[:n].astype(f32) + far[:n].astype(f32) * jnp.exp(log)).astype(bf16)
        write_log(out, log + log_of(far))


def ring_kernel(at, *refs):
    fronts, logs, outs = refs[:RING], [r[...] for r in refs[RING : 2 * RING]], refs[2 * RING :]
    p = at[0]
    for j in range(RING):
        own = lax.bitwise_xor(p, j)
        total = 0.0
        for i in range(RING):
            if i != j:
                there = lax.bitwise_xor(p, i)
                weight = jnp.exp(log_over(p, logs, lambda k: (k > own) & (k < there)))
                total += fronts[i][0].astype(f32) * jnp.where(there > own, weight, 0.0)
        outs[j][0] = total.astype(bf16)


def finish_kernel(n_heads, n_w, outer, share, at, *refs):
    locals_, refs = refs[:RING], refs[RING:]
    rings, refs = refs[:RING], refs[RING:]
    quarters, refs = refs[:RING], refs[RING:]
    logs, refs = [r[...] for r in refs[:RING]], refs[RING:]
    tops, refs = refs[:RING], refs[RING:]
    bottoms, refs = refs[:RING], refs[RING:]
    cums, refs = refs[:RING], refs[RING:]
    w, refs = refs[:n_w], refs[n_w:]
    x, acts, own, write, *tiles, total = refs
    g, p = pl.program_id(0), at[0]
    heads = n_heads // RING
    rows = own.shape[0]
    width = own.shape[1] // heads
    n = quarters[0].shape[0] - EXTRA
    source = lax.bitwise_xor(p, g)
    carried = quarters[0][:n].astype(f32)
    for j in range(1, RING):
        carried = jnp.where(source == j, quarters[j][:n].astype(f32), carried)

    @pl.when(g == 0)
    def _():
        write[...] = jnp.zeros_like(write)
        total[...] = jnp.zeros_like(total)

    for j in range(RING):
        col = group_of(cums[j][...], g, heads, 1)
        tail = spread(jnp.exp(col[rows - 1 : rows, :] - col), width)
        place = lax.bitwise_xor(p, j)
        weight = jnp.exp(log_over(p, logs, lambda k: k > place))
        grads = (carried * weight + rings[j][0].astype(f32)).astype(bf16)
        b = jnp.concatenate([tops[j][...], bottoms[j][...]], axis=0)
        out = mm(b, grads, NN) * tail + locals_[j][...].astype(f32)
        out = out.astype(acts.dtype)
        acts[j * rows : (j + 1) * rows, :] = out
        if j == 0:
            own[...] = out
            write[...] += mm((x[...].astype(f32) * tail).astype(bf16), grads, NT)
    for k in range(n_w):
        n_rows = w[k].shape[0]
        total[:, k * n_rows : (k + 1) * n_rows] += mm(acts[...], w[k][...], NT)

    @pl.when(g == pl.num_programs(0) - 1)
    def _():
        if len(tiles) == 1:
            for k in range(n_w):
                put_tile(tiles[0], lax.rem(at[1] + k, outer), total, k, n_rows)
        else:
            for tile in tiles:
                tile[...] = jnp.zeros_like(tile)
            for k in range(n_w):
                o = lax.rem(at[1] + k, outer)
                for tile, side in zip(tiles, (at[2], 1 - at[2])):

                    @pl.when(lax.div(o, share) == side)
                    def _():
                        put_tile(tile, lax.rem(o, share), total, k, n_rows)


def put_tile(tile, slot, total, k, n_rows):
    rows = total.shape[0] // RING
    for j in range(RING):
        part = total[j * rows : (j + 1) * rows, k * n_rows : (k + 1) * n_rows]
        tile[j, slot] = part.astype(tile.dtype)


def read_kernel(n_heads, at, *refs):
    tops, refs = refs[:RING], refs[RING:]
    bottoms, refs = refs[:RING], refs[RING:]
    cums, refs = refs[:RING], refs[RING:]
    parts, (carried, *outs) = refs[:RING], refs[RING:]
    logs = [log_of(part) for part in parts]
    p = at[0]
    heads = n_heads // RING
    half = tops[0].shape[0]
    n = carried.shape[0] - EXTRA
    width = carried.shape[1] // heads
    for j in range(RING):
        own = lax.bitwise_xor(p, j)
        total = carried[:n].astype(f32) * jnp.exp(log_over(p, logs, lambda k: k < own))
        for i in range(RING):
            if i != j:
                there = lax.bitwise_xor(p, i)
                weight = jnp.exp(log_over(p, logs, lambda k: (k < own) & (k > there)))
                total += parts[i][:n].astype(f32) * jnp.where(there < own, weight, 0.0)
        states = total.astype(bf16)
        decay = spread(jnp.exp(group_of(cums[j][...], p, heads, 1)), width)
        for i, dy in enumerate((tops[j], bottoms[j])):
            at_rows = slice(i * half, (i + 1) * half)
            scaled = (dy[...].astype(f32) * decay[at_rows]).astype(bf16)
            outs[j][at_rows] = mm(scaled, states, NT).astype(bf16)


def place_kernel(outer, share, at, *refs):
    blocks, late, out = refs[:RING], refs[RING:-1], refs[-1]
    p, z, side = at[0], at[1], at[2]
    width = out.shape[1] // (share * RING)
    last = lax.rem(z + outer - 1, outer)
    for slot in range(share):
        for j in range(RING):
            column = pl.multiple_of((slot * RING + lax.bitwise_xor(p, j)) * width, width)

            @pl.when(side * share + slot == last)
            def _():
                out[:, pl.ds(column, width)] = late[j][...]

            @pl.when(side * share + slot != last)
            def _():
                out[:, pl.ds(column, width)] = blocks[j][slot]


def call(kernel, name, grid, in_specs, out_specs, out_shape, scratch=(), after=()):
    n_in, n_after = len(in_specs), len(after)

    def body(at, *refs):
        kernel(at, *refs[:n_in], *refs[n_in + n_after :])

    fn = pl.pallas_call(
        body,
        grid_spec=pltpu.PrefetchScalarGridSpec(
            num_scalar_prefetch=1,
            grid=grid,
            in_specs=list(in_specs) + [pl.BlockSpec(memory_space=pl.ANY)] * n_after,
            out_specs=out_specs,
            scratch_shapes=list(scratch),
        ),
        out_shape=out_shape,
        compiler_params=pltpu.CompilerParams(vmem_limit_bytes=56 * 2**20),
        cost_estimate=pl.CostEstimate(flops=0, bytes_accessed=0, transcendentals=0),
        name=name,
    )
    return lambda *operands: fn(*operands, *after)


def local(x, dy, write_proj, read_proj, log_decay, w_in):
    rows, columns = x.shape
    half = rows // 2
    state_dim = write_proj.shape[1]
    n_heads = log_decay.shape[1]
    heads = n_heads // RING
    width = columns // n_heads
    part = heads * width
    w_rows = w_in.shape[0]
    n_seq, n_head = lax.axis_size("seq"), lax.axis_size("head")
    outer = n_seq // RING
    place = lax.axis_index("seq")
    side = lax.axis_index("head")
    p, z = place % RING, place // RING
    at = jnp.stack([p, z, side]).astype(jnp.int32)

    def swap(value, j):
        return lax.ppermute(value, "seq", [(s, s ^ j) for s in range(n_seq)])

    def along(value, d):
        return lax.ppermute(
            value, "seq", [(s, s + d * RING) for s in range(n_seq) if 0 <= s + d * RING < n_seq]
        )

    w_blocks = [w_in]

    def turn_w():
        turn = [(s, (s - RING) % n_seq) for s in range(n_seq)]
        w_blocks.append(lax.ppermute(w_blocks[-1], "seq", turn))

    turn_w()

    def const(*shape):
        return pl.BlockSpec(shape, lambda g, q: (0,) * len(shape))

    by_group = pl.BlockSpec((rows, part), lambda g, q: (0, g))
    state_spec = pl.BlockSpec((1, state_dim, part), lambda g, q: (g, 0, 0))
    log_spec = pl.BlockSpec((1, part), lambda g, q: (0, g))
    cum_spec = const(rows, LANES)
    proj_spec = const(rows, state_dim)
    message_spec = const(state_dim + EXTRA, part)
    shape = jax.ShapeDtypeStruct
    state_shape = shape((RING, state_dim, part), bf16)
    log_shape = shape((1, columns), f32)
    cum_shape = shape((rows, LANES), f32)
    message_shape = shape((state_dim + EXTRA, part), bf16)
    cum_scratch, cum_t_scratch = pltpu.VMEM((rows, LANES), f32), pltpu.VMEM((LANES, rows), f32)

    log_in_spec = const(n_heads, rows)
    log_t = log_decay.T
    own_specs = [by_group, by_group, proj_spec, proj_spec, log_in_spec]
    part_spec = const(2 * state_dim + EXTRA, part)
    parts = call(
        functools.partial(edge_kernel, n_heads),
        "edges",
        (RING,),
        own_specs,
        [part_spec] * RING,
        [shape((2 * state_dim + EXTRA, part), bf16)] * RING,
        [cum_scratch],
    )(at, x, dy, write_proj, read_proj, log_t)
    parts = [parts[0]] + [swap(parts[j], j) for j in range(1, RING)]

    write_local, read_local = call(
        functools.partial(lambda *refs: own_kernel(n_heads, *refs[1:])),
        "own_tokens",
        (RING,),
        own_specs,
        [proj_spec] * 2,
        [shape((rows, state_dim), f32)] * 2,
        [pltpu.VMEM((rows, rows), f32), cum_scratch, cum_t_scratch],
    )(at, x, dy, write_proj, read_proj, log_t)

    packed = call(
        functools.partial(lambda *refs: pack_kernel(n_heads, *refs[1:])),
        "pack",
        (1,),
        [const(rows, columns), proj_spec, proj_spec, log_in_spec],
        const(rows, columns + 3 * LANES),
        shape((rows, columns + 3 * LANES), bf16),
    )(at, dy, write_proj, read_proj, log_t)

    def halves(width, column):
        upper = pl.BlockSpec((half, width), lambda g, q: (0, column(g, q)))
        lower = pl.BlockSpec((half, width), lambda g, q: (1, column(g, q)))
        return [(upper, lower)] * (RING - 1) + [(upper, upper)]

    half_specs = halves(part, lambda g, q: g)
    mine_specs = halves(part, lambda g, q: q[0])
    tile_specs = [halves(LANES, lambda g, q, i=i: columns // LANES + i) for i in range(3)]

    def block(j, top, bottom):
        return call(
            functools.partial(lambda *refs: block_kernel(n_heads, *refs[1:])),
            "tokens",
            (RING,),
            [*half_specs[j]] + [spec for specs in tile_specs for spec in specs[j]],
            [by_group, state_spec, log_spec, cum_spec],
            [shape((rows, columns), bf16), state_shape, log_shape, cum_shape],
            [cum_t_scratch],
        )(at, top, bottom, *([top, bottom] * 3))

    results = [block(0, packed, packed)]
    logs = [results[0][2]]
    packed, parts, logs, read_local = lax.optimization_barrier((packed, parts, logs, read_local))
    from_x, from_y = lax.optimization_barrier((swap(packed, 1), swap(packed, 2)))

    def combine():
        return call(
            combine_kernel,
            "messages",
            (1,),
            [part_spec] * RING,
            [message_spec] * 2,
            [message_shape] * 2,
        )(at, *parts)

    def merge(*pairs):
        return call(
            lambda q, *refs: merge_kernel(*refs),
            "merge",
            (1,),
            [message_spec] * 4,
            [message_spec] * 2,
            [message_shape] * 2,
        )(at, *pairs)

    state_span, grad_span = combine()
    d = 1
    while d < outer:
        state_got, grad_got = along(state_span, d), along(grad_span, -d)
        if d == 1:
            state_part, grad_part = state_got, grad_got
        else:
            state_part, grad_part = merge(state_part, state_got, grad_part, grad_got)
        if 2 * d < outer:
            state_span, grad_span = merge(state_span, state_got, grad_span, grad_got)
        d *= 2
    state_got, grad_got, w_blocks[-1] = lax.optimization_barrier(
        (state_got, grad_got, w_blocks[-1])
    )
    turn_w()
    from_x, from_y, grad_part = lax.optimization_barrier((from_x, from_y, grad_part))
    blocks = [(packed, packed), (from_x, from_x), (from_y, from_y)]
    blocks.append((swap(from_x[:half], 2), swap(from_y[half:], 1)))
    results += [block(j, *blocks[j]) for j in range(1, RING - 1)]
    logs += [v[2] for v in results[1:]]
    logs, blocks[-1] = lax.optimization_barrier((logs, blocks[-1]))
    results.append(block(RING - 1, *blocks[-1]))
    logs.append(results[-1][2])
    logs, grad_part = lax.optimization_barrier((logs, grad_part))
    grad_parts = [grad_part] + [swap(grad_part, j) for j in range(1, RING)]
    local_acts, fronts, _, cums = zip(*results)
    fronts = list(fronts)
    if outer > 2:
        fronts[-1], w_blocks[-1] = lax.optimization_barrier((fronts[-1], w_blocks[-1]))
    while len(w_blocks) < outer:
        turn_w()

    ring_grads = call(
        ring_kernel,
        "ring_grads",
        (RING,),
        [state_spec] * RING + [log_spec] * RING,
        [state_spec] * RING,
        [state_shape] * RING,
    )(at, *fronts, *logs)

    read_parts = call(
        functools.partial(read_kernel, n_heads),
        "read_carry",
        (1,),
        [spec[0] for spec in mine_specs]
        + [spec[1] for spec in mine_specs]
        + [cum_spec] * RING + [part_spec] * RING + [message_spec],
        [proj_spec] * RING,
        [shape((rows, state_dim), bf16)] * RING,
        after=ring_grads[:1],
    )(
        at,
        *[top for top, _ in blocks],
        *[bottom for _, bottom in blocks],
        *cums,
        *parts,
        state_part,
    )
    two = n_head == 2 and w_rows % LANES == 0
    share = outer // n_head
    n_w = outer - 1 if two else outer
    tall = pl.BlockSpec((RING * rows, part), lambda g, q: (0, g))
    w_spec = pl.BlockSpec((w_rows, part), lambda g, q: (0, g))
    tile_shapes = [(RING, share, rows, w_rows)] * 2 if two else [(RING, outer, rows, w_rows)]
    acts, act_grad, write_carry, *tiles = call(
        functools.partial(finish_kernel, n_heads, n_w, outer, share),
        "finish",
        (RING,),
        [by_group] * RING
        + [state_spec] * RING
        + [message_spec] * RING
        + [log_spec] * RING
        + [spec[0] for spec in tile_specs[0]]
        + [spec[1] for spec in tile_specs[0]]
        + [cum_spec] * RING
        + [w_spec] * n_w
        + [by_group],
        [tall, by_group, proj_spec] + [const(*v) for v in tile_shapes],
        [
            shape((RING * rows, columns), bf16),
            shape((rows, columns), bf16),
            shape((rows, state_dim), f32),
        ]
        + [shape(v, bf16) for v in tile_shapes],
        [pltpu.VMEM((RING * rows, n_w * w_rows), f32)],
        after=[read_parts[0]],
    )(
        at,
        *local_acts,
        *ring_grads,
        *grad_parts,
        *logs,
        *[top for top, _ in blocks],
        *[bottom for _, bottom in blocks],
        *cums,
        *w_blocks[:n_w],
        x,
    )

    def to_owners(tile):
        return [tile[0]] + [swap(tile[j], j) for j in range(1, RING)]

    if two:
        mine, theirs = tiles
        got = lax.ppermute(theirs, "head", [(0, 1), (1, 0)])
        tile = mm(acts, w_blocks[-1], NT).astype(bf16)
        got, tile = lax.optimization_barrier((got, tile))
        early = (mine.astype(f32) + got.astype(f32)).astype(bf16)
        early, read_parts = lax.optimization_barrier((early, read_parts))

        def owner(s):
            return (s // RING + outer - 1) % outer // share

        both_axes = ("seq", "head")
        got = lax.ppermute(
            tile, both_axes, [(2 * s + 1 - owner(s), 2 * s + owner(s)) for s in range(n_seq)]
        )
        read_got = [swap(read_parts[j], j) for j in range(1, RING)]
        got, read_got = lax.optimization_barrier((got, read_got))
        tile = (tile.astype(f32) + got.astype(f32)).astype(bf16).reshape(RING, rows, w_rows)
        late = [tile[0]] + [
            lax.ppermute(
                tile[j],
                both_axes,
                [(2 * s + owner(s), 2 * (s ^ j) + owner(s)) for s in range(n_seq)],
            )
            for j in range(1, RING)
        ]
        early = to_owners(early)
        input_grad = pl.pallas_call(
            functools.partial(place_kernel, outer, share),
            in_specs=[pl.BlockSpec(memory_space=pltpu.SMEM)]
            + [pl.BlockSpec(memory_space=pltpu.VMEM)] * (2 * RING),
            out_specs=pl.BlockSpec(memory_space=pltpu.VMEM),
            out_shape=shape((rows, share * RING * w_rows), bf16),
            compiler_params=pltpu.CompilerParams(vmem_limit_bytes=32 * 2**20),
            name="place",
        )(at, *early, *late)
    else:
        summed = lax.psum_scatter(tiles[0], "head", scatter_dimension=1, tiled=True)
        pieces = jnp.take(jnp.stack(to_owners(summed)), p ^ jnp.arange(RING), axis=0)
        input_grad = pieces.transpose(2, 1, 0, 3).reshape(rows, share * RING * w_rows)
    if not two:
        read_got = [swap(read_parts[j], j) for j in range(1, RING)]
    read_carry = read_parts[0].astype(f32) + sum(v.astype(f32) for v in read_got)
    both = jnp.stack([write_local + write_carry, read_local + read_carry])
    if n_head == 2:
        both = both + lax.ppermute(both, "head", [(0, 1), (1, 0)])
    else:
        both = lax.psum(both, "head")
    return (input_grad, act_grad, both[0], both[1])


def solution(mesh):
    return jax.shard_map(
        local,
        mesh=mesh,
        in_specs=(
            P("seq", "head"),
            P("seq", "head"),
            P("seq", None),
            P("seq", None),
            P("seq", "head"),
            P("seq", "head"),
        ),
        out_specs=(P("seq", "head"), P("seq", "head"), P("seq", None), P("seq", None)),
        check_vma=False,
    )
```

```python
import functools

import jax
import jax.numpy as jnp
from jax import lax
from jax.experimental import pallas as pl
from jax.experimental.pallas import tpu as pltpu
from jax.sharding import PartitionSpec as P

RING = 4
LANES = 128
EXTRA = 16
NT = (((1,), (1,)), ((), ()))
TN = (((0,), (0,)), ((), ()))
NN = (((1,), (0,)), ((), ()))
bf16, f32 = jnp.bfloat16, jnp.float32


def mm(a, b, dims):
    return lax.dot_general(a, b, dims, preferred_element_type=f32)


def mm_exact(a, b, dims):
    return lax.dot_general(a, b, dims, precision=lax.Precision.HIGHEST, preferred_element_type=f32)


def spread(columns, width):
    rows = columns.shape[0]
    return jnp.concatenate(
        [jnp.broadcast_to(columns[:, h : h + 1], (rows, width)) for h in range(columns.shape[1])],
        axis=1,
    )


def iota(shape, axis):
    return lax.broadcasted_iota(jnp.int32, shape, axis)


def three_parts(value):
    first = value.astype(bf16).astype(f32)
    second = (value - first).astype(bf16).astype(f32)
    return first, second, value - first - second


def cumulate(n_heads, log_tiles, cum, cum_t):
    parts = jnp.concatenate([tile[...] for tile in log_tiles], axis=0)
    rows = parts.shape[0]
    source, head = iota((LANES, LANES), 0), iota((LANES, LANES), 1)
    pick = (source < 3 * n_heads) & (lax.rem(source, n_heads) == head)
    logs = mm(parts, pick.astype(f32).astype(bf16), NN)
    upto = (iota((rows, rows), 0) <= iota((rows, rows), 1)).astype(f32)
    cum[...] = mm_exact(upto, logs, TN)
    if cum_t is not None:
        cum_t[...] = mm_exact(logs, upto, TN)


def group_of(value, g, heads, axis):
    shift = lax.rem(LANES - g * heads, LANES)
    value = pltpu.roll(value, shift, axis)
    return value[:, :heads] if axis == 1 else value[:heads]


def diagonal(heads, half, lo, col, row, each):
    later = iota((half, half), 1) >= iota((half, half), 0)
    for h in range(heads):
        log = row[h : h + 1, lo : lo + half] - col[lo : lo + half, h : h + 1]
        each(h, jnp.exp(jnp.where(later, log, -jnp.inf)))


def cumulate_own(log_t, cum, cum_t):
    n_heads, rows = log_t.shape
    logs = jnp.concatenate([log_t[...], jnp.zeros((LANES - n_heads, rows), f32)], axis=0)
    upto = (iota((rows, rows), 0) <= iota((rows, rows), 1)).astype(f32)
    cum[...] = mm_exact(upto, logs, (((0,), (1,)), ((), ())))
    if cum_t is not None:
        cum_t[...] = mm_exact(logs, upto, NN)


def edge_kernel(n_heads, at, x, dy, b, c, log_t, *refs):
    messages, cum = refs[:RING], refs[RING]
    g = pl.program_id(0)
    heads = n_heads // RING
    rows = x.shape[0]
    width = x.shape[1] // heads
    n = b.shape[1]

    @pl.when(g == 0)
    def _():
        cumulate_own(log_t, cum, None)

    col = group_of(cum[...], g, heads, 1)
    last = col[rows - 1 : rows, :]
    tailed = (x[...].astype(f32) * spread(jnp.exp(last - col), width)).astype(bf16)
    decayed = (dy[...].astype(f32) * spread(jnp.exp(col), width)).astype(bf16)
    ends = mm(b[...], tailed, TN).astype(bf16)
    fronts = mm(c[...], decayed, TN).astype(bf16)
    log = spread(last, width)
    for j in range(RING):

        @pl.when(lax.bitwise_xor(at[0], g) == j)
        def _():
            messages[j][:n] = ends
            messages[j][n : 2 * n] = fronts
            write_log(messages[j], log)


def pack_kernel(n_heads, dy, b, c, log_t, out):
    rows, columns = dy.shape
    fill = jnp.zeros((LANES - 3 * n_heads, rows), f32)
    logs = jnp.concatenate([*three_parts(log_t[...]), fill], axis=0)
    out[:, :columns] = dy[...]
    out[:, columns : columns + LANES] = b[...]
    out[:, columns + LANES : columns + 2 * LANES] = c[...]
    out[:, columns + 2 * LANES :] = logs.T.astype(bf16)


def own_kernel(n_heads, x, dy, b, c, log_t, write_local, read_local, total, cum, cum_t):
    g = pl.program_id(0)
    heads = n_heads // RING
    rows = x.shape[0]
    half = rows // 2
    width = x.shape[1] // heads

    @pl.when(g == 0)
    def _():
        total[...] = jnp.zeros_like(total)
        cumulate_own(log_t, cum, cum_t)

    col, row = group_of(cum[...], g, heads, 1), group_of(cum_t[...], g, heads, 0)
    mid = col[half - 1 : half, :]
    for i in range(2):
        lo = i * half
        parts = []

        def add(h, decay):
            span = slice(h * width, (h + 1) * width)
            parts.append(decay * mm(x[lo : lo + half, span], dy[lo : lo + half, span], NT))

        diagonal(heads, half, lo, col, row, add)
        total[lo : lo + half, lo : lo + half] += sum(parts)
    early = (x[:half].astype(f32) * spread(jnp.exp(mid - col[:half]), width)).astype(bf16)
    late = (dy[half:].astype(f32) * spread(jnp.exp(col[half:] - mid), width)).astype(bf16)
    total[:half, half:] += mm(early, late, NT)

    @pl.when(g == pl.num_programs(0) - 1)
    def _():
        write_local[...] = mm_exact(total[...], c[...].astype(f32), NN)
        read_local[...] = mm_exact(total[...], b[...].astype(f32), TN)


def block_kernel(n_heads, top, bottom, *refs):
    tiles, (act, fronts, log_row, cum_out, cum_t) = refs[:6], refs[6:]
    b = jnp.concatenate([tiles[0][...], tiles[1][...]], axis=0)
    c = jnp.concatenate([tiles[2][...], tiles[3][...]], axis=0)
    g = pl.program_id(0)
    heads = n_heads // RING
    half = top.shape[0]
    rows = 2 * half
    width = top.shape[1] // heads

    @pl.when(g == 0)
    def _():
        cumulate(n_heads, tiles[4:], cum_out, cum_t)

    col, row = group_of(cum_out[...], g, heads, 1), group_of(cum_t[...], g, heads, 0)
    mid, last = col[half - 1 : half, :], col[rows - 1 : rows, :]
    log_row[...] = spread(last, width)
    scores = mm(b, c, NT)
    late_f = bottom[...].astype(f32) * spread(jnp.exp(col[half:] - mid), width)
    late = late_f.astype(bf16)
    first = (top[...].astype(f32) * spread(jnp.exp(col[:half]), width)).astype(bf16)
    second = (late_f * spread(jnp.exp(mid), width)).astype(bf16)
    fronts[0] = (mm(c[:half], first, TN) + mm(c[half:], second, TN)).astype(bf16)
    cross = mm(scores[:half, half:].astype(bf16), late, NN)
    to_mid = jnp.exp(mid - col[:half])
    for i, dy in enumerate((top, bottom)):
        lo = i * half
        score = scores[lo : lo + half, lo : lo + half]

        def put(h, decay):
            span = slice(h * width, (h + 1) * width)
            out = mm((decay * score).astype(bf16), dy[:, span], NN)
            if i == 0:
                out += cross[:, span] * to_mid[:, h : h + 1]
            act[lo : lo + half, span] = out.astype(act.dtype)

        diagonal(heads, half, lo, col, row, put)


def log_over(p, logs, wanted):
    total = jnp.zeros_like(logs[0])
    for k in range(RING):
        total += jnp.where(wanted(lax.bitwise_xor(p, k)), logs[k], 0.0)
    return total


def combine_kernel(at, *refs):
    parts, (state_out, grad_out) = refs[:RING], refs[RING:]
    n = state_out.shape[0] - EXTRA
    logs = [log_of(part) for part in parts]
    p = at[0]
    state, grad = 0.0, 0.0
    for j in range(RING):
        own = lax.bitwise_xor(p, j)
        state += parts[j][:n].astype(f32) * jnp.exp(log_over(p, logs, lambda k: k > own))
        grad += parts[j][n : 2 * n].astype(f32) * jnp.exp(log_over(p, logs, lambda k: k < own))
    for out, value in ((state_out, state), (grad_out, grad)):
        out[:n] = value.astype(bf16)
        write_log(out, sum(logs))


def write_log(out, log):
    n, width = out.shape
    row = iota((EXTRA, width), 0)
    rows = jnp.zeros((EXTRA, width), f32)
    for i, part in enumerate(three_parts(log)):
        rows = jnp.where(row == i, part, rows)
    out[n - EXTRA :] = rows.astype(bf16)


def log_of(message):
    n = message.shape[0] - EXTRA
    tail = message[n:].astype(f32)
    return tail[0:1] + tail[1:2] + tail[2:3]


def merge_kernel(*refs):
    for near, far, out in ((*refs[:2], refs[4]), (*refs[2:4], refs[5])):
        n = near.shape[0] - EXTRA
        log = log_of(near)
        out[:n] = (near[:n].astype(f32) + far[:n].astype(f32) * jnp.exp(log)).astype(bf16)
        write_log(out, log + log_of(far))


def finish_kernel(n_heads, n_w, outer, share, at, *refs):
    locals_, refs = refs[:RING], refs[RING:]
    fronts, refs = refs[:RING], refs[RING:]
    quarters, refs = refs[:RING], refs[RING:]
    logs, refs = [r[...] for r in refs[:RING]], refs[RING:]
    tops, refs = refs[:RING], refs[RING:]
    bottoms, refs = refs[:RING], refs[RING:]
    cums, refs = refs[:RING], refs[RING:]
    w, refs = refs[:n_w], refs[n_w:]
    x, acts, own, write, *tiles, total = refs
    g, p = pl.program_id(0), at[0]
    heads = n_heads // RING
    rows = own.shape[0]
    width = own.shape[1] // heads
    n = quarters[0].shape[0] - EXTRA
    source = lax.bitwise_xor(p, g)
    carried = quarters[0][:n].astype(f32)
    for j in range(1, RING):
        carried = jnp.where(source == j, quarters[j][:n].astype(f32), carried)

    @pl.when(g == 0)
    def _():
        write[...] = jnp.zeros_like(write)
        total[...] = jnp.zeros_like(total)

    added = [front[0].astype(f32) for front in fronts]
    for j in range(RING):
        col = group_of(cums[j][...], g, heads, 1)
        tail = spread(jnp.exp(col[rows - 1 : rows, :] - col), width)
        place = lax.bitwise_xor(p, j)
        grads = carried * jnp.exp(log_over(p, logs, lambda k: k > place))
        for i in range(RING):
            if i != j:
                there = lax.bitwise_xor(p, i)
                weight = jnp.exp(log_over(p, logs, lambda k: (k > place) & (k < there)))
                grads += added[i] * jnp.where(there > place, weight, 0.0)
        grads = grads.astype(bf16)
        b = jnp.concatenate([tops[j][...], bottoms[j][...]], axis=0)
        out = mm(b, grads, NN) * tail + locals_[j][...].astype(f32)
        out = out.astype(acts.dtype)
        acts[j * rows : (j + 1) * rows, :] = out
        if j == 0:
            own[...] = out
            write[...] += mm((x[...].astype(f32) * tail).astype(bf16), grads, NT)
    for k in range(n_w):
        n_rows = w[k].shape[0]
        total[:, k * n_rows : (k + 1) * n_rows] += mm(acts[...], w[k][...], NT)

    @pl.when(g == pl.num_programs(0) - 1)
    def _():
        if len(tiles) == 1:
            for k in range(n_w):
                put_tile(tiles[0], lax.rem(at[1] + k, outer), total, k, n_rows)
        else:
            for tile in tiles:
                tile[...] = jnp.zeros_like(tile)
            for k in range(n_w):
                o = lax.rem(at[1] + k, outer)
                for tile, side in zip(tiles, (at[2], 1 - at[2])):

                    @pl.when(lax.div(o, share) == side)
                    def _():
                        put_tile(tile, lax.rem(o, share), total, k, n_rows)


def put_tile(tile, slot, total, k, n_rows):
    rows = total.shape[0] // RING
    for j in range(RING):
        part = total[j * rows : (j + 1) * rows, k * n_rows : (k + 1) * n_rows]
        tile[j, slot] = part.astype(tile.dtype)


def read_kernel(n_heads, at, *refs):
    tops, refs = refs[:RING], refs[RING:]
    bottoms, refs = refs[:RING], refs[RING:]
    cums, refs = refs[:RING], refs[RING:]
    parts, (carried, *outs) = refs[:RING], refs[RING:]
    logs = [log_of(part) for part in parts]
    p = at[0]
    heads = n_heads // RING
    half = tops[0].shape[0]
    n = carried.shape[0] - EXTRA
    width = carried.shape[1] // heads
    for j in range(RING):
        own = lax.bitwise_xor(p, j)
        total = carried[:n].astype(f32) * jnp.exp(log_over(p, logs, lambda k: k < own))
        for i in range(RING):
            if i != j:
                there = lax.bitwise_xor(p, i)
                weight = jnp.exp(log_over(p, logs, lambda k: (k < own) & (k > there)))
                total += parts[i][:n].astype(f32) * jnp.where(there < own, weight, 0.0)
        states = total.astype(bf16)
        decay = spread(jnp.exp(group_of(cums[j][...], p, heads, 1)), width)
        for i, dy in enumerate((tops[j], bottoms[j])):
            at_rows = slice(i * half, (i + 1) * half)
            scaled = (dy[...].astype(f32) * decay[at_rows]).astype(bf16)
            outs[j][at_rows] = mm(scaled, states, NT).astype(bf16)


def place_kernel(outer, share, at, *refs):
    blocks, late, out = refs[:RING], refs[RING:-1], refs[-1]
    p, z, side = at[0], at[1], at[2]
    width = out.shape[1] // (share * RING)
    last = lax.rem(z + outer - 1, outer)
    for slot in range(share):
        for j in range(RING):
            column = pl.multiple_of((slot * RING + lax.bitwise_xor(p, j)) * width, width)

            @pl.when(side * share + slot == last)
            def _():
                out[:, pl.ds(column, width)] = late[j][...]

            @pl.when(side * share + slot != last)
            def _():
                out[:, pl.ds(column, width)] = blocks[j][slot]


def call(kernel, name, grid, in_specs, out_specs, out_shape, scratch=(), after=()):
    n_in, n_after = len(in_specs), len(after)

    def body(at, *refs):
        kernel(at, *refs[:n_in], *refs[n_in + n_after :])

    fn = pl.pallas_call(
        body,
        grid_spec=pltpu.PrefetchScalarGridSpec(
            num_scalar_prefetch=1,
            grid=grid,
            in_specs=list(in_specs) + [pl.BlockSpec(memory_space=pl.ANY)] * n_after,
            out_specs=out_specs,
            scratch_shapes=list(scratch),
        ),
        out_shape=out_shape,
        compiler_params=pltpu.CompilerParams(vmem_limit_bytes=56 * 2**20),
        cost_estimate=pl.CostEstimate(flops=0, bytes_accessed=0, transcendentals=0),
        name=name,
    )
    return lambda *operands: fn(*operands, *after)


def local(x, dy, write_proj, read_proj, log_decay, w_in):
    rows, columns = x.shape
    half = rows // 2
    state_dim = write_proj.shape[1]
    n_heads = log_decay.shape[1]
    heads = n_heads // RING
    width = columns // n_heads
    part = heads * width
    w_rows = w_in.shape[0]
    n_seq, n_head = lax.axis_size("seq"), lax.axis_size("head")
    outer = n_seq // RING
    place = lax.axis_index("seq")
    side = lax.axis_index("head")
    p, z = place % RING, place // RING
    at = jnp.stack([p, z, side]).astype(jnp.int32)

    def swap(value, j):
        return lax.ppermute(value, "seq", [(s, s ^ j) for s in range(n_seq)])

    def along(value, d):
        return lax.ppermute(
            value, "seq", [(s, s + d * RING) for s in range(n_seq) if 0 <= s + d * RING < n_seq]
        )

    w_blocks = [w_in]

    def turn_w():
        turn = [(s, (s - RING) % n_seq) for s in range(n_seq)]
        w_blocks.append(lax.ppermute(w_blocks[-1], "seq", turn))

    turn_w()

    def const(*shape):
        return pl.BlockSpec(shape, lambda g, q: (0,) * len(shape))

    by_group = pl.BlockSpec((rows, part), lambda g, q: (0, g))
    state_spec = pl.BlockSpec((1, state_dim, part), lambda g, q: (g, 0, 0))
    log_spec = pl.BlockSpec((1, part), lambda g, q: (0, g))
    cum_spec = const(rows, LANES)
    proj_spec = const(rows, state_dim)
    message_spec = const(state_dim + EXTRA, part)
    shape = jax.ShapeDtypeStruct
    state_shape = shape((RING, state_dim, part), bf16)
    log_shape = shape((1, columns), f32)
    cum_shape = shape((rows, LANES), f32)
    message_shape = shape((state_dim + EXTRA, part), bf16)
    cum_scratch, cum_t_scratch = pltpu.VMEM((rows, LANES), f32), pltpu.VMEM((LANES, rows), f32)

    log_in_spec = const(n_heads, rows)
    log_t = log_decay.T
    own_specs = [by_group, by_group, proj_spec, proj_spec, log_in_spec]
    part_spec = const(2 * state_dim + EXTRA, part)
    parts = call(
        functools.partial(edge_kernel, n_heads),
        "edges",
        (RING,),
        own_specs,
        [part_spec] * RING,
        [shape((2 * state_dim + EXTRA, part), bf16)] * RING,
        [cum_scratch],
    )(at, x, dy, write_proj, read_proj, log_t)
    parts = [parts[0]] + [swap(parts[j], j) for j in range(1, RING)]

    write_local, read_local = call(
        functools.partial(lambda *refs: own_kernel(n_heads, *refs[1:])),
        "own_tokens",
        (RING,),
        own_specs,
        [proj_spec] * 2,
        [shape((rows, state_dim), f32)] * 2,
        [pltpu.VMEM((rows, rows), f32), cum_scratch, cum_t_scratch],
    )(at, x, dy, write_proj, read_proj, log_t)

    packed = call(
        functools.partial(lambda *refs: pack_kernel(n_heads, *refs[1:])),
        "pack",
        (1,),
        [const(rows, columns), proj_spec, proj_spec, log_in_spec],
        const(rows, columns + 3 * LANES),
        shape((rows, columns + 3 * LANES), bf16),
    )(at, dy, write_proj, read_proj, log_t)

    def halves(width, column):
        upper = pl.BlockSpec((half, width), lambda g, q: (0, column(g, q)))
        lower = pl.BlockSpec((half, width), lambda g, q: (1, column(g, q)))
        return [(upper, lower)] * (RING - 1) + [(upper, upper)]

    half_specs = halves(part, lambda g, q: g)
    mine_specs = halves(part, lambda g, q: q[0])
    tile_specs = [halves(LANES, lambda g, q, i=i: columns // LANES + i) for i in range(3)]

    def block(j, top, bottom):
        return call(
            functools.partial(lambda *refs: block_kernel(n_heads, *refs[1:])),
            "tokens",
            (RING,),
            [*half_specs[j]] + [spec for specs in tile_specs for spec in specs[j]],
            [by_group, state_spec, log_spec, cum_spec],
            [shape((rows, columns), bf16), state_shape, log_shape, cum_shape],
            [cum_t_scratch],
        )(at, top, bottom, *([top, bottom] * 3))

    results = [block(0, packed, packed)]
    logs = [results[0][2]]
    packed, parts, logs, read_local = lax.optimization_barrier((packed, parts, logs, read_local))
    from_x, from_y = lax.optimization_barrier((swap(packed, 1), swap(packed, 2)))

    def combine():
        return call(
            combine_kernel,
            "messages",
            (1,),
            [part_spec] * RING,
            [message_spec] * 2,
            [message_shape] * 2,
        )(at, *parts)

    def merge(*pairs):
        return call(
            lambda q, *refs: merge_kernel(*refs),
            "merge",
            (1,),
            [message_spec] * 4,
            [message_spec] * 2,
            [message_shape] * 2,
        )(at, *pairs)

    state_span, grad_span = combine()
    d = 1
    while d < outer:
        state_got, grad_got = along(state_span, d), along(grad_span, -d)
        if d == 1:
            state_part, grad_part = state_got, grad_got
        else:
            state_part, grad_part = merge(state_part, state_got, grad_part, grad_got)
        if 2 * d < outer:
            state_span, grad_span = merge(state_span, state_got, grad_span, grad_got)
        d *= 2
    state_got, grad_got, w_blocks[-1] = lax.optimization_barrier(
        (state_got, grad_got, w_blocks[-1])
    )
    turn_w()
    from_x, from_y, grad_part = lax.optimization_barrier((from_x, from_y, grad_part))
    blocks = [(packed, packed), (from_x, from_x), (from_y, from_y)]
    blocks.append((swap(from_x[:half], 2), swap(from_y[half:], 1)))
    results += [block(j, *blocks[j]) for j in range(1, RING - 1)]
    logs += [v[2] for v in results[1:]]
    logs, blocks[-1] = lax.optimization_barrier((logs, blocks[-1]))
    results.append(block(RING - 1, *blocks[-1]))
    logs.append(results[-1][2])
    logs, grad_part = lax.optimization_barrier((logs, grad_part))
    grad_parts = [grad_part] + [swap(grad_part, j) for j in range(1, RING)]
    local_acts, fronts, _, cums = zip(*results)
    fronts = list(fronts)
    if outer > 2:
        fronts[-1], w_blocks[-1] = lax.optimization_barrier((fronts[-1], w_blocks[-1]))
    while len(w_blocks) < outer:
        turn_w()

    read_parts = call(
        functools.partial(read_kernel, n_heads),
        "read_carry",
        (1,),
        [spec[0] for spec in mine_specs]
        + [spec[1] for spec in mine_specs]
        + [cum_spec] * RING + [part_spec] * RING + [message_spec],
        [proj_spec] * RING,
        [shape((rows, state_dim), bf16)] * RING,
    )(
        at,
        *[top for top, _ in blocks],
        *[bottom for _, bottom in blocks],
        *cums,
        *parts,
        state_part,
    )
    two = n_head == 2 and w_rows % LANES == 0
    share = outer // n_head
    n_w = outer - 1 if two else outer
    tall = pl.BlockSpec((RING * rows, part), lambda g, q: (0, g))
    w_spec = pl.BlockSpec((w_rows, part), lambda g, q: (0, g))
    tile_shapes = [(RING, share, rows, w_rows)] * 2 if two else [(RING, outer, rows, w_rows)]
    acts, act_grad, write_carry, *tiles = call(
        functools.partial(finish_kernel, n_heads, n_w, outer, share),
        "finish",
        (RING,),
        [by_group] * RING
        + [state_spec] * RING
        + [message_spec] * RING
        + [log_spec] * RING
        + [spec[0] for spec in tile_specs[0]]
        + [spec[1] for spec in tile_specs[0]]
        + [cum_spec] * RING
        + [w_spec] * n_w
        + [by_group],
        [tall, by_group, proj_spec] + [const(*v) for v in tile_shapes],
        [
            shape((RING * rows, columns), bf16),
            shape((rows, columns), bf16),
            shape((rows, state_dim), f32),
        ]
        + [shape(v, bf16) for v in tile_shapes],
        [pltpu.VMEM((RING * rows, n_w * w_rows), f32)],
        after=[read_parts[0]],
    )(
        at,
        *local_acts,
        *fronts,
        *grad_parts,
        *logs,
        *[top for top, _ in blocks],
        *[bottom for _, bottom in blocks],
        *cums,
        *w_blocks[:n_w],
        x,
    )

    def to_owners(tile):
        return [tile[0]] + [swap(tile[j], j) for j in range(1, RING)]

    if two:
        mine, theirs = tiles
        got = lax.ppermute(theirs, "head", [(0, 1), (1, 0)])
        early = (mine.astype(f32) + got.astype(f32)).astype(bf16)
        read_got = [swap(read_parts[j], j) for j in range(1, RING)]
        early, read_got, w_last = lax.optimization_barrier((early, read_got, w_blocks[-1]))
        tile = mm(acts, w_last, NT).astype(bf16)

        def owner(s):
            return (s // RING + outer - 1) % outer // share

        both_axes = ("seq", "head")
        got = lax.ppermute(
            tile, both_axes, [(2 * s + 1 - owner(s), 2 * s + owner(s)) for s in range(n_seq)]
        )
        tile = (tile.astype(f32) + got.astype(f32)).astype(bf16).reshape(RING, rows, w_rows)
        late = [tile[0]] + [
            lax.ppermute(
                tile[j],
                both_axes,
                [(2 * s + owner(s), 2 * (s ^ j) + owner(s)) for s in range(n_seq)],
            )
            for j in range(1, RING)
        ]
        early = to_owners(early)
        input_grad = pl.pallas_call(
            functools.partial(place_kernel, outer, share),
            in_specs=[pl.BlockSpec(memory_space=pltpu.SMEM)]
            + [pl.BlockSpec(memory_space=pltpu.VMEM)] * (2 * RING),
            out_specs=pl.BlockSpec(memory_space=pltpu.VMEM),
            out_shape=shape((rows, share * RING * w_rows), bf16),
            compiler_params=pltpu.CompilerParams(vmem_limit_bytes=32 * 2**20),
            name="place",
        )(at, *early, *late)
    else:
        summed = lax.psum_scatter(tiles[0], "head", scatter_dimension=1, tiled=True)
        pieces = jnp.take(jnp.stack(to_owners(summed)), p ^ jnp.arange(RING), axis=0)
        input_grad = pieces.transpose(2, 1, 0, 3).reshape(rows, share * RING * w_rows)
    if not two:
        read_got = [swap(read_parts[j], j) for j in range(1, RING)]
    read_carry = read_parts[0].astype(f32) + sum(v.astype(f32) for v in read_got)
    both = jnp.stack([write_local + write_carry, read_local + read_carry])
    if n_head == 2:
        both = both + lax.ppermute(both, "head", [(0, 1), (1, 0)])
    else:
        both = lax.psum(both, "head")
    return (input_grad, act_grad, both[0], both[1])


def solution(mesh):
    return jax.shard_map(
        local,
        mesh=mesh,
        in_specs=(
            P("seq", "head"),
            P("seq", "head"),
            P("seq", None),
            P("seq", None),
            P("seq", "head"),
            P("seq", "head"),
        ),
        out_specs=(P("seq", "head"), P("seq", "head"), P("seq", None), P("seq", None)),
        check_vma=False,
    )
```

```python
import functools

import jax
import jax.numpy as jnp
from jax import lax
from jax.experimental import pallas as pl
from jax.experimental.pallas import tpu as pltpu
from jax.sharding import PartitionSpec as P

RING = 4
LANES = 128
EXTRA = 16
NT = (((1,), (1,)), ((), ()))
TN = (((0,), (0,)), ((), ()))
NN = (((1,), (0,)), ((), ()))
bf16, f32 = jnp.bfloat16, jnp.float32


def mm(a, b, dims):
    return lax.dot_general(a, b, dims, preferred_element_type=f32)


def mm_exact(a, b, dims):
    return lax.dot_general(a, b, dims, precision=lax.Precision.HIGHEST, preferred_element_type=f32)


def spread(columns, width):
    rows = columns.shape[0]
    return jnp.concatenate(
        [jnp.broadcast_to(columns[:, h : h + 1], (rows, width)) for h in range(columns.shape[1])],
        axis=1,
    )


def iota(shape, axis):
    return lax.broadcasted_iota(jnp.int32, shape, axis)


def three_parts(value):
    first = value.astype(bf16).astype(f32)
    second = (value - first).astype(bf16).astype(f32)
    return first, second, value - first - second


def cumulate(n_heads, log_tiles, cum, cum_t):
    parts = jnp.concatenate([tile[...] for tile in log_tiles], axis=0)
    rows = parts.shape[0]
    source, head = iota((LANES, LANES), 0), iota((LANES, LANES), 1)
    pick = (source < 3 * n_heads) & (lax.rem(source, n_heads) == head)
    logs = mm(parts, pick.astype(f32).astype(bf16), NN)
    upto = (iota((rows, rows), 0) <= iota((rows, rows), 1)).astype(f32)
    cum[...] = mm_exact(upto, logs, TN)
    if cum_t is not None:
        cum_t[...] = mm_exact(logs, upto, TN)


def group_of(value, g, heads, axis):
    shift = lax.rem(LANES - g * heads, LANES)
    value = pltpu.roll(value, shift, axis)
    return value[:, :heads] if axis == 1 else value[:heads]


def diagonal(heads, half, lo, col, row, each):
    later = iota((half, half), 1) >= iota((half, half), 0)
    for h in range(heads):
        log = row[h : h + 1, lo : lo + half] - col[lo : lo + half, h : h + 1]
        each(h, jnp.exp(jnp.where(later, log, -jnp.inf)))


def cumulate_own(log_t, cum, cum_t):
    n_heads, rows = log_t.shape
    logs = jnp.concatenate([log_t[...], jnp.zeros((LANES - n_heads, rows), f32)], axis=0)
    upto = (iota((rows, rows), 0) <= iota((rows, rows), 1)).astype(f32)
    cum[...] = mm_exact(upto, logs, (((0,), (1,)), ((), ())))
    if cum_t is not None:
        cum_t[...] = mm_exact(logs, upto, NN)


def edge_kernel(n_heads, at, x, dy, b, c, log_t, *refs):
    messages, cum = refs[:RING], refs[RING]
    g = pl.program_id(0)
    heads = n_heads // RING
    rows = x.shape[0]
    width = x.shape[1] // heads
    n = b.shape[1]

    @pl.when(g == 0)
    def _():
        cumulate_own(log_t, cum, None)

    col = group_of(cum[...], g, heads, 1)
    last = col[rows - 1 : rows, :]
    tailed = (x[...].astype(f32) * spread(jnp.exp(last - col), width)).astype(bf16)
    decayed = (dy[...].astype(f32) * spread(jnp.exp(col), width)).astype(bf16)
    ends = mm(b[...], tailed, TN).astype(bf16)
    fronts = mm(c[...], decayed, TN).astype(bf16)
    log = spread(last, width)
    for j in range(RING):

        @pl.when(lax.bitwise_xor(at[0], g) == j)
        def _():
            messages[j][:n] = ends
            messages[j][n : 2 * n] = fronts
            write_log(messages[j], log)


def pack_kernel(n_heads, dy, b, c, log_t, out):
    rows, columns = dy.shape
    fill = jnp.zeros((LANES - 3 * n_heads, rows), f32)
    logs = jnp.concatenate([*three_parts(log_t[...]), fill], axis=0)
    out[:, :columns] = dy[...]
    out[:, columns : columns + LANES] = b[...]
    out[:, columns + LANES : columns + 2 * LANES] = c[...]
    out[:, columns + 2 * LANES :] = logs.T.astype(bf16)


def own_kernel(n_heads, x, dy, b, c, log_t, write_local, read_local, total, cum, cum_t):
    g = pl.program_id(0)
    heads = n_heads // RING
    rows = x.shape[0]
    half = rows // 2
    width = x.shape[1] // heads

    @pl.when(g == 0)
    def _():
        total[...] = jnp.zeros_like(total)
        cumulate_own(log_t, cum, cum_t)

    col, row = group_of(cum[...], g, heads, 1), group_of(cum_t[...], g, heads, 0)
    mid = col[half - 1 : half, :]
    for i in range(2):
        lo = i * half
        parts = []

        def add(h, decay):
            span = slice(h * width, (h + 1) * width)
            parts.append(decay * mm(x[lo : lo + half, span], dy[lo : lo + half, span], NT))

        diagonal(heads, half, lo, col, row, add)
        total[lo : lo + half, lo : lo + half] += sum(parts)
    early = (x[:half].astype(f32) * spread(jnp.exp(mid - col[:half]), width)).astype(bf16)
    late = (dy[half:].astype(f32) * spread(jnp.exp(col[half:] - mid), width)).astype(bf16)
    total[:half, half:] += mm(early, late, NT)

    @pl.when(g == pl.num_programs(0) - 1)
    def _():
        write_local[...] = mm_exact(total[...], c[...].astype(f32), NN)
        read_local[...] = mm_exact(total[...], b[...].astype(f32), TN)


def block_kernel(n_heads, top, bottom, *refs):
    tiles, (act, fronts, log_row, cum_out, cum_t) = refs[:6], refs[6:]
    b = jnp.concatenate([tiles[0][...], tiles[1][...]], axis=0)
    c = jnp.concatenate([tiles[2][...], tiles[3][...]], axis=0)
    g = pl.program_id(0)
    heads = n_heads // RING
    half = top.shape[0]
    rows = 2 * half
    width = top.shape[1] // heads

    @pl.when(g == 0)
    def _():
        cumulate(n_heads, tiles[4:], cum_out, cum_t)

    col, row = group_of(cum_out[...], g, heads, 1), group_of(cum_t[...], g, heads, 0)
    mid, last = col[half - 1 : half, :], col[rows - 1 : rows, :]
    log_row[...] = spread(last, width)
    scores = mm(b, c, NT)
    late_f = bottom[...].astype(f32) * spread(jnp.exp(col[half:] - mid), width)
    late = late_f.astype(bf16)
    first = (top[...].astype(f32) * spread(jnp.exp(col[:half]), width)).astype(bf16)
    second = (late_f * spread(jnp.exp(mid), width)).astype(bf16)
    fronts[0] = (mm(c[:half], first, TN) + mm(c[half:], second, TN)).astype(bf16)
    cross = mm(scores[:half, half:].astype(bf16), late, NN)
    to_mid = jnp.exp(mid - col[:half])
    for i, dy in enumerate((top, bottom)):
        lo = i * half
        score = scores[lo : lo + half, lo : lo + half]

        def put(h, decay):
            span = slice(h * width, (h + 1) * width)
            out = mm((decay * score).astype(bf16), dy[:, span], NN)
            if i == 0:
                out += cross[:, span] * to_mid[:, h : h + 1]
            act[lo : lo + half, span] = out.astype(act.dtype)

        diagonal(heads, half, lo, col, row, put)


def log_over(p, logs, wanted):
    total = jnp.zeros_like(logs[0])
    for k in range(RING):
        total += jnp.where(wanted(lax.bitwise_xor(p, k)), logs[k], 0.0)
    return total


def combine_kernel(at, *refs):
    parts, (state_out, grad_out) = refs[:RING], refs[RING:]
    n = state_out.shape[0] - EXTRA
    logs = [log_of(part) for part in parts]
    p = at[0]
    state, grad = 0.0, 0.0
    for j in range(RING):
        own = lax.bitwise_xor(p, j)
        state += parts[j][:n].astype(f32) * jnp.exp(log_over(p, logs, lambda k: k > own))
        grad += parts[j][n : 2 * n].astype(f32) * jnp.exp(log_over(p, logs, lambda k: k < own))
    for out, value in ((state_out, state), (grad_out, grad)):
        out[:n] = value.astype(bf16)
        write_log(out, sum(logs))


def write_log(out, log):
    n, width = out.shape
    row = iota((EXTRA, width), 0)
    rows = jnp.zeros((EXTRA, width), f32)
    for i, part in enumerate(three_parts(log)):
        rows = jnp.where(row == i, part, rows)
    out[n - EXTRA :] = rows.astype(bf16)


def log_of(message):
    n = message.shape[0] - EXTRA
    tail = message[n:].astype(f32)
    return tail[0:1] + tail[1:2] + tail[2:3]


def merge_kernel(*refs):
    for near, far, out in ((*refs[:2], refs[4]), (*refs[2:4], refs[5])):
        n = near.shape[0] - EXTRA
        log = log_of(near)
        out[:n] = (near[:n].astype(f32) + far[:n].astype(f32) * jnp.exp(log)).astype(bf16)
        write_log(out, log + log_of(far))


def finish_kernel(n_heads, n_w, outer, share, at, *refs):
    locals_, refs = refs[:RING], refs[RING:]
    fronts, refs = refs[:RING], refs[RING:]
    quarters, refs = refs[:RING], refs[RING:]
    logs, refs = [r[...] for r in refs[:RING]], refs[RING:]
    tops, refs = refs[:RING], refs[RING:]
    bottoms, refs = refs[:RING], refs[RING:]
    cums, refs = refs[:RING], refs[RING:]
    w, refs = refs[:n_w], refs[n_w:]
    x, acts, own, write, *tiles, total = refs
    g, p = pl.program_id(0), at[0]
    heads = n_heads // RING
    rows = own.shape[0]
    width = own.shape[1] // heads
    n = quarters[0].shape[0] - EXTRA
    source = lax.bitwise_xor(p, g)
    carried = quarters[0][:n].astype(f32)
    for j in range(1, RING):
        carried = jnp.where(source == j, quarters[j][:n].astype(f32), carried)

    @pl.when(g == 0)
    def _():
        write[...] = jnp.zeros_like(write)
        total[...] = jnp.zeros_like(total)

    added = [front[0].astype(f32) for front in fronts]
    for j in range(RING):
        col = group_of(cums[j][...], g, heads, 1)
        tail = spread(jnp.exp(col[rows - 1 : rows, :] - col), width)
        place = lax.bitwise_xor(p, j)
        grads = carried * jnp.exp(log_over(p, logs, lambda k: k > place))
        for i in range(RING):
            if i != j:
                there = lax.bitwise_xor(p, i)
                weight = jnp.exp(log_over(p, logs, lambda k: (k > place) & (k < there)))
                grads += added[i] * jnp.where(there > place, weight, 0.0)
        grads = grads.astype(bf16)
        b = jnp.concatenate([tops[j][...], bottoms[j][...]], axis=0)
        out = mm(b, grads, NN) * tail + locals_[j][...].astype(f32)
        out = out.astype(acts.dtype)
        acts[j * rows : (j + 1) * rows, :] = out
        if j == 0:
            own[...] = out
            write[...] += mm((x[...].astype(f32) * tail).astype(bf16), grads, NT)
    for k in range(n_w):
        n_rows = w[k].shape[0]
        total[:, k * n_rows : (k + 1) * n_rows] += mm(acts[...], w[k][...], NT)

    @pl.when(g == pl.num_programs(0) - 1)
    def _():
        if len(tiles) == 1:
            for k in range(n_w):
                put_tile(tiles[0], lax.rem(at[1] + k, outer), total, k, n_rows)
        else:
            for tile in tiles:
                tile[...] = jnp.zeros_like(tile)
            for k in range(n_w):
                o = lax.rem(at[1] + k, outer)
                for tile, side in zip(tiles, (at[2], 1 - at[2])):

                    @pl.when(lax.div(o, share) == side)
                    def _():
                        put_tile(tile, lax.rem(o, share), total, k, n_rows)


def put_tile(tile, slot, total, k, n_rows):
    rows = total.shape[0] // RING
    for j in range(RING):
        part = total[j * rows : (j + 1) * rows, k * n_rows : (k + 1) * n_rows]
        tile[j, slot] = part.astype(tile.dtype)


def read_kernel(n_heads, at, *refs):
    tops, refs = refs[:RING], refs[RING:]
    bottoms, refs = refs[:RING], refs[RING:]
    cums, refs = list(refs[: RING - 1]), refs[RING - 1 :]
    log_tiles, refs = refs[:2], refs[2:]
    parts, (carried, *outs, last_cum) = refs[:RING], refs[RING:]
    cumulate(n_heads, log_tiles, last_cum, None)
    cums.append(last_cum)
    logs = [log_of(part) for part in parts]
    p = at[0]
    heads = n_heads // RING
    half = tops[0].shape[0]
    n = carried.shape[0] - EXTRA
    width = carried.shape[1] // heads
    for j in range(RING):
        own = lax.bitwise_xor(p, j)
        total = carried[:n].astype(f32) * jnp.exp(log_over(p, logs, lambda k: k < own))
        for i in range(RING):
            if i != j:
                there = lax.bitwise_xor(p, i)
                weight = jnp.exp(log_over(p, logs, lambda k: (k < own) & (k > there)))
                total += parts[i][:n].astype(f32) * jnp.where(there < own, weight, 0.0)
        states = total.astype(bf16)
        decay = spread(jnp.exp(group_of(cums[j][...], p, heads, 1)), width)
        for i, dy in enumerate((tops[j], bottoms[j])):
            at_rows = slice(i * half, (i + 1) * half)
            scaled = (dy[...].astype(f32) * decay[at_rows]).astype(bf16)
            outs[j][at_rows] = mm(scaled, states, NT).astype(bf16)


def place_kernel(outer, share, at, *refs):
    blocks, late, out = refs[:RING], refs[RING:-1], refs[-1]
    p, z, side = at[0], at[1], at[2]
    width = out.shape[1] // (share * RING)
    last = lax.rem(z + outer - 1, outer)
    for slot in range(share):
        for j in range(RING):
            column = pl.multiple_of((slot * RING + lax.bitwise_xor(p, j)) * width, width)

            @pl.when(side * share + slot == last)
            def _():
                out[:, pl.ds(column, width)] = late[j][...]

            @pl.when(side * share + slot != last)
            def _():
                out[:, pl.ds(column, width)] = blocks[j][slot]


def call(kernel, name, grid, in_specs, out_specs, out_shape, scratch=(), after=()):
    n_in, n_after = len(in_specs), len(after)

    def body(at, *refs):
        kernel(at, *refs[:n_in], *refs[n_in + n_after :])

    fn = pl.pallas_call(
        body,
        grid_spec=pltpu.PrefetchScalarGridSpec(
            num_scalar_prefetch=1,
            grid=grid,
            in_specs=list(in_specs) + [pl.BlockSpec(memory_space=pl.ANY)] * n_after,
            out_specs=out_specs,
            scratch_shapes=list(scratch),
        ),
        out_shape=out_shape,
        compiler_params=pltpu.CompilerParams(vmem_limit_bytes=56 * 2**20),
        cost_estimate=pl.CostEstimate(flops=0, bytes_accessed=0, transcendentals=0),
        name=name,
    )
    return lambda *operands: fn(*operands, *after)


def local(x, dy, write_proj, read_proj, log_decay, w_in):
    rows, columns = x.shape
    half = rows // 2
    state_dim = write_proj.shape[1]
    n_heads = log_decay.shape[1]
    heads = n_heads // RING
    width = columns // n_heads
    part = heads * width
    w_rows = w_in.shape[0]
    n_seq, n_head = lax.axis_size("seq"), lax.axis_size("head")
    outer = n_seq // RING
    place = lax.axis_index("seq")
    side = lax.axis_index("head")
    p, z = place % RING, place // RING
    at = jnp.stack([p, z, side]).astype(jnp.int32)

    def swap(value, j):
        return lax.ppermute(value, "seq", [(s, s ^ j) for s in range(n_seq)])

    def along(value, d):
        return lax.ppermute(
            value, "seq", [(s, s + d * RING) for s in range(n_seq) if 0 <= s + d * RING < n_seq]
        )

    w_blocks = [w_in]

    def turn_w():
        turn = [(s, (s - RING) % n_seq) for s in range(n_seq)]
        w_blocks.append(lax.ppermute(w_blocks[-1], "seq", turn))

    turn_w()

    def const(*shape):
        return pl.BlockSpec(shape, lambda g, q: (0,) * len(shape))

    by_group = pl.BlockSpec((rows, part), lambda g, q: (0, g))
    state_spec = pl.BlockSpec((1, state_dim, part), lambda g, q: (g, 0, 0))
    log_spec = pl.BlockSpec((1, part), lambda g, q: (0, g))
    cum_spec = const(rows, LANES)
    proj_spec = const(rows, state_dim)
    message_spec = const(state_dim + EXTRA, part)
    shape = jax.ShapeDtypeStruct
    state_shape = shape((RING, state_dim, part), bf16)
    log_shape = shape((1, columns), f32)
    cum_shape = shape((rows, LANES), f32)
    message_shape = shape((state_dim + EXTRA, part), bf16)
    cum_scratch, cum_t_scratch = pltpu.VMEM((rows, LANES), f32), pltpu.VMEM((LANES, rows), f32)

    log_in_spec = const(n_heads, rows)
    log_t = log_decay.T
    own_specs = [by_group, by_group, proj_spec, proj_spec, log_in_spec]
    part_spec = const(2 * state_dim + EXTRA, part)
    parts = call(
        functools.partial(edge_kernel, n_heads),
        "edges",
        (RING,),
        own_specs,
        [part_spec] * RING,
        [shape((2 * state_dim + EXTRA, part), bf16)] * RING,
        [cum_scratch],
    )(at, x, dy, write_proj, read_proj, log_t)
    parts = [parts[0]] + [swap(parts[j], j) for j in range(1, RING)]

    write_local, read_local = call(
        functools.partial(lambda *refs: own_kernel(n_heads, *refs[1:])),
        "own_tokens",
        (RING,),
        own_specs,
        [proj_spec] * 2,
        [shape((rows, state_dim), f32)] * 2,
        [pltpu.VMEM((rows, rows), f32), cum_scratch, cum_t_scratch],
    )(at, x, dy, write_proj, read_proj, log_t)

    packed = call(
        functools.partial(lambda *refs: pack_kernel(n_heads, *refs[1:])),
        "pack",
        (1,),
        [const(rows, columns), proj_spec, proj_spec, log_in_spec],
        const(rows, columns + 3 * LANES),
        shape((rows, columns + 3 * LANES), bf16),
    )(at, dy, write_proj, read_proj, log_t)

    def halves(width, column):
        upper = pl.BlockSpec((half, width), lambda g, q: (0, column(g, q)))
        lower = pl.BlockSpec((half, width), lambda g, q: (1, column(g, q)))
        return [(upper, lower)] * (RING - 1) + [(upper, upper)]

    half_specs = halves(part, lambda g, q: g)
    mine_specs = halves(part, lambda g, q: q[0])
    tile_specs = [halves(LANES, lambda g, q, i=i: columns // LANES + i) for i in range(3)]

    def block(j, top, bottom, after=()):
        return call(
            functools.partial(lambda *refs: block_kernel(n_heads, *refs[1:])),
            "tokens",
            (RING,),
            [*half_specs[j]] + [spec for specs in tile_specs for spec in specs[j]],
            [by_group, state_spec, log_spec, cum_spec],
            [shape((rows, columns), bf16), state_shape, log_shape, cum_shape],
            [cum_t_scratch],
            after,
        )(at, top, bottom, *([top, bottom] * 3))

    results = [block(0, packed, packed)]
    logs = [results[0][2]]
    packed, parts, logs, read_local = lax.optimization_barrier((packed, parts, logs, read_local))
    from_x, from_y = lax.optimization_barrier((swap(packed, 1), swap(packed, 2)))

    def combine():
        return call(
            combine_kernel,
            "messages",
            (1,),
            [part_spec] * RING,
            [message_spec] * 2,
            [message_shape] * 2,
        )(at, *parts)

    def merge(*pairs):
        return call(
            lambda q, *refs: merge_kernel(*refs),
            "merge",
            (1,),
            [message_spec] * 4,
            [message_spec] * 2,
            [message_shape] * 2,
        )(at, *pairs)

    state_span, grad_span = combine()
    d = 1
    while d < outer:
        state_got, grad_got = along(state_span, d), along(grad_span, -d)
        if d == 1:
            state_part, grad_part = state_got, grad_got
        else:
            state_part, grad_part = merge(state_part, state_got, grad_part, grad_got)
        if 2 * d < outer:
            state_span, grad_span = merge(state_span, state_got, grad_span, grad_got)
        d *= 2
    state_got, grad_got, w_blocks[-1] = lax.optimization_barrier(
        (state_got, grad_got, w_blocks[-1])
    )
    turn_w()
    from_x, from_y, grad_part = lax.optimization_barrier((from_x, from_y, grad_part))
    blocks = [(packed, packed), (from_x, from_x), (from_y, from_y)]
    blocks.append((swap(from_x[:half], 2), swap(from_y[half:], 1)))
    results += [block(j, *blocks[j]) for j in range(1, RING - 1)]
    logs += [v[2] for v in results[1:]]
    logs, grad_part = lax.optimization_barrier((logs, grad_part))
    grad_parts = [grad_part] + [swap(grad_part, j) for j in range(1, RING)]

    read_parts = call(
        functools.partial(read_kernel, n_heads),
        "read_carry",
        (1,),
        [spec[0] for spec in mine_specs]
        + [spec[1] for spec in mine_specs]
        + [cum_spec] * (RING - 1)
        + list(tile_specs[2][-1])
        + [part_spec] * RING
        + [message_spec],
        [proj_spec] * RING,
        [shape((rows, state_dim), bf16)] * RING,
        [cum_scratch],
    )(
        at,
        *[top for top, _ in blocks],
        *[bottom for _, bottom in blocks],
        *[v[3] for v in results],
        *blocks[-1],
        *parts,
        state_part,
    )

    read_parts, w_blocks[-1] = lax.optimization_barrier((read_parts, w_blocks[-1]))
    after = [read_parts[0]]
    if outer > 2:
        after.append(w_blocks[-1])
    results.append(block(RING - 1, *blocks[-1], after))
    logs.append(results[-1][2])
    while len(w_blocks) < outer:
        turn_w()
    local_acts, fronts, _, cums = zip(*results)
    two = n_head == 2 and w_rows % LANES == 0
    share = outer // n_head
    n_w = outer - 1 if two else outer
    tall = pl.BlockSpec((RING * rows, part), lambda g, q: (0, g))
    w_spec = pl.BlockSpec((w_rows, part), lambda g, q: (0, g))
    tile_shapes = [(RING, share, rows, w_rows)] * 2 if two else [(RING, outer, rows, w_rows)]
    acts, act_grad, write_carry, *tiles = call(
        functools.partial(finish_kernel, n_heads, n_w, outer, share),
        "finish",
        (RING,),
        [by_group] * RING
        + [state_spec] * RING
        + [message_spec] * RING
        + [log_spec] * RING
        + [spec[0] for spec in tile_specs[0]]
        + [spec[1] for spec in tile_specs[0]]
        + [cum_spec] * RING
        + [w_spec] * n_w
        + [by_group],
        [tall, by_group, proj_spec] + [const(*v) for v in tile_shapes],
        [
            shape((RING * rows, columns), bf16),
            shape((rows, columns), bf16),
            shape((rows, state_dim), f32),
        ]
        + [shape(v, bf16) for v in tile_shapes],
        [pltpu.VMEM((RING * rows, n_w * w_rows), f32)],
    )(
        at,
        *local_acts,
        *fronts,
        *grad_parts,
        *logs,
        *[top for top, _ in blocks],
        *[bottom for _, bottom in blocks],
        *cums,
        *w_blocks[:n_w],
        x,
    )

    def to_owners(tile):
        return [tile[0]] + [swap(tile[j], j) for j in range(1, RING)]

    if two:
        mine, theirs = tiles
        got = lax.ppermute(theirs, "head", [(0, 1), (1, 0)])
        early = (mine.astype(f32) + got.astype(f32)).astype(bf16)
        read_got = [swap(read_parts[j], j) for j in range(1, RING)]
        early, read_got, w_last = lax.optimization_barrier((early, read_got, w_blocks[-1]))
        tile = mm(acts, w_last, NT).astype(bf16)

        def owner(s):
            return (s // RING + outer - 1) % outer // share

        both_axes = ("seq", "head")
        got = lax.ppermute(
            tile, both_axes, [(2 * s + 1 - owner(s), 2 * s + owner(s)) for s in range(n_seq)]
        )
        tile = (tile.astype(f32) + got.astype(f32)).astype(bf16).reshape(RING, rows, w_rows)
        late = [tile[0]] + [
            lax.ppermute(
                tile[j],
                both_axes,
                [(2 * s + owner(s), 2 * (s ^ j) + owner(s)) for s in range(n_seq)],
            )
            for j in range(1, RING)
        ]
        early = to_owners(early)
        input_grad = pl.pallas_call(
            functools.partial(place_kernel, outer, share),
            in_specs=[pl.BlockSpec(memory_space=pltpu.SMEM)]
            + [pl.BlockSpec(memory_space=pltpu.VMEM)] * (2 * RING),
            out_specs=pl.BlockSpec(memory_space=pltpu.VMEM),
            out_shape=shape((rows, share * RING * w_rows), bf16),
            compiler_params=pltpu.CompilerParams(vmem_limit_bytes=32 * 2**20),
            name="place",
        )(at, *early, *late)
    else:
        summed = lax.psum_scatter(tiles[0], "head", scatter_dimension=1, tiled=True)
        pieces = jnp.take(jnp.stack(to_owners(summed)), p ^ jnp.arange(RING), axis=0)
        input_grad = pieces.transpose(2, 1, 0, 3).reshape(rows, share * RING * w_rows)
    if not two:
        read_got = [swap(read_parts[j], j) for j in range(1, RING)]
    read_carry = read_parts[0].astype(f32) + sum(v.astype(f32) for v in read_got)
    both = jnp.stack([write_local + write_carry, read_local + read_carry])
    if n_head == 2:
        both = both + lax.ppermute(both, "head", [(0, 1), (1, 0)])
    else:
        both = lax.psum(both, "head")
    return (input_grad, act_grad, both[0], both[1])


def solution(mesh):
    return jax.shard_map(
        local,
        mesh=mesh,
        in_specs=(
            P("seq", "head"),
            P("seq", "head"),
            P("seq", None),
            P("seq", None),
            P("seq", "head"),
            P("seq", "head"),
        ),
        out_specs=(P("seq", "head"), P("seq", "head"), P("seq", None), P("seq", None)),
        check_vma=False,
    )
```

```python
import functools

import jax
import jax.numpy as jnp
from jax import lax
from jax.experimental import pallas as pl
from jax.experimental.pallas import tpu as pltpu
from jax.sharding import PartitionSpec as P

RING = 4
LANES = 128
EXTRA = 16
NT = (((1,), (1,)), ((), ()))
TN = (((0,), (0,)), ((), ()))
NN = (((1,), (0,)), ((), ()))
bf16, f32 = jnp.bfloat16, jnp.float32


def mm(a, b, dims):
    return lax.dot_general(a, b, dims, preferred_element_type=f32)


def mm_exact(a, b, dims):
    return lax.dot_general(a, b, dims, precision=lax.Precision.HIGHEST, preferred_element_type=f32)


def spread(columns, width):
    rows = columns.shape[0]
    return jnp.concatenate(
        [jnp.broadcast_to(columns[:, h : h + 1], (rows, width)) for h in range(columns.shape[1])],
        axis=1,
    )


def iota(shape, axis):
    return lax.broadcasted_iota(jnp.int32, shape, axis)


def three_parts(value):
    first = value.astype(bf16).astype(f32)
    second = (value - first).astype(bf16).astype(f32)
    return first, second, value - first - second


def cumulate(n_heads, log_tiles, cum, cum_t):
    parts = jnp.concatenate([tile[...] for tile in log_tiles], axis=0)
    rows = parts.shape[0]
    source, head = iota((LANES, LANES), 0), iota((LANES, LANES), 1)
    pick = (source < 3 * n_heads) & (lax.rem(source, n_heads) == head)
    logs = mm(parts, pick.astype(f32).astype(bf16), NN)
    upto = (iota((rows, rows), 0) <= iota((rows, rows), 1)).astype(f32)
    cum[...] = mm_exact(upto, logs, TN)
    if cum_t is not None:
        cum_t[...] = mm_exact(logs, upto, TN)


def group_of(value, g, heads, axis):
    shift = lax.rem(LANES - g * heads, LANES)
    value = pltpu.roll(value, shift, axis)
    return value[:, :heads] if axis == 1 else value[:heads]


def diagonal(heads, half, lo, col, row, each):
    later = iota((half, half), 1) >= iota((half, half), 0)
    for h in range(heads):
        log = row[h : h + 1, lo : lo + half] - col[lo : lo + half, h : h + 1]
        each(h, jnp.exp(jnp.where(later, log, -jnp.inf)))


def cumulate_own(log_t, cum, cum_t):
    n_heads, rows = log_t.shape
    logs = jnp.concatenate([log_t[...], jnp.zeros((LANES - n_heads, rows), f32)], axis=0)
    upto = (iota((rows, rows), 0) <= iota((rows, rows), 1)).astype(f32)
    cum[...] = mm_exact(upto, logs, (((0,), (1,)), ((), ())))
    if cum_t is not None:
        cum_t[...] = mm_exact(logs, upto, NN)


def edge_kernel(n_heads, at, x, dy, b, c, log_t, *refs):
    messages, cum = refs[:RING], refs[RING]
    g = pl.program_id(0)
    heads = n_heads // RING
    rows = x.shape[0]
    width = x.shape[1] // heads
    n = b.shape[1]

    @pl.when(g == 0)
    def _():
        cumulate_own(log_t, cum, None)

    col = group_of(cum[...], g, heads, 1)
    last = col[rows - 1 : rows, :]
    tailed = (x[...].astype(f32) * spread(jnp.exp(last - col), width)).astype(bf16)
    decayed = (dy[...].astype(f32) * spread(jnp.exp(col), width)).astype(bf16)
    ends = mm(b[...], tailed, TN).astype(bf16)
    fronts = mm(c[...], decayed, TN).astype(bf16)
    log = spread(last, width)
    for j in range(RING):

        @pl.when(lax.bitwise_xor(at[0], g) == j)
        def _():
            messages[j][:n] = ends
            messages[j][n : 2 * n] = fronts
            write_log(messages[j], log)


def pack_kernel(n_heads, dy, b, c, log_t, out):
    rows, columns = dy.shape
    fill = jnp.zeros((LANES - 3 * n_heads, rows), f32)
    logs = jnp.concatenate([*three_parts(log_t[...]), fill], axis=0)
    out[:, :columns] = dy[...]
    out[:, columns : columns + LANES] = b[...]
    out[:, columns + LANES : columns + 2 * LANES] = c[...]
    out[:, columns + 2 * LANES :] = logs.T.astype(bf16)


def own_kernel(n_heads, x, dy, b, c, log_t, write_local, read_local, total, cum, cum_t):
    g = pl.program_id(0)
    heads = n_heads // RING
    rows = x.shape[0]
    half = rows // 2
    width = x.shape[1] // heads

    @pl.when(g == 0)
    def _():
        total[...] = jnp.zeros_like(total)
        cumulate_own(log_t, cum, cum_t)

    col, row = group_of(cum[...], g, heads, 1), group_of(cum_t[...], g, heads, 0)
    mid = col[half - 1 : half, :]
    for i in range(2):
        lo = i * half
        parts = []

        def add(h, decay):
            span = slice(h * width, (h + 1) * width)
            parts.append(decay * mm(x[lo : lo + half, span], dy[lo : lo + half, span], NT))

        diagonal(heads, half, lo, col, row, add)
        total[lo : lo + half, lo : lo + half] += sum(parts)
    early = (x[:half].astype(f32) * spread(jnp.exp(mid - col[:half]), width)).astype(bf16)
    late = (dy[half:].astype(f32) * spread(jnp.exp(col[half:] - mid), width)).astype(bf16)
    total[:half, half:] += mm(early, late, NT)

    @pl.when(g == pl.num_programs(0) - 1)
    def _():
        write_local[...] = mm_exact(total[...], c[...].astype(f32), NN)
        read_local[...] = mm_exact(total[...], b[...].astype(f32), TN)


def block_kernel(n_heads, top, bottom, *refs):
    tiles, (act, fronts, log_row, cum_out, cum_t) = refs[:6], refs[6:]
    b = jnp.concatenate([tiles[0][...], tiles[1][...]], axis=0)
    c = jnp.concatenate([tiles[2][...], tiles[3][...]], axis=0)
    g = pl.program_id(0)
    heads = n_heads // RING
    half = top.shape[0]
    rows = 2 * half
    width = top.shape[1] // heads

    @pl.when(g == 0)
    def _():
        cumulate(n_heads, tiles[4:], cum_out, cum_t)

    col, row = group_of(cum_out[...], g, heads, 1), group_of(cum_t[...], g, heads, 0)
    mid, last = col[half - 1 : half, :], col[rows - 1 : rows, :]
    log_row[...] = spread(last, width)
    scores = mm(b, c, NT)
    late_f = bottom[...].astype(f32) * spread(jnp.exp(col[half:] - mid), width)
    late = late_f.astype(bf16)
    first = (top[...].astype(f32) * spread(jnp.exp(col[:half]), width)).astype(bf16)
    second = (late_f * spread(jnp.exp(mid), width)).astype(bf16)
    fronts[0] = (mm(c[:half], first, TN) + mm(c[half:], second, TN)).astype(bf16)
    cross = mm(scores[:half, half:].astype(bf16), late, NN)
    to_mid = jnp.exp(mid - col[:half])
    for i, dy in enumerate((top, bottom)):
        lo = i * half
        score = scores[lo : lo + half, lo : lo + half]

        def put(h, decay):
            span = slice(h * width, (h + 1) * width)
            out = mm((decay * score).astype(bf16), dy[:, span], NN)
            if i == 0:
                out += cross[:, span] * to_mid[:, h : h + 1]
            act[lo : lo + half, span] = out.astype(act.dtype)

        diagonal(heads, half, lo, col, row, put)


def log_over(p, logs, wanted):
    total = jnp.zeros_like(logs[0])
    for k in range(RING):
        total += jnp.where(wanted(lax.bitwise_xor(p, k)), logs[k], 0.0)
    return total


def combine_kernel(at, *refs):
    parts, (state_out, grad_out) = refs[:RING], refs[RING:]
    n = state_out.shape[0] - EXTRA
    logs = [log_of(part) for part in parts]
    p = at[0]
    state, grad = 0.0, 0.0
    for j in range(RING):
        own = lax.bitwise_xor(p, j)
        state += parts[j][:n].astype(f32) * jnp.exp(log_over(p, logs, lambda k: k > own))
        grad += parts[j][n : 2 * n].astype(f32) * jnp.exp(log_over(p, logs, lambda k: k < own))
    for out, value in ((state_out, state), (grad_out, grad)):
        out[:n] = value.astype(bf16)
        write_log(out, sum(logs))


def write_log(out, log):
    n, width = out.shape
    row = iota((EXTRA, width), 0)
    rows = jnp.zeros((EXTRA, width), f32)
    for i, part in enumerate(three_parts(log)):
        rows = jnp.where(row == i, part, rows)
    out[n - EXTRA :] = rows.astype(bf16)


def log_of(message):
    n = message.shape[0] - EXTRA
    tail = message[n:].astype(f32)
    return tail[0:1] + tail[1:2] + tail[2:3]


def merge_kernel(*refs):
    for near, far, out in ((*refs[:2], refs[4]), (*refs[2:4], refs[5])):
        n = near.shape[0] - EXTRA
        log = log_of(near)
        out[:n] = (near[:n].astype(f32) + far[:n].astype(f32) * jnp.exp(log)).astype(bf16)
        write_log(out, log + log_of(far))


def merged(near, far, weight=1.0):
    n = near.shape[0] - EXTRA
    log = log_of(near)
    value = near[:n].astype(f32) + far[:n].astype(f32) * (jnp.exp(log) * weight)
    return value, log + log_of(far)


def across_kernel(outer, at, state, state_far, grad, grad_far, out):
    n = out.shape[0] - EXTRA
    lower = at[1] < outer // 2
    (state_value, state_log), (grad_value, grad_log) = merged(state, state_far), merged(grad, grad_far)
    out[:n] = jnp.where(lower, state_value, grad_value).astype(bf16)
    write_log(out, jnp.where(lower, state_log, grad_log))


def settle_kernel(outer, at, state, grad, got, state_out, grad_out):
    lower = (at[1] < outer // 2).astype(f32)
    for near, weight, out in ((state, 1.0 - lower, state_out), (grad, lower, grad_out)):
        n = near.shape[0] - EXTRA
        value, log = merged(near, got, weight)
        out[:n] = value.astype(bf16)
        write_log(out, log)


def finish_kernel(n_heads, n_w, outer, share, at, *refs):
    locals_, refs = refs[:RING], refs[RING:]
    fronts, refs = refs[:RING], refs[RING:]
    quarters, refs = refs[:RING], refs[RING:]
    logs, refs = [r[...] for r in refs[:RING]], refs[RING:]
    tops, refs = refs[:RING], refs[RING:]
    bottoms, refs = refs[:RING], refs[RING:]
    cums, refs = refs[:RING], refs[RING:]
    w, refs = refs[:n_w], refs[n_w:]
    x, acts, own, write, *tiles, total = refs
    g, p = pl.program_id(0), at[0]
    heads = n_heads // RING
    rows = own.shape[0]
    width = own.shape[1] // heads
    n = quarters[0].shape[0] - EXTRA
    source = lax.bitwise_xor(p, g)
    carried = quarters[0][:n].astype(f32)
    for j in range(1, RING):
        carried = jnp.where(source == j, quarters[j][:n].astype(f32), carried)

    @pl.when(g == 0)
    def _():
        write[...] = jnp.zeros_like(write)
        total[...] = jnp.zeros_like(total)

    added = [front[0].astype(f32) for front in fronts]
    for j in range(RING):
        col = group_of(cums[j][...], g, heads, 1)
        tail = spread(jnp.exp(col[rows - 1 : rows, :] - col), width)
        place = lax.bitwise_xor(p, j)
        grads = carried * jnp.exp(log_over(p, logs, lambda k: k > place))
        for i in range(RING):
            if i != j:
                there = lax.bitwise_xor(p, i)
                weight = jnp.exp(log_over(p, logs, lambda k: (k > place) & (k < there)))
                grads += added[i] * jnp.where(there > place, weight, 0.0)
        grads = grads.astype(bf16)
        b = jnp.concatenate([tops[j][...], bottoms[j][...]], axis=0)
        out = mm(b, grads, NN) * tail + locals_[j][...].astype(f32)
        out = out.astype(acts.dtype)
        acts[j * rows : (j + 1) * rows, :] = out
        if j == 0:
            own[...] = out
            write[...] += mm((x[...].astype(f32) * tail).astype(bf16), grads, NT)
    for k in range(n_w):
        n_rows = w[k].shape[0]
        total[:, k * n_rows : (k + 1) * n_rows] += mm(acts[...], w[k][...], NT)

    @pl.when(g == pl.num_programs(0) - 1)
    def _():
        if len(tiles) == 1:
            for k in range(n_w):
                put_tile(tiles[0], lax.rem(at[1] + k, outer), total, k, n_rows)
        else:
            for tile in tiles:
                tile[...] = jnp.zeros_like(tile)
            for k in range(n_w):
                o = lax.rem(at[1] + k, outer)
                for tile, side in zip(tiles, (at[2], 1 - at[2])):

                    @pl.when(lax.div(o, share) == side)
                    def _():
                        put_tile(tile, lax.rem(o, share), total, k, n_rows)


def put_tile(tile, slot, total, k, n_rows):
    rows = total.shape[0] // RING
    for j in range(RING):
        part = total[j * rows : (j + 1) * rows, k * n_rows : (k + 1) * n_rows]
        tile[j, slot] = part.astype(tile.dtype)


def read_kernel(n_heads, at, *refs):
    tops, refs = refs[:RING], refs[RING:]
    bottoms, refs = refs[:RING], refs[RING:]
    cums, refs = list(refs[: RING - 1]), refs[RING - 1 :]
    log_tiles, refs = refs[:2], refs[2:]
    parts, (carried, *outs, last_cum) = refs[:RING], refs[RING:]
    cumulate(n_heads, log_tiles, last_cum, None)
    cums.append(last_cum)
    logs = [log_of(part) for part in parts]
    p = at[0]
    heads = n_heads // RING
    half = tops[0].shape[0]
    n = carried.shape[0] - EXTRA
    width = carried.shape[1] // heads
    for j in range(RING):
        own = lax.bitwise_xor(p, j)
        total = carried[:n].astype(f32) * jnp.exp(log_over(p, logs, lambda k: k < own))
        for i in range(RING):
            if i != j:
                there = lax.bitwise_xor(p, i)
                weight = jnp.exp(log_over(p, logs, lambda k: (k < own) & (k > there)))
                total += parts[i][:n].astype(f32) * jnp.where(there < own, weight, 0.0)
        states = total.astype(bf16)
        decay = spread(jnp.exp(group_of(cums[j][...], p, heads, 1)), width)
        for i, dy in enumerate((tops[j], bottoms[j])):
            at_rows = slice(i * half, (i + 1) * half)
            scaled = (dy[...].astype(f32) * decay[at_rows]).astype(bf16)
            outs[j][at_rows] = mm(scaled, states, NT).astype(bf16)


def place_kernel(outer, share, at, *refs):
    blocks, late, out = refs[:RING], refs[RING:-1], refs[-1]
    p, z, side = at[0], at[1], at[2]
    width = out.shape[1] // (share * RING)
    last = lax.rem(z + outer - 1, outer)
    for slot in range(share):
        for j in range(RING):
            column = pl.multiple_of((slot * RING + lax.bitwise_xor(p, j)) * width, width)

            @pl.when(side * share + slot == last)
            def _():
                out[:, pl.ds(column, width)] = late[j][...]

            @pl.when(side * share + slot != last)
            def _():
                out[:, pl.ds(column, width)] = blocks[j][slot]


def call(kernel, name, grid, in_specs, out_specs, out_shape, scratch=(), after=()):
    n_in, n_after = len(in_specs), len(after)

    def body(at, *refs):
        kernel(at, *refs[:n_in], *refs[n_in + n_after :])

    fn = pl.pallas_call(
        body,
        grid_spec=pltpu.PrefetchScalarGridSpec(
            num_scalar_prefetch=1,
            grid=grid,
            in_specs=list(in_specs) + [pl.BlockSpec(memory_space=pl.ANY)] * n_after,
            out_specs=out_specs,
            scratch_shapes=list(scratch),
        ),
        out_shape=out_shape,
        compiler_params=pltpu.CompilerParams(vmem_limit_bytes=56 * 2**20),
        cost_estimate=pl.CostEstimate(flops=0, bytes_accessed=0, transcendentals=0),
        name=name,
    )
    return lambda *operands: fn(*operands, *after)


def local(x, dy, write_proj, read_proj, log_decay, w_in):
    rows, columns = x.shape
    half = rows // 2
    state_dim = write_proj.shape[1]
    n_heads = log_decay.shape[1]
    heads = n_heads // RING
    width = columns // n_heads
    part = heads * width
    w_rows = w_in.shape[0]
    n_seq, n_head = lax.axis_size("seq"), lax.axis_size("head")
    outer = n_seq // RING
    place = lax.axis_index("seq")
    side = lax.axis_index("head")
    p, z = place % RING, place // RING
    at = jnp.stack([p, z, side]).astype(jnp.int32)

    def swap(value, j):
        return lax.ppermute(value, "seq", [(s, s ^ j) for s in range(n_seq)])

    def along(value, d):
        return lax.ppermute(
            value, "seq", [(s, s + d * RING) for s in range(n_seq) if 0 <= s + d * RING < n_seq]
        )

    w_blocks = [w_in]

    def turn_w():
        turn = [(s, (s - RING) % n_seq) for s in range(n_seq)]
        w_blocks.append(lax.ppermute(w_blocks[-1], "seq", turn))

    turn_w()

    def const(*shape):
        return pl.BlockSpec(shape, lambda g, q: (0,) * len(shape))

    by_group = pl.BlockSpec((rows, part), lambda g, q: (0, g))
    state_spec = pl.BlockSpec((1, state_dim, part), lambda g, q: (g, 0, 0))
    log_spec = pl.BlockSpec((1, part), lambda g, q: (0, g))
    cum_spec = const(rows, LANES)
    proj_spec = const(rows, state_dim)
    message_spec = const(state_dim + EXTRA, part)
    shape = jax.ShapeDtypeStruct
    state_shape = shape((RING, state_dim, part), bf16)
    log_shape = shape((1, columns), f32)
    cum_shape = shape((rows, LANES), f32)
    message_shape = shape((state_dim + EXTRA, part), bf16)
    cum_scratch, cum_t_scratch = pltpu.VMEM((rows, LANES), f32), pltpu.VMEM((LANES, rows), f32)

    log_in_spec = const(n_heads, rows)
    log_t = log_decay.T
    own_specs = [by_group, by_group, proj_spec, proj_spec, log_in_spec]
    part_spec = const(2 * state_dim + EXTRA, part)
    parts = call(
        functools.partial(edge_kernel, n_heads),
        "edges",
        (RING,),
        own_specs,
        [part_spec] * RING,
        [shape((2 * state_dim + EXTRA, part), bf16)] * RING,
        [cum_scratch],
    )(at, x, dy, write_proj, read_proj, log_t)
    parts = [parts[0]] + [swap(parts[j], j) for j in range(1, RING)]

    write_local, read_local = call(
        functools.partial(lambda *refs: own_kernel(n_heads, *refs[1:])),
        "own_tokens",
        (RING,),
        own_specs,
        [proj_spec] * 2,
        [shape((rows, state_dim), f32)] * 2,
        [pltpu.VMEM((rows, rows), f32), cum_scratch, cum_t_scratch],
    )(at, x, dy, write_proj, read_proj, log_t)

    packed = call(
        functools.partial(lambda *refs: pack_kernel(n_heads, *refs[1:])),
        "pack",
        (1,),
        [const(rows, columns), proj_spec, proj_spec, log_in_spec],
        const(rows, columns + 3 * LANES),
        shape((rows, columns + 3 * LANES), bf16),
    )(at, dy, write_proj, read_proj, log_t)

    def halves(width, column):
        upper = pl.BlockSpec((half, width), lambda g, q: (0, column(g, q)))
        lower = pl.BlockSpec((half, width), lambda g, q: (1, column(g, q)))
        return [(upper, lower)] * (RING - 1) + [(upper, upper)]

    half_specs = halves(part, lambda g, q: g)
    mine_specs = halves(part, lambda g, q: q[0])
    tile_specs = [halves(LANES, lambda g, q, i=i: columns // LANES + i) for i in range(3)]

    def block(j, top, bottom, after=()):
        return call(
            functools.partial(lambda *refs: block_kernel(n_heads, *refs[1:])),
            "tokens",
            (RING,),
            [*half_specs[j]] + [spec for specs in tile_specs for spec in specs[j]],
            [by_group, state_spec, log_spec, cum_spec],
            [shape((rows, columns), bf16), state_shape, log_shape, cum_shape],
            [cum_t_scratch],
            after,
        )(at, top, bottom, *([top, bottom] * 3))

    results = [block(0, packed, packed)]
    logs = [results[0][2]]
    packed, parts, logs, read_local = lax.optimization_barrier((packed, parts, logs, read_local))
    from_x, from_y = lax.optimization_barrier((swap(packed, 1), swap(packed, 2)))

    def combine():
        return call(
            combine_kernel,
            "messages",
            (1,),
            [part_spec] * RING,
            [message_spec] * 2,
            [message_shape] * 2,
        )(at, *parts)

    def merge(*pairs):
        return call(
            lambda q, *refs: merge_kernel(*refs),
            "merge",
            (1,),
            [message_spec] * 4,
            [message_spec] * 2,
            [message_shape] * 2,
        )(at, *pairs)

    state_span, grad_span = combine()
    d = 1
    while d < outer:
        if outer == 4 and d == 2:
            got = lax.ppermute(across, "seq", [(s, s ^ (d * RING)) for s in range(n_seq)])
            state_part, grad_part = call(
                functools.partial(settle_kernel, outer),
                "settle",
                (1,),
                [message_spec] * 3,
                [message_spec] * 2,
                [message_shape] * 2,
            )(at, state_part, grad_part, got)
            got, w_blocks[-1] = lax.optimization_barrier((got, w_blocks[-1]))
            break
        state_got, grad_got = along(state_span, d), along(grad_span, -d)
        if d == 1:
            state_part, grad_part = state_got, grad_got
        else:
            state_part, grad_part = merge(state_part, state_got, grad_part, grad_got)
        if outer == 4:
            across = call(
                functools.partial(across_kernel, outer),
                "across",
                (1,),
                [message_spec] * 4,
                message_spec,
                message_shape,
            )(at, state_span, state_got, grad_span, grad_got)
        elif 2 * d < outer:
            state_span, grad_span = merge(state_span, state_got, grad_span, grad_got)
        d *= 2
    turn_w()
    from_x, from_y, grad_part = lax.optimization_barrier((from_x, from_y, grad_part))
    blocks = [(packed, packed), (from_x, from_x), (from_y, from_y)]
    blocks.append((swap(from_x[:half], 2), swap(from_y[half:], 1)))
    results += [block(j, *blocks[j]) for j in range(1, RING - 1)]
    logs += [v[2] for v in results[1:]]
    logs, grad_part = lax.optimization_barrier((logs, grad_part))
    grad_parts = [grad_part] + [swap(grad_part, j) for j in range(1, RING)]

    read_parts = call(
        functools.partial(read_kernel, n_heads),
        "read_carry",
        (1,),
        [spec[0] for spec in mine_specs]
        + [spec[1] for spec in mine_specs]
        + [cum_spec] * (RING - 1)
        + list(tile_specs[2][-1])
        + [part_spec] * RING
        + [message_spec],
        [proj_spec] * RING,
        [shape((rows, state_dim), bf16)] * RING,
        [cum_scratch],
    )(
        at,
        *[top for top, _ in blocks],
        *[bottom for _, bottom in blocks],
        *[v[3] for v in results],
        *blocks[-1],
        *parts,
        state_part,
    )

    read_parts, w_blocks[-1] = lax.optimization_barrier((read_parts, w_blocks[-1]))
    after = [read_parts[0]]
    if outer > 2:
        after.append(w_blocks[-1])
    results.append(block(RING - 1, *blocks[-1], after))
    logs.append(results[-1][2])
    while len(w_blocks) < outer:
        turn_w()
    local_acts, fronts, _, cums = zip(*results)
    two = n_head == 2 and w_rows % LANES == 0
    share = outer // n_head
    n_w = outer - 1 if two else outer
    tall = pl.BlockSpec((RING * rows, part), lambda g, q: (0, g))
    w_spec = pl.BlockSpec((w_rows, part), lambda g, q: (0, g))
    tile_shapes = [(RING, share, rows, w_rows)] * 2 if two else [(RING, outer, rows, w_rows)]
    acts, act_grad, write_carry, *tiles = call(
        functools.partial(finish_kernel, n_heads, n_w, outer, share),
        "finish",
        (RING,),
        [by_group] * RING
        + [state_spec] * RING
        + [message_spec] * RING
        + [log_spec] * RING
        + [spec[0] for spec in tile_specs[0]]
        + [spec[1] for spec in tile_specs[0]]
        + [cum_spec] * RING
        + [w_spec] * n_w
        + [by_group],
        [tall, by_group, proj_spec] + [const(*v) for v in tile_shapes],
        [
            shape((RING * rows, columns), bf16),
            shape((rows, columns), bf16),
            shape((rows, state_dim), f32),
        ]
        + [shape(v, bf16) for v in tile_shapes],
        [pltpu.VMEM((RING * rows, n_w * w_rows), f32)],
    )(
        at,
        *local_acts,
        *fronts,
        *grad_parts,
        *logs,
        *[top for top, _ in blocks],
        *[bottom for _, bottom in blocks],
        *cums,
        *w_blocks[:n_w],
        x,
    )

    def to_owners(tile):
        return [tile[0]] + [swap(tile[j], j) for j in range(1, RING)]

    if two:
        mine, theirs = tiles
        got = lax.ppermute(theirs, "head", [(0, 1), (1, 0)])
        early = (mine.astype(f32) + got.astype(f32)).astype(bf16)
        read_got = [swap(read_parts[j], j) for j in range(1, RING)]
        early, read_got, w_last = lax.optimization_barrier((early, read_got, w_blocks[-1]))
        tile = mm(acts, w_last, NT).astype(bf16)

        def owner(s):
            return (s // RING + outer - 1) % outer // share

        both_axes = ("seq", "head")
        got = lax.ppermute(
            tile, both_axes, [(2 * s + 1 - owner(s), 2 * s + owner(s)) for s in range(n_seq)]
        )
        tile = (tile.astype(f32) + got.astype(f32)).astype(bf16).reshape(RING, rows, w_rows)
        late = [tile[0]] + [
            lax.ppermute(
                tile[j],
                both_axes,
                [(2 * s + owner(s), 2 * (s ^ j) + owner(s)) for s in range(n_seq)],
            )
            for j in range(1, RING)
        ]
        early = to_owners(early)
        input_grad = pl.pallas_call(
            functools.partial(place_kernel, outer, share),
            in_specs=[pl.BlockSpec(memory_space=pltpu.SMEM)]
            + [pl.BlockSpec(memory_space=pltpu.VMEM)] * (2 * RING),
            out_specs=pl.BlockSpec(memory_space=pltpu.VMEM),
            out_shape=shape((rows, share * RING * w_rows), bf16),
            compiler_params=pltpu.CompilerParams(vmem_limit_bytes=32 * 2**20),
            name="place",
        )(at, *early, *late)
    else:
        summed = lax.psum_scatter(tiles[0], "head", scatter_dimension=1, tiled=True)
        pieces = jnp.take(jnp.stack(to_owners(summed)), p ^ jnp.arange(RING), axis=0)
        input_grad = pieces.transpose(2, 1, 0, 3).reshape(rows, share * RING * w_rows)
    if not two:
        read_got = [swap(read_parts[j], j) for j in range(1, RING)]
    read_carry = read_parts[0].astype(f32) + sum(v.astype(f32) for v in read_got)
    both = jnp.stack([write_local + write_carry, read_local + read_carry])
    if n_head == 2:
        both = both + lax.ppermute(both, "head", [(0, 1), (1, 0)])
    else:
        both = lax.psum(both, "head")
    return (input_grad, act_grad, both[0], both[1])


def solution(mesh):
    return jax.shard_map(
        local,
        mesh=mesh,
        in_specs=(
            P("seq", "head"),
            P("seq", "head"),
            P("seq", None),
            P("seq", None),
            P("seq", "head"),
            P("seq", "head"),
        ),
        out_specs=(P("seq", "head"), P("seq", "head"), P("seq", None), P("seq", None)),
        check_vma=False,
    )
```

```python
import functools

import jax
import jax.numpy as jnp
from jax import lax
from jax.experimental import pallas as pl
from jax.experimental.pallas import tpu as pltpu
from jax.sharding import PartitionSpec as P

RING = 4
LANES = 128
EXTRA = 16
NT = (((1,), (1,)), ((), ()))
TN = (((0,), (0,)), ((), ()))
NN = (((1,), (0,)), ((), ()))
bf16, f32 = jnp.bfloat16, jnp.float32


def mm(a, b, dims):
    return lax.dot_general(a, b, dims, preferred_element_type=f32)


def mm_exact(a, b, dims):
    return lax.dot_general(a, b, dims, precision=lax.Precision.HIGHEST, preferred_element_type=f32)


def spread(columns, width):
    rows = columns.shape[0]
    return jnp.concatenate(
        [jnp.broadcast_to(columns[:, h : h + 1], (rows, width)) for h in range(columns.shape[1])],
        axis=1,
    )


def iota(shape, axis):
    return lax.broadcasted_iota(jnp.int32, shape, axis)


def three_parts(value):
    first = value.astype(bf16).astype(f32)
    second = (value - first).astype(bf16).astype(f32)
    return first, second, value - first - second


def cumulate(n_heads, log_tiles, cum, cum_t):
    parts = jnp.concatenate([tile[...] for tile in log_tiles], axis=0)
    rows = parts.shape[0]
    source, head = iota((LANES, LANES), 0), iota((LANES, LANES), 1)
    pick = (source < 3 * n_heads) & (lax.rem(source, n_heads) == head)
    logs = mm(parts, pick.astype(f32).astype(bf16), NN)
    upto = (iota((rows, rows), 0) <= iota((rows, rows), 1)).astype(f32)
    cum[...] = mm_exact(upto, logs, TN)
    if cum_t is not None:
        cum_t[...] = mm_exact(logs, upto, TN)


def group_of(value, g, heads, axis):
    shift = lax.rem(LANES - g * heads, LANES)
    value = pltpu.roll(value, shift, axis)
    return value[:, :heads] if axis == 1 else value[:heads]


def diagonal(heads, half, lo, col, row, each):
    later = iota((half, half), 1) >= iota((half, half), 0)
    for h in range(heads):
        log = row[h : h + 1, lo : lo + half] - col[lo : lo + half, h : h + 1]
        each(h, jnp.exp(jnp.where(later, log, -jnp.inf)))


def cumulate_own(log_t, cum, cum_t):
    n_heads, rows = log_t.shape
    logs = jnp.concatenate([log_t[...], jnp.zeros((LANES - n_heads, rows), f32)], axis=0)
    upto = (iota((rows, rows), 0) <= iota((rows, rows), 1)).astype(f32)
    cum[...] = mm_exact(upto, logs, (((0,), (1,)), ((), ())))
    if cum_t is not None:
        cum_t[...] = mm_exact(logs, upto, NN)


def edge_kernel(n_heads, at, x, dy, b, c, log_t, *refs):
    messages, cum = refs[:RING], refs[RING]
    g = pl.program_id(0)
    heads = n_heads // RING
    rows = x.shape[0]
    width = x.shape[1] // heads
    n = b.shape[1]

    @pl.when(g == 0)
    def _():
        cumulate_own(log_t, cum, None)

    col = group_of(cum[...], g, heads, 1)
    last = col[rows - 1 : rows, :]
    tailed = (x[...].astype(f32) * spread(jnp.exp(last - col), width)).astype(bf16)
    decayed = (dy[...].astype(f32) * spread(jnp.exp(col), width)).astype(bf16)
    ends = mm(b[...], tailed, TN).astype(bf16)
    fronts = mm(c[...], decayed, TN).astype(bf16)
    log = spread(last, width)
    for j in range(RING):

        @pl.when(lax.bitwise_xor(at[0], g) == j)
        def _():
            messages[j][:n] = ends
            messages[j][n : 2 * n] = fronts
            write_log(messages[j], log)


def pack_kernel(n_heads, dy, b, c, log_t, out):
    rows, columns = dy.shape
    fill = jnp.zeros((LANES - 3 * n_heads, rows), f32)
    logs = jnp.concatenate([*three_parts(log_t[...]), fill], axis=0)
    out[:, :columns] = dy[...]
    out[:, columns : columns + LANES] = b[...]
    out[:, columns + LANES : columns + 2 * LANES] = c[...]
    out[:, columns + 2 * LANES :] = logs.T.astype(bf16)


def own_kernel(n_heads, x, dy, b, c, log_t, write_local, read_local, total, cum, cum_t):
    g = pl.program_id(0)
    heads = n_heads // RING
    rows = x.shape[0]
    half = rows // 2
    width = x.shape[1] // heads

    @pl.when(g == 0)
    def _():
        total[...] = jnp.zeros_like(total)
        cumulate_own(log_t, cum, cum_t)

    col, row = group_of(cum[...], g, heads, 1), group_of(cum_t[...], g, heads, 0)
    mid = col[half - 1 : half, :]
    for i in range(2):
        lo = i * half
        parts = []

        def add(h, decay):
            span = slice(h * width, (h + 1) * width)
            parts.append(decay * mm(x[lo : lo + half, span], dy[lo : lo + half, span], NT))

        diagonal(heads, half, lo, col, row, add)
        total[lo : lo + half, lo : lo + half] += sum(parts)
    early = (x[:half].astype(f32) * spread(jnp.exp(mid - col[:half]), width)).astype(bf16)
    late = (dy[half:].astype(f32) * spread(jnp.exp(col[half:] - mid), width)).astype(bf16)
    total[:half, half:] += mm(early, late, NT)

    @pl.when(g == pl.num_programs(0) - 1)
    def _():
        write_local[...] = mm_exact(total[...], c[...].astype(f32), NN)
        read_local[...] = mm_exact(total[...], b[...].astype(f32), TN)


def block_kernel(n_heads, top, bottom, *refs):
    tiles, (act, fronts, log_row, cum_out, cum_t) = refs[:6], refs[6:]
    b = jnp.concatenate([tiles[0][...], tiles[1][...]], axis=0)
    c = jnp.concatenate([tiles[2][...], tiles[3][...]], axis=0)
    g = pl.program_id(0)
    heads = n_heads // RING
    half = top.shape[0]
    rows = 2 * half
    width = top.shape[1] // heads

    @pl.when(g == 0)
    def _():
        cumulate(n_heads, tiles[4:], cum_out, cum_t)

    col, row = group_of(cum_out[...], g, heads, 1), group_of(cum_t[...], g, heads, 0)
    mid, last = col[half - 1 : half, :], col[rows - 1 : rows, :]
    log_row[...] = spread(last, width)
    scores = mm(b, c, NT)
    late_f = bottom[...].astype(f32) * spread(jnp.exp(col[half:] - mid), width)
    late = late_f.astype(bf16)
    first = (top[...].astype(f32) * spread(jnp.exp(col[:half]), width)).astype(bf16)
    second = (late_f * spread(jnp.exp(mid), width)).astype(bf16)
    fronts[0] = (mm(c[:half], first, TN) + mm(c[half:], second, TN)).astype(bf16)
    cross = mm(scores[:half, half:].astype(bf16), late, NN)
    to_mid = jnp.exp(mid - col[:half])
    for i, dy in enumerate((top, bottom)):
        lo = i * half
        score = scores[lo : lo + half, lo : lo + half]

        def put(h, decay):
            span = slice(h * width, (h + 1) * width)
            out = mm((decay * score).astype(bf16), dy[:, span], NN)
            if i == 0:
                out += cross[:, span] * to_mid[:, h : h + 1]
            act[lo : lo + half, span] = out.astype(act.dtype)

        diagonal(heads, half, lo, col, row, put)


def log_over(p, logs, wanted):
    total = jnp.zeros_like(logs[0])
    for k in range(RING):
        total += jnp.where(wanted(lax.bitwise_xor(p, k)), logs[k], 0.0)
    return total


def combine_kernel(at, *refs):
    parts, (state_out, grad_out) = refs[:RING], refs[RING:]
    n = state_out.shape[0] - EXTRA
    logs = [log_of(part) for part in parts]
    p = at[0]
    state, grad = 0.0, 0.0
    for j in range(RING):
        own = lax.bitwise_xor(p, j)
        state += parts[j][:n].astype(f32) * jnp.exp(log_over(p, logs, lambda k: k > own))
        grad += parts[j][n : 2 * n].astype(f32) * jnp.exp(log_over(p, logs, lambda k: k < own))
    for out, value in ((state_out, state), (grad_out, grad)):
        out[:n] = value.astype(bf16)
        write_log(out, sum(logs))


def write_log(out, log):
    n, width = out.shape
    row = iota((EXTRA, width), 0)
    rows = jnp.zeros((EXTRA, width), f32)
    for i, part in enumerate(three_parts(log)):
        rows = jnp.where(row == i, part, rows)
    out[n - EXTRA :] = rows.astype(bf16)


def log_of(message):
    n = message.shape[0] - EXTRA
    tail = message[n:].astype(f32)
    return tail[0:1] + tail[1:2] + tail[2:3]


def merge_kernel(*refs):
    for near, far, out in ((*refs[:2], refs[4]), (*refs[2:4], refs[5])):
        n = near.shape[0] - EXTRA
        log = log_of(near)
        out[:n] = (near[:n].astype(f32) + far[:n].astype(f32) * jnp.exp(log)).astype(bf16)
        write_log(out, log + log_of(far))


def merged(near, far, weight=1.0):
    n = near.shape[0] - EXTRA
    log = log_of(near)
    value = near[:n].astype(f32) + far[:n].astype(f32) * (jnp.exp(log) * weight)
    return value, log + log_of(far)


def across_kernel(outer, at, state, state_far, grad, grad_far, out):
    n = out.shape[0] - EXTRA
    lower = at[1] < outer // 2
    (state_value, state_log), (grad_value, grad_log) = merged(state, state_far), merged(grad, grad_far)
    out[:n] = jnp.where(lower, state_value, grad_value).astype(bf16)
    write_log(out, jnp.where(lower, state_log, grad_log))


def settle_kernel(outer, at, state, grad, got, state_out, grad_out):
    lower = (at[1] < outer // 2).astype(f32)
    for near, weight, out in ((state, 1.0 - lower, state_out), (grad, lower, grad_out)):
        n = near.shape[0] - EXTRA
        value, log = merged(near, got, weight)
        out[:n] = value.astype(bf16)
        write_log(out, log)


def finish_kernel(n_heads, n_w, outer, share, at, *refs):
    locals_, refs = refs[:RING], refs[RING:]
    fronts, refs = refs[:RING], refs[RING:]
    quarters, refs = refs[:RING], refs[RING:]
    logs, refs = [r[...] for r in refs[:RING]], refs[RING:]
    tops, refs = refs[:RING], refs[RING:]
    bottoms, refs = refs[:RING], refs[RING:]
    cums, refs = refs[:RING], refs[RING:]
    w, refs = refs[:n_w], refs[n_w:]
    x, acts, own, write, *tiles, total = refs
    g, p = pl.program_id(0), at[0]
    heads = n_heads // RING
    rows = own.shape[0]
    width = own.shape[1] // heads
    n = quarters[0].shape[0] - EXTRA
    source = lax.bitwise_xor(p, g)
    carried = quarters[0][:n].astype(f32)
    for j in range(1, RING):
        carried = jnp.where(source == j, quarters[j][:n].astype(f32), carried)

    @pl.when(g == 0)
    def _():
        write[...] = jnp.zeros_like(write)
        total[...] = jnp.zeros_like(total)

    added = [front[0].astype(f32) for front in fronts]
    for j in range(RING):
        col = group_of(cums[j][...], g, heads, 1)
        tail = spread(jnp.exp(col[rows - 1 : rows, :] - col), width)
        place = lax.bitwise_xor(p, j)
        grads = carried * jnp.exp(log_over(p, logs, lambda k: k > place))
        for i in range(RING):
            if i != j:
                there = lax.bitwise_xor(p, i)
                weight = jnp.exp(log_over(p, logs, lambda k: (k > place) & (k < there)))
                grads += added[i] * jnp.where(there > place, weight, 0.0)
        grads = grads.astype(bf16)
        b = jnp.concatenate([tops[j][...], bottoms[j][...]], axis=0)
        out = mm(b, grads, NN) * tail + locals_[j][...].astype(f32)
        out = out.astype(acts.dtype)
        acts[j * rows : (j + 1) * rows, :] = out
        if j == 0:
            own[...] = out
            write[...] += mm((x[...].astype(f32) * tail).astype(bf16), grads, NT)
    for k in range(n_w):
        n_rows = w[k].shape[0]
        total[:, k * n_rows : (k + 1) * n_rows] += mm(acts[...], w[k][...], NT)

    @pl.when(g == pl.num_programs(0) - 1)
    def _():
        if len(tiles) == 1:
            for k in range(n_w):
                put_tile(tiles[0], lax.rem(at[1] + k, outer), total, k, n_rows)
        else:
            for tile in tiles:
                tile[...] = jnp.zeros_like(tile)
            for k in range(n_w):
                o = lax.rem(at[1] + k, outer)
                for tile, side in zip(tiles, (at[2], 1 - at[2])):

                    @pl.when(lax.div(o, share) == side)
                    def _():
                        put_tile(tile, lax.rem(o, share), total, k, n_rows)


def put_tile(tile, slot, total, k, n_rows):
    rows = total.shape[0] // RING
    for j in range(RING):
        part = total[j * rows : (j + 1) * rows, k * n_rows : (k + 1) * n_rows]
        tile[j, slot] = part.astype(tile.dtype)


def read_kernel(n_heads, at, *refs):
    tops, refs = refs[:RING], refs[RING:]
    bottoms, refs = refs[:RING], refs[RING:]
    cums, refs = list(refs[: RING - 1]), refs[RING - 1 :]
    log_tiles, refs = refs[:2], refs[2:]
    parts, (carried, *outs, last_cum) = refs[:RING], refs[RING:]
    cumulate(n_heads, log_tiles, last_cum, None)
    cums.append(last_cum)
    logs = [log_of(part) for part in parts]
    p = at[0]
    heads = n_heads // RING
    half = tops[0].shape[0]
    n = carried.shape[0] - EXTRA
    width = carried.shape[1] // heads
    for j in range(RING):
        own = lax.bitwise_xor(p, j)
        total = carried[:n].astype(f32) * jnp.exp(log_over(p, logs, lambda k: k < own))
        for i in range(RING):
            if i != j:
                there = lax.bitwise_xor(p, i)
                weight = jnp.exp(log_over(p, logs, lambda k: (k < own) & (k > there)))
                total += parts[i][:n].astype(f32) * jnp.where(there < own, weight, 0.0)
        states = total.astype(bf16)
        decay = spread(jnp.exp(group_of(cums[j][...], p, heads, 1)), width)
        for i, dy in enumerate((tops[j], bottoms[j])):
            at_rows = slice(i * half, (i + 1) * half)
            scaled = (dy[...].astype(f32) * decay[at_rows]).astype(bf16)
            outs[j][at_rows] = mm(scaled, states, NT).astype(bf16)


def early_kernel(at, mine, got, *refs):
    reads, outs = refs[:RING], refs[RING:]
    width = mine.shape[3]
    for j in range(RING):
        for slot in range(mine.shape[1]):
            value = mine[j, slot].astype(f32) + got[j, slot].astype(f32)
            outs[j][:, slot * width : (slot + 1) * width] = value.astype(bf16)
        outs[j][:, mine.shape[1] * width :] = reads[j][...]


def place_kernel(outer, share, at, *refs):
    blocks, late, out = refs[:RING], refs[RING:-1], refs[-1]
    p, z, side = at[0], at[1], at[2]
    width = out.shape[1] // (share * RING)
    last = lax.rem(z + outer - 1, outer)
    for slot in range(share):
        for j in range(RING):
            column = pl.multiple_of((slot * RING + lax.bitwise_xor(p, j)) * width, width)

            @pl.when(side * share + slot == last)
            def _():
                out[:, pl.ds(column, width)] = late[j][...]

            @pl.when(side * share + slot != last)
            def _():
                out[:, pl.ds(column, width)] = blocks[j][:, slot * width : (slot + 1) * width]


def call(kernel, name, grid, in_specs, out_specs, out_shape, scratch=(), after=()):
    n_in, n_after = len(in_specs), len(after)

    def body(at, *refs):
        kernel(at, *refs[:n_in], *refs[n_in + n_after :])

    fn = pl.pallas_call(
        body,
        grid_spec=pltpu.PrefetchScalarGridSpec(
            num_scalar_prefetch=1,
            grid=grid,
            in_specs=list(in_specs) + [pl.BlockSpec(memory_space=pl.ANY)] * n_after,
            out_specs=out_specs,
            scratch_shapes=list(scratch),
        ),
        out_shape=out_shape,
        compiler_params=pltpu.CompilerParams(vmem_limit_bytes=56 * 2**20),
        cost_estimate=pl.CostEstimate(flops=0, bytes_accessed=0, transcendentals=0),
        name=name,
    )
    return lambda *operands: fn(*operands, *after)


def local(x, dy, write_proj, read_proj, log_decay, w_in):
    rows, columns = x.shape
    half = rows // 2
    state_dim = write_proj.shape[1]
    n_heads = log_decay.shape[1]
    heads = n_heads // RING
    width = columns // n_heads
    part = heads * width
    w_rows = w_in.shape[0]
    n_seq, n_head = lax.axis_size("seq"), lax.axis_size("head")
    outer = n_seq // RING
    place = lax.axis_index("seq")
    side = lax.axis_index("head")
    p, z = place % RING, place // RING
    at = jnp.stack([p, z, side]).astype(jnp.int32)

    def swap(value, j):
        return lax.ppermute(value, "seq", [(s, s ^ j) for s in range(n_seq)])

    def along(value, d):
        return lax.ppermute(
            value, "seq", [(s, s + d * RING) for s in range(n_seq) if 0 <= s + d * RING < n_seq]
        )

    w_blocks = [w_in]

    def turn_w():
        turn = [(s, (s - RING) % n_seq) for s in range(n_seq)]
        w_blocks.append(lax.ppermute(w_blocks[-1], "seq", turn))

    turn_w()

    def const(*shape):
        return pl.BlockSpec(shape, lambda g, q: (0,) * len(shape))

    by_group = pl.BlockSpec((rows, part), lambda g, q: (0, g))
    state_spec = pl.BlockSpec((1, state_dim, part), lambda g, q: (g, 0, 0))
    log_spec = pl.BlockSpec((1, part), lambda g, q: (0, g))
    cum_spec = const(rows, LANES)
    proj_spec = const(rows, state_dim)
    message_spec = const(state_dim + EXTRA, part)
    shape = jax.ShapeDtypeStruct
    state_shape = shape((RING, state_dim, part), bf16)
    log_shape = shape((1, columns), f32)
    cum_shape = shape((rows, LANES), f32)
    message_shape = shape((state_dim + EXTRA, part), bf16)
    cum_scratch, cum_t_scratch = pltpu.VMEM((rows, LANES), f32), pltpu.VMEM((LANES, rows), f32)

    log_in_spec = const(n_heads, rows)
    log_t = log_decay.T
    own_specs = [by_group, by_group, proj_spec, proj_spec, log_in_spec]
    part_spec = const(2 * state_dim + EXTRA, part)
    parts = call(
        functools.partial(edge_kernel, n_heads),
        "edges",
        (RING,),
        own_specs,
        [part_spec] * RING,
        [shape((2 * state_dim + EXTRA, part), bf16)] * RING,
        [cum_scratch],
    )(at, x, dy, write_proj, read_proj, log_t)
    parts = [parts[0]] + [swap(parts[j], j) for j in range(1, RING)]

    write_local, read_local = call(
        functools.partial(lambda *refs: own_kernel(n_heads, *refs[1:])),
        "own_tokens",
        (RING,),
        own_specs,
        [proj_spec] * 2,
        [shape((rows, state_dim), f32)] * 2,
        [pltpu.VMEM((rows, rows), f32), cum_scratch, cum_t_scratch],
    )(at, x, dy, write_proj, read_proj, log_t)

    packed = call(
        functools.partial(lambda *refs: pack_kernel(n_heads, *refs[1:])),
        "pack",
        (1,),
        [const(rows, columns), proj_spec, proj_spec, log_in_spec],
        const(rows, columns + 3 * LANES),
        shape((rows, columns + 3 * LANES), bf16),
    )(at, dy, write_proj, read_proj, log_t)

    def halves(width, column):
        upper = pl.BlockSpec((half, width), lambda g, q: (0, column(g, q)))
        lower = pl.BlockSpec((half, width), lambda g, q: (1, column(g, q)))
        return [(upper, lower)] * (RING - 1) + [(upper, upper)]

    half_specs = halves(part, lambda g, q: g)
    mine_specs = halves(part, lambda g, q: q[0])
    tile_specs = [halves(LANES, lambda g, q, i=i: columns // LANES + i) for i in range(3)]

    def block(j, top, bottom, after=()):
        return call(
            functools.partial(lambda *refs: block_kernel(n_heads, *refs[1:])),
            "tokens",
            (RING,),
            [*half_specs[j]] + [spec for specs in tile_specs for spec in specs[j]],
            [by_group, state_spec, log_spec, cum_spec],
            [shape((rows, columns), bf16), state_shape, log_shape, cum_shape],
            [cum_t_scratch],
            after,
        )(at, top, bottom, *([top, bottom] * 3))

    results = [block(0, packed, packed)]
    logs = [results[0][2]]
    packed, parts, logs, read_local = lax.optimization_barrier((packed, parts, logs, read_local))
    from_x, from_y = lax.optimization_barrier((swap(packed, 1), swap(packed, 2)))

    def combine():
        return call(
            combine_kernel,
            "messages",
            (1,),
            [part_spec] * RING,
            [message_spec] * 2,
            [message_shape] * 2,
        )(at, *parts)

    def merge(*pairs):
        return call(
            lambda q, *refs: merge_kernel(*refs),
            "merge",
            (1,),
            [message_spec] * 4,
            [message_spec] * 2,
            [message_shape] * 2,
        )(at, *pairs)

    state_span, grad_span = combine()
    d = 1
    while d < outer:
        if outer == 4 and d == 2:
            got = lax.ppermute(across, "seq", [(s, s ^ (d * RING)) for s in range(n_seq)])
            state_part, grad_part = call(
                functools.partial(settle_kernel, outer),
                "settle",
                (1,),
                [message_spec] * 3,
                [message_spec] * 2,
                [message_shape] * 2,
            )(at, state_part, grad_part, got)
            got, w_blocks[-1] = lax.optimization_barrier((got, w_blocks[-1]))
            break
        state_got, grad_got = along(state_span, d), along(grad_span, -d)
        if d == 1:
            state_part, grad_part = state_got, grad_got
        else:
            state_part, grad_part = merge(state_part, state_got, grad_part, grad_got)
        if outer == 4:
            across = call(
                functools.partial(across_kernel, outer),
                "across",
                (1,),
                [message_spec] * 4,
                message_spec,
                message_shape,
            )(at, state_span, state_got, grad_span, grad_got)
        elif 2 * d < outer:
            state_span, grad_span = merge(state_span, state_got, grad_span, grad_got)
        d *= 2
    turn_w()
    from_x, from_y, grad_part = lax.optimization_barrier((from_x, from_y, grad_part))
    blocks = [(packed, packed), (from_x, from_x), (from_y, from_y)]
    blocks.append((swap(from_x[:half], 2), swap(from_y[half:], 1)))
    results += [block(j, *blocks[j]) for j in range(1, RING - 1)]
    logs += [v[2] for v in results[1:]]
    logs, grad_part = lax.optimization_barrier((logs, grad_part))
    grad_parts = [grad_part] + [swap(grad_part, j) for j in range(1, RING)]

    read_parts = call(
        functools.partial(read_kernel, n_heads),
        "read_carry",
        (1,),
        [spec[0] for spec in mine_specs]
        + [spec[1] for spec in mine_specs]
        + [cum_spec] * (RING - 1)
        + list(tile_specs[2][-1])
        + [part_spec] * RING
        + [message_spec],
        [proj_spec] * RING,
        [shape((rows, state_dim), bf16)] * RING,
        [cum_scratch],
    )(
        at,
        *[top for top, _ in blocks],
        *[bottom for _, bottom in blocks],
        *[v[3] for v in results],
        *blocks[-1],
        *parts,
        state_part,
    )

    read_parts, w_blocks[-1] = lax.optimization_barrier((read_parts, w_blocks[-1]))
    after = [read_parts[0]]
    if outer > 2:
        after.append(w_blocks[-1])
    results.append(block(RING - 1, *blocks[-1], after))
    logs.append(results[-1][2])
    while len(w_blocks) < outer:
        turn_w()
    local_acts, fronts, _, cums = zip(*results)
    two = n_head == 2 and w_rows % LANES == 0
    share = outer // n_head
    n_w = outer - 1 if two else outer
    tall = pl.BlockSpec((RING * rows, part), lambda g, q: (0, g))
    w_spec = pl.BlockSpec((w_rows, part), lambda g, q: (0, g))
    tile_shapes = [(RING, share, rows, w_rows)] * 2 if two else [(RING, outer, rows, w_rows)]
    acts, act_grad, write_carry, *tiles = call(
        functools.partial(finish_kernel, n_heads, n_w, outer, share),
        "finish",
        (RING,),
        [by_group] * RING
        + [state_spec] * RING
        + [message_spec] * RING
        + [log_spec] * RING
        + [spec[0] for spec in tile_specs[0]]
        + [spec[1] for spec in tile_specs[0]]
        + [cum_spec] * RING
        + [w_spec] * n_w
        + [by_group],
        [tall, by_group, proj_spec] + [const(*v) for v in tile_shapes],
        [
            shape((RING * rows, columns), bf16),
            shape((rows, columns), bf16),
            shape((rows, state_dim), f32),
        ]
        + [shape(v, bf16) for v in tile_shapes],
        [pltpu.VMEM((RING * rows, n_w * w_rows), f32)],
    )(
        at,
        *local_acts,
        *fronts,
        *grad_parts,
        *logs,
        *[top for top, _ in blocks],
        *[bottom for _, bottom in blocks],
        *cums,
        *w_blocks[:n_w],
        x,
    )

    def to_owners(tile):
        return [tile[0]] + [swap(tile[j], j) for j in range(1, RING)]

    if two:
        mine, theirs = tiles
        got = lax.ppermute(theirs, "head", [(0, 1), (1, 0)])
        pack_width = share * w_rows + state_dim
        early = call(
            early_kernel,
            "early_sums",
            (1,),
            [const(*mine.shape)] * 2 + [proj_spec] * RING,
            [const(rows, pack_width)] * RING,
            [shape((rows, pack_width), bf16)] * RING,
        )(at, mine, got, *read_parts)
        early, w_last = lax.optimization_barrier((early, w_blocks[-1]))
        tile = mm(acts, w_last, NT).astype(bf16)

        def owner(s):
            return (s // RING + outer - 1) % outer // share

        both_axes = ("seq", "head")
        got = lax.ppermute(
            tile, both_axes, [(2 * s + 1 - owner(s), 2 * s + owner(s)) for s in range(n_seq)]
        )
        tile = (tile.astype(f32) + got.astype(f32)).astype(bf16).reshape(RING, rows, w_rows)
        late = [tile[0]] + [
            lax.ppermute(
                tile[j],
                both_axes,
                [(2 * s + owner(s), 2 * (s ^ j) + owner(s)) for s in range(n_seq)],
            )
            for j in range(1, RING)
        ]
        early = to_owners(early)
        read_got = [v[:, share * w_rows :] for v in early[1:]]
        input_grad = pl.pallas_call(
            functools.partial(place_kernel, outer, share),
            in_specs=[pl.BlockSpec(memory_space=pltpu.SMEM)]
            + [pl.BlockSpec(memory_space=pltpu.VMEM)] * (2 * RING),
            out_specs=pl.BlockSpec(memory_space=pltpu.VMEM),
            out_shape=shape((rows, share * RING * w_rows), bf16),
            compiler_params=pltpu.CompilerParams(vmem_limit_bytes=32 * 2**20),
            name="place",
        )(at, *early, *late)
    else:
        summed = lax.psum_scatter(tiles[0], "head", scatter_dimension=1, tiled=True)
        pieces = jnp.take(jnp.stack(to_owners(summed)), p ^ jnp.arange(RING), axis=0)
        input_grad = pieces.transpose(2, 1, 0, 3).reshape(rows, share * RING * w_rows)
    if not two:
        read_got = [swap(read_parts[j], j) for j in range(1, RING)]
    read_carry = read_parts[0].astype(f32) + sum(v.astype(f32) for v in read_got)
    both = jnp.stack([write_local + write_carry, read_local + read_carry])
    if n_head == 2:
        both = both + lax.ppermute(both, "head", [(0, 1), (1, 0)])
    else:
        both = lax.psum(both, "head")
    return (input_grad, act_grad, both[0], both[1])


def solution(mesh):
    return jax.shard_map(
        local,
        mesh=mesh,
        in_specs=(
            P("seq", "head"),
            P("seq", "head"),
            P("seq", None),
            P("seq", None),
            P("seq", "head"),
            P("seq", "head"),
        ),
        out_specs=(P("seq", "head"), P("seq", "head"), P("seq", None), P("seq", None)),
        check_vma=False,
    )
```

```python
import functools

import jax
import jax.numpy as jnp
from jax import lax
from jax.experimental import pallas as pl
from jax.experimental.pallas import tpu as pltpu
from jax.sharding import PartitionSpec as P

RING = 4
LANES = 128
EXTRA = 16
NT = (((1,), (1,)), ((), ()))
TN = (((0,), (0,)), ((), ()))
NN = (((1,), (0,)), ((), ()))
bf16, f32 = jnp.bfloat16, jnp.float32


def mm(a, b, dims):
    return lax.dot_general(a, b, dims, preferred_element_type=f32)


def mm_exact(a, b, dims):
    return lax.dot_general(a, b, dims, precision=lax.Precision.HIGHEST, preferred_element_type=f32)


def spread(columns, width):
    rows = columns.shape[0]
    return jnp.concatenate(
        [jnp.broadcast_to(columns[:, h : h + 1], (rows, width)) for h in range(columns.shape[1])],
        axis=1,
    )


def iota(shape, axis):
    return lax.broadcasted_iota(jnp.int32, shape, axis)


def three_parts(value):
    first = value.astype(bf16).astype(f32)
    second = (value - first).astype(bf16).astype(f32)
    return first, second, value - first - second


def cumulate(n_heads, log_tiles, cum, cum_t):
    parts = jnp.concatenate([tile[...] for tile in log_tiles], axis=0)
    rows = parts.shape[0]
    source, head = iota((LANES, LANES), 0), iota((LANES, LANES), 1)
    pick = (source < 3 * n_heads) & (lax.rem(source, n_heads) == head)
    logs = mm(parts, pick.astype(f32).astype(bf16), NN)
    upto = (iota((rows, rows), 0) <= iota((rows, rows), 1)).astype(f32)
    cum[...] = mm_exact(upto, logs, TN)
    if cum_t is not None:
        cum_t[...] = mm_exact(logs, upto, TN)


def group_of(value, g, heads, axis):
    shift = lax.rem(LANES - g * heads, LANES)
    value = pltpu.roll(value, shift, axis)
    return value[:, :heads] if axis == 1 else value[:heads]


def diagonal(heads, half, lo, col, row, each):
    later = iota((half, half), 1) >= iota((half, half), 0)
    for h in range(heads):
        log = row[h : h + 1, lo : lo + half] - col[lo : lo + half, h : h + 1]
        each(h, jnp.exp(jnp.where(later, log, -jnp.inf)))


def cumulate_own(log_t, cum, cum_t):
    n_heads, rows = log_t.shape
    logs = jnp.concatenate([log_t[...], jnp.zeros((LANES - n_heads, rows), f32)], axis=0)
    upto = (iota((rows, rows), 0) <= iota((rows, rows), 1)).astype(f32)
    cum[...] = mm_exact(upto, logs, (((0,), (1,)), ((), ())))
    if cum_t is not None:
        cum_t[...] = mm_exact(logs, upto, NN)


def edge_kernel(n_heads, at, x, dy, b, c, log_t, *refs):
    messages, cum = refs[:RING], refs[RING]
    g = pl.program_id(0)
    heads = n_heads // RING
    rows = x.shape[0]
    width = x.shape[1] // heads
    n = b.shape[1]

    @pl.when(g == 0)
    def _():
        cumulate_own(log_t, cum, None)

    col = group_of(cum[...], g, heads, 1)
    last = col[rows - 1 : rows, :]
    tailed = (x[...].astype(f32) * spread(jnp.exp(last - col), width)).astype(bf16)
    decayed = (dy[...].astype(f32) * spread(jnp.exp(col), width)).astype(bf16)
    ends = mm(b[...], tailed, TN).astype(bf16)
    fronts = mm(c[...], decayed, TN).astype(bf16)
    log = spread(last, width)
    for j in range(RING):

        @pl.when(lax.bitwise_xor(at[0], g) == j)
        def _():
            messages[j][:n] = ends
            messages[j][n : 2 * n] = fronts
            write_log(messages[j], log)


def pack_kernel(n_heads, dy, b, c, log_t, out):
    rows, columns = dy.shape
    fill = jnp.zeros((LANES - 3 * n_heads, rows), f32)
    logs = jnp.concatenate([*three_parts(log_t[...]), fill], axis=0)
    out[:, :columns] = dy[...]
    out[:, columns : columns + LANES] = b[...]
    out[:, columns + LANES : columns + 2 * LANES] = c[...]
    out[:, columns + 2 * LANES :] = logs.T.astype(bf16)


def own_kernel(n_heads, x, dy, b, c, log_t, write_local, read_local, total, cum, cum_t):
    g = pl.program_id(0)
    heads = n_heads // RING
    rows = x.shape[0]
    half = rows // 2
    width = x.shape[1] // heads

    @pl.when(g == 0)
    def _():
        total[...] = jnp.zeros_like(total)
        cumulate_own(log_t, cum, cum_t)

    col, row = group_of(cum[...], g, heads, 1), group_of(cum_t[...], g, heads, 0)
    mid = col[half - 1 : half, :]
    for i in range(2):
        lo = i * half
        parts = []

        def add(h, decay):
            span = slice(h * width, (h + 1) * width)
            parts.append(decay * mm(x[lo : lo + half, span], dy[lo : lo + half, span], NT))

        diagonal(heads, half, lo, col, row, add)
        total[lo : lo + half, lo : lo + half] += sum(parts)
    early = (x[:half].astype(f32) * spread(jnp.exp(mid - col[:half]), width)).astype(bf16)
    late = (dy[half:].astype(f32) * spread(jnp.exp(col[half:] - mid), width)).astype(bf16)
    total[:half, half:] += mm(early, late, NT)

    @pl.when(g == pl.num_programs(0) - 1)
    def _():
        write_local[...] = mm_exact(total[...], c[...].astype(f32), NN)
        read_local[...] = mm_exact(total[...], b[...].astype(f32), TN)


def block_kernel(n_heads, top, bottom, *refs):
    tiles, (act, fronts, log_row, cum_out, cum_t) = refs[:6], refs[6:]
    b = jnp.concatenate([tiles[0][...], tiles[1][...]], axis=0)
    c = jnp.concatenate([tiles[2][...], tiles[3][...]], axis=0)
    g = pl.program_id(0)
    heads = n_heads // RING
    half = top.shape[0]
    rows = 2 * half
    width = top.shape[1] // heads

    @pl.when(g == 0)
    def _():
        cumulate(n_heads, tiles[4:], cum_out, cum_t)

    col, row = group_of(cum_out[...], g, heads, 1), group_of(cum_t[...], g, heads, 0)
    mid, last = col[half - 1 : half, :], col[rows - 1 : rows, :]
    log_row[...] = spread(last, width)
    scores = mm(b, c, NT)
    late_f = bottom[...].astype(f32) * spread(jnp.exp(col[half:] - mid), width)
    late = late_f.astype(bf16)
    first = (top[...].astype(f32) * spread(jnp.exp(col[:half]), width)).astype(bf16)
    second = (late_f * spread(jnp.exp(mid), width)).astype(bf16)
    fronts[0] = (mm(c[:half], first, TN) + mm(c[half:], second, TN)).astype(bf16)
    cross = mm(scores[:half, half:].astype(bf16), late, NN)
    to_mid = jnp.exp(mid - col[:half])
    for i, dy in enumerate((top, bottom)):
        lo = i * half
        score = scores[lo : lo + half, lo : lo + half]

        def put(h, decay):
            span = slice(h * width, (h + 1) * width)
            out = mm((decay * score).astype(bf16), dy[:, span], NN)
            if i == 0:
                out += cross[:, span] * to_mid[:, h : h + 1]
            act[lo : lo + half, span] = out.astype(act.dtype)

        diagonal(heads, half, lo, col, row, put)


def log_over(p, logs, wanted):
    total = jnp.zeros_like(logs[0])
    for k in range(RING):
        total += jnp.where(wanted(lax.bitwise_xor(p, k)), logs[k], 0.0)
    return total


def combine_kernel(at, *refs):
    parts, (state_out, grad_out) = refs[:RING], refs[RING:]
    n = state_out.shape[0] - EXTRA
    logs = [log_of(part) for part in parts]
    p = at[0]
    state, grad = 0.0, 0.0
    for j in range(RING):
        own = lax.bitwise_xor(p, j)
        state += parts[j][:n].astype(f32) * jnp.exp(log_over(p, logs, lambda k: k > own))
        grad += parts[j][n : 2 * n].astype(f32) * jnp.exp(log_over(p, logs, lambda k: k < own))
    for out, value in ((state_out, state), (grad_out, grad)):
        out[:n] = value.astype(bf16)
        write_log(out, sum(logs))


def write_log(out, log):
    n, width = out.shape
    row = iota((EXTRA, width), 0)
    rows = jnp.zeros((EXTRA, width), f32)
    for i, part in enumerate(three_parts(log)):
        rows = jnp.where(row == i, part, rows)
    out[n - EXTRA :] = rows.astype(bf16)


def log_of(message):
    n = message.shape[0] - EXTRA
    tail = message[n:].astype(f32)
    return tail[0:1] + tail[1:2] + tail[2:3]


def merge_kernel(*refs):
    for near, far, out in ((*refs[:2], refs[4]), (*refs[2:4], refs[5])):
        n = near.shape[0] - EXTRA
        log = log_of(near)
        out[:n] = (near[:n].astype(f32) + far[:n].astype(f32) * jnp.exp(log)).astype(bf16)
        write_log(out, log + log_of(far))


def merged(near, far, weight=1.0):
    n = near.shape[0] - EXTRA
    log = log_of(near)
    value = near[:n].astype(f32) + far[:n].astype(f32) * (jnp.exp(log) * weight)
    return value, log + log_of(far)


def across_kernel(outer, at, state, state_far, grad, grad_far, out):
    n = out.shape[0] - EXTRA
    lower = at[1] < outer // 2
    (state_value, state_log), (grad_value, grad_log) = merged(state, state_far), merged(grad, grad_far)
    out[:n] = jnp.where(lower, state_value, grad_value).astype(bf16)
    write_log(out, jnp.where(lower, state_log, grad_log))


def settle_kernel(outer, at, state, grad, got, state_out, grad_out):
    lower = (at[1] < outer // 2).astype(f32)
    for near, weight, out in ((state, 1.0 - lower, state_out), (grad, lower, grad_out)):
        n = near.shape[0] - EXTRA
        value, log = merged(near, got, weight)
        out[:n] = value.astype(bf16)
        write_log(out, log)


def finish_kernel(n_heads, n_w, outer, share, at, *refs):
    locals_, refs = refs[:RING], refs[RING:]
    fronts, refs = refs[:RING], refs[RING:]
    quarters, refs = refs[:RING], refs[RING:]
    logs, refs = [r[...] for r in refs[:RING]], refs[RING:]
    tops, refs = refs[:RING], refs[RING:]
    bottoms, refs = refs[:RING], refs[RING:]
    cums, refs = refs[:RING], refs[RING:]
    w, refs = refs[:n_w], refs[n_w:]
    x, acts, own, write, *tiles, total = refs
    g, p = pl.program_id(0), at[0]
    heads = n_heads // RING
    rows = own.shape[0]
    width = own.shape[1] // heads
    n = quarters[0].shape[0] - EXTRA
    source = lax.bitwise_xor(p, g)
    carried = quarters[0][:n].astype(f32)
    for j in range(1, RING):
        carried = jnp.where(source == j, quarters[j][:n].astype(f32), carried)

    @pl.when(g == 0)
    def _():
        write[...] = jnp.zeros_like(write)
        total[...] = jnp.zeros_like(total)

    added = [front[0].astype(f32) for front in fronts]
    for j in range(RING):
        col = group_of(cums[j][...], g, heads, 1)
        tail = spread(jnp.exp(col[rows - 1 : rows, :] - col), width)
        place = lax.bitwise_xor(p, j)
        grads = carried * jnp.exp(log_over(p, logs, lambda k: k > place))
        for i in range(RING):
            if i != j:
                there = lax.bitwise_xor(p, i)
                weight = jnp.exp(log_over(p, logs, lambda k: (k > place) & (k < there)))
                grads += added[i] * jnp.where(there > place, weight, 0.0)
        grads = grads.astype(bf16)
        b = jnp.concatenate([tops[j][...], bottoms[j][...]], axis=0)
        out = mm(b, grads, NN) * tail + locals_[j][...].astype(f32)
        out = out.astype(acts.dtype)
        acts[j * rows : (j + 1) * rows, :] = out
        if j == 0:
            own[...] = out
            write[...] += mm((x[...].astype(f32) * tail).astype(bf16), grads, NT)
    for k in range(n_w):
        n_rows = w[k].shape[0]
        total[:, k * n_rows : (k + 1) * n_rows] += mm(acts[...], w[k][...], NT)

    @pl.when(g == pl.num_programs(0) - 1)
    def _():
        if len(tiles) == 1:
            for k in range(n_w):
                put_tile(tiles[0], lax.rem(at[1] + k, outer), total, k, n_rows)
        else:
            for tile in tiles:
                tile[...] = jnp.zeros_like(tile)
            for k in range(n_w):
                o = lax.rem(at[1] + k, outer)
                for tile, side in zip(tiles, (at[2], 1 - at[2])):

                    @pl.when(lax.div(o, share) == side)
                    def _():
                        put_tile(tile, lax.rem(o, share), total, k, n_rows)


def put_tile(tile, slot, total, k, n_rows):
    rows = total.shape[0] // RING
    for j in range(RING):
        part = total[j * rows : (j + 1) * rows, k * n_rows : (k + 1) * n_rows]
        tile[j, slot] = part.astype(tile.dtype)


def read_kernel(n_heads, at, *refs):
    tops, refs = refs[:RING], refs[RING:]
    bottoms, refs = refs[:RING], refs[RING:]
    cums, refs = list(refs[: RING - 1]), refs[RING - 1 :]
    log_tiles, refs = refs[:2], refs[2:]
    parts, (carried, *outs, last_cum) = refs[:RING], refs[RING:]
    cumulate(n_heads, log_tiles, last_cum, None)
    cums.append(last_cum)
    logs = [log_of(part) for part in parts]
    p = at[0]
    heads = n_heads // RING
    half = tops[0].shape[0]
    n = carried.shape[0] - EXTRA
    width = carried.shape[1] // heads
    for j in range(RING):
        own = lax.bitwise_xor(p, j)
        total = carried[:n].astype(f32) * jnp.exp(log_over(p, logs, lambda k: k < own))
        for i in range(RING):
            if i != j:
                there = lax.bitwise_xor(p, i)
                weight = jnp.exp(log_over(p, logs, lambda k: (k < own) & (k > there)))
                total += parts[i][:n].astype(f32) * jnp.where(there < own, weight, 0.0)
        states = total.astype(bf16)
        decay = spread(jnp.exp(group_of(cums[j][...], p, heads, 1)), width)
        for i, dy in enumerate((tops[j], bottoms[j])):
            at_rows = slice(i * half, (i + 1) * half)
            scaled = (dy[...].astype(f32) * decay[at_rows]).astype(bf16)
            outs[j][at_rows] = mm(scaled, states, NT).astype(bf16)


def place_kernel(outer, share, at, *refs):
    blocks, late, out = refs[:RING], refs[RING:-1], refs[-1]
    p, z, side = at[0], at[1], at[2]
    width = out.shape[1] // (share * RING)
    last = lax.rem(z + outer - 1, outer)
    for slot in range(share):
        for j in range(RING):
            column = pl.multiple_of((slot * RING + lax.bitwise_xor(p, j)) * width, width)

            @pl.when(side * share + slot == last)
            def _():
                out[:, pl.ds(column, width)] = late[j][...]

            @pl.when(side * share + slot != last)
            def _():
                out[:, pl.ds(column, width)] = blocks[j][slot]


def call(kernel, name, grid, in_specs, out_specs, out_shape, scratch=(), after=()):
    n_in, n_after = len(in_specs), len(after)

    def body(at, *refs):
        kernel(at, *refs[:n_in], *refs[n_in + n_after :])

    fn = pl.pallas_call(
        body,
        grid_spec=pltpu.PrefetchScalarGridSpec(
            num_scalar_prefetch=1,
            grid=grid,
            in_specs=list(in_specs) + [pl.BlockSpec(memory_space=pl.ANY)] * n_after,
            out_specs=out_specs,
            scratch_shapes=list(scratch),
        ),
        out_shape=out_shape,
        compiler_params=pltpu.CompilerParams(vmem_limit_bytes=56 * 2**20),
        cost_estimate=pl.CostEstimate(flops=0, bytes_accessed=0, transcendentals=0),
        name=name,
    )
    return lambda *operands: fn(*operands, *after)


def local(x, dy, write_proj, read_proj, log_decay, w_in):
    rows, columns = x.shape
    half = rows // 2
    state_dim = write_proj.shape[1]
    n_heads = log_decay.shape[1]
    heads = n_heads // RING
    width = columns // n_heads
    part = heads * width
    w_rows = w_in.shape[0]
    n_seq, n_head = lax.axis_size("seq"), lax.axis_size("head")
    outer = n_seq // RING
    place = lax.axis_index("seq")
    side = lax.axis_index("head")
    p, z = place % RING, place // RING
    at = jnp.stack([p, z, side]).astype(jnp.int32)

    def swap(value, j):
        return lax.ppermute(value, "seq", [(s, s ^ j) for s in range(n_seq)])

    def along(value, d):
        return lax.ppermute(
            value, "seq", [(s, s + d * RING) for s in range(n_seq) if 0 <= s + d * RING < n_seq]
        )

    w_blocks = [w_in]

    def turn_w():
        turn = [(s, (s - RING) % n_seq) for s in range(n_seq)]
        w_blocks.append(lax.ppermute(w_blocks[-1], "seq", turn))

    turn_w()

    def const(*shape):
        return pl.BlockSpec(shape, lambda g, q: (0,) * len(shape))

    by_group = pl.BlockSpec((rows, part), lambda g, q: (0, g))
    state_spec = pl.BlockSpec((1, state_dim, part), lambda g, q: (g, 0, 0))
    log_spec = pl.BlockSpec((1, part), lambda g, q: (0, g))
    cum_spec = const(rows, LANES)
    proj_spec = const(rows, state_dim)
    message_spec = const(state_dim + EXTRA, part)
    shape = jax.ShapeDtypeStruct
    state_shape = shape((RING, state_dim, part), bf16)
    log_shape = shape((1, columns), f32)
    cum_shape = shape((rows, LANES), f32)
    message_shape = shape((state_dim + EXTRA, part), bf16)
    cum_scratch, cum_t_scratch = pltpu.VMEM((rows, LANES), f32), pltpu.VMEM((LANES, rows), f32)

    log_in_spec = const(n_heads, rows)
    log_t = log_decay.T
    own_specs = [by_group, by_group, proj_spec, proj_spec, log_in_spec]
    part_spec = const(2 * state_dim + EXTRA, part)
    parts = call(
        functools.partial(edge_kernel, n_heads),
        "edges",
        (RING,),
        own_specs,
        [part_spec] * RING,
        [shape((2 * state_dim + EXTRA, part), bf16)] * RING,
        [cum_scratch],
    )(at, x, dy, write_proj, read_proj, log_t)
    parts = [parts[0]] + [swap(parts[j], j) for j in range(1, RING)]

    write_local, read_local = call(
        functools.partial(lambda *refs: own_kernel(n_heads, *refs[1:])),
        "own_tokens",
        (RING,),
        own_specs,
        [proj_spec] * 2,
        [shape((rows, state_dim), f32)] * 2,
        [pltpu.VMEM((rows, rows), f32), cum_scratch, cum_t_scratch],
    )(at, x, dy, write_proj, read_proj, log_t)

    packed = call(
        functools.partial(lambda *refs: pack_kernel(n_heads, *refs[1:])),
        "pack",
        (1,),
        [const(rows, columns), proj_spec, proj_spec, log_in_spec],
        const(rows, columns + 3 * LANES),
        shape((rows, columns + 3 * LANES), bf16),
    )(at, dy, write_proj, read_proj, log_t)

    def halves(width, column):
        upper = pl.BlockSpec((half, width), lambda g, q: (0, column(g, q)))
        lower = pl.BlockSpec((half, width), lambda g, q: (1, column(g, q)))
        return [(upper, lower)] * (RING - 1) + [(upper, upper)]

    half_specs = halves(part, lambda g, q: g)
    mine_specs = halves(part, lambda g, q: q[0])
    tile_specs = [halves(LANES, lambda g, q, i=i: columns // LANES + i) for i in range(3)]

    def block(j, top, bottom, after=()):
        return call(
            functools.partial(lambda *refs: block_kernel(n_heads, *refs[1:])),
            "tokens",
            (RING,),
            [*half_specs[j]] + [spec for specs in tile_specs for spec in specs[j]],
            [by_group, state_spec, log_spec, cum_spec],
            [shape((rows, columns), bf16), state_shape, log_shape, cum_shape],
            [cum_t_scratch],
            after,
        )(at, top, bottom, *([top, bottom] * 3))

    results = [block(0, packed, packed)]
    logs = [results[0][2]]
    packed, parts, logs, read_local = lax.optimization_barrier((packed, parts, logs, read_local))
    from_x, from_y = lax.optimization_barrier((swap(packed, 1), swap(packed, 2)))

    def combine():
        return call(
            combine_kernel,
            "messages",
            (1,),
            [part_spec] * RING,
            [message_spec] * 2,
            [message_shape] * 2,
        )(at, *parts)

    def merge(*pairs):
        return call(
            lambda q, *refs: merge_kernel(*refs),
            "merge",
            (1,),
            [message_spec] * 4,
            [message_spec] * 2,
            [message_shape] * 2,
        )(at, *pairs)

    state_span, grad_span = combine()
    d = 1
    while d < outer:
        if outer == 4 and d == 2:
            got = lax.ppermute(across, "seq", [(s, s ^ (d * RING)) for s in range(n_seq)])
            state_part, grad_part = call(
                functools.partial(settle_kernel, outer),
                "settle",
                (1,),
                [message_spec] * 3,
                [message_spec] * 2,
                [message_shape] * 2,
            )(at, state_part, grad_part, got)
            got, w_blocks[-1] = lax.optimization_barrier((got, w_blocks[-1]))
            break
        state_got, grad_got = along(state_span, d), along(grad_span, -d)
        if d == 1:
            state_part, grad_part = state_got, grad_got
        else:
            state_part, grad_part = merge(state_part, state_got, grad_part, grad_got)
        if outer == 4:
            across = call(
                functools.partial(across_kernel, outer),
                "across",
                (1,),
                [message_spec] * 4,
                message_spec,
                message_shape,
            )(at, state_span, state_got, grad_span, grad_got)
        elif 2 * d < outer:
            state_span, grad_span = merge(state_span, state_got, grad_span, grad_got)
        d *= 2
    turn_w()
    from_x, from_y, grad_part = lax.optimization_barrier((from_x, from_y, grad_part))
    blocks = [(packed, packed), (from_x, from_x), (from_y, from_y)]
    blocks.append((swap(from_x[:half], 2), swap(from_y[half:], 1)))
    results += [block(j, *blocks[j]) for j in range(1, RING - 1)]
    logs += [v[2] for v in results[1:]]
    logs, w_blocks[-1] = lax.optimization_barrier((logs, w_blocks[-1]))
    logs, grad_part = lax.optimization_barrier((logs, grad_part))
    grad_parts = [grad_part] + [swap(grad_part, j) for j in range(1, RING)]

    read_parts = call(
        functools.partial(read_kernel, n_heads),
        "read_carry",
        (1,),
        [spec[0] for spec in mine_specs]
        + [spec[1] for spec in mine_specs]
        + [cum_spec] * (RING - 1)
        + list(tile_specs[2][-1])
        + [part_spec] * RING
        + [message_spec],
        [proj_spec] * RING,
        [shape((rows, state_dim), bf16)] * RING,
        [cum_scratch],
    )(
        at,
        *[top for top, _ in blocks],
        *[bottom for _, bottom in blocks],
        *[v[3] for v in results],
        *blocks[-1],
        *parts,
        state_part,
    )

    after = []
    if outer > 2:
        after.append(w_blocks[-1])
    results.append(block(RING - 1, *blocks[-1], after))
    logs.append(results[-1][2])
    while len(w_blocks) < outer:
        turn_w()
    local_acts, fronts, _, cums = zip(*results)
    two = n_head == 2 and w_rows % LANES == 0
    share = outer // n_head
    n_w = outer - 1 if two else outer
    tall = pl.BlockSpec((RING * rows, part), lambda g, q: (0, g))
    w_spec = pl.BlockSpec((w_rows, part), lambda g, q: (0, g))
    tile_shapes = [(RING, share, rows, w_rows)] * 2 if two else [(RING, outer, rows, w_rows)]
    acts, act_grad, write_carry, *tiles = call(
        functools.partial(finish_kernel, n_heads, n_w, outer, share),
        "finish",
        (RING,),
        [by_group] * RING
        + [state_spec] * RING
        + [message_spec] * RING
        + [log_spec] * RING
        + [spec[0] for spec in tile_specs[0]]
        + [spec[1] for spec in tile_specs[0]]
        + [cum_spec] * RING
        + [w_spec] * n_w
        + [by_group],
        [tall, by_group, proj_spec] + [const(*v) for v in tile_shapes],
        [
            shape((RING * rows, columns), bf16),
            shape((rows, columns), bf16),
            shape((rows, state_dim), f32),
        ]
        + [shape(v, bf16) for v in tile_shapes],
        [pltpu.VMEM((RING * rows, n_w * w_rows), f32)],
        after=[read_parts[0]],
    )(
        at,
        *local_acts,
        *fronts,
        *grad_parts,
        *logs,
        *[top for top, _ in blocks],
        *[bottom for _, bottom in blocks],
        *cums,
        *w_blocks[:n_w],
        x,
    )

    def to_owners(tile):
        return [tile[0]] + [swap(tile[j], j) for j in range(1, RING)]

    if two:
        mine, theirs = tiles
        got = lax.ppermute(theirs, "head", [(0, 1), (1, 0)])
        early = (mine.astype(f32) + got.astype(f32)).astype(bf16)
        read_got = [swap(read_parts[j], j) for j in range(1, RING)]
        early, read_got, w_last = lax.optimization_barrier((early, read_got, w_blocks[-1]))
        tile = mm(acts, w_last, NT).astype(bf16)

        def owner(s):
            return (s // RING + outer - 1) % outer // share

        both_axes = ("seq", "head")
        got = lax.ppermute(
            tile, both_axes, [(2 * s + 1 - owner(s), 2 * s + owner(s)) for s in range(n_seq)]
        )
        tile = (tile.astype(f32) + got.astype(f32)).astype(bf16).reshape(RING, rows, w_rows)
        late = [tile[0]] + [
            lax.ppermute(
                tile[j],
                both_axes,
                [(2 * s + owner(s), 2 * (s ^ j) + owner(s)) for s in range(n_seq)],
            )
            for j in range(1, RING)
        ]
        early = to_owners(early)
        input_grad = pl.pallas_call(
            functools.partial(place_kernel, outer, share),
            in_specs=[pl.BlockSpec(memory_space=pltpu.SMEM)]
            + [pl.BlockSpec(memory_space=pltpu.VMEM)] * (2 * RING),
            out_specs=pl.BlockSpec(memory_space=pltpu.VMEM),
            out_shape=shape((rows, share * RING * w_rows), bf16),
            compiler_params=pltpu.CompilerParams(vmem_limit_bytes=32 * 2**20),
            name="place",
        )(at, *early, *late)
    else:
        summed = lax.psum_scatter(tiles[0], "head", scatter_dimension=1, tiled=True)
        pieces = jnp.take(jnp.stack(to_owners(summed)), p ^ jnp.arange(RING), axis=0)
        input_grad = pieces.transpose(2, 1, 0, 3).reshape(rows, share * RING * w_rows)
    if not two:
        read_got = [swap(read_parts[j], j) for j in range(1, RING)]
    read_carry = read_parts[0].astype(f32) + sum(v.astype(f32) for v in read_got)
    both = jnp.stack([write_local + write_carry, read_local + read_carry])
    if n_head == 2:
        both = both + lax.ppermute(both, "head", [(0, 1), (1, 0)])
    else:
        both = lax.psum(both, "head")
    return (input_grad, act_grad, both[0], both[1])


def solution(mesh):
    return jax.shard_map(
        local,
        mesh=mesh,
        in_specs=(
            P("seq", "head"),
            P("seq", "head"),
            P("seq", None),
            P("seq", None),
            P("seq", "head"),
            P("seq", "head"),
        ),
        out_specs=(P("seq", "head"), P("seq", "head"), P("seq", None), P("seq", None)),
        check_vma=False,
    )
```

```python
import functools

import jax
import jax.numpy as jnp
from jax import lax
from jax.experimental import pallas as pl
from jax.experimental.pallas import tpu as pltpu
from jax.sharding import PartitionSpec as P

RING = 4
LANES = 128
EXTRA = 16
NT = (((1,), (1,)), ((), ()))
TN = (((0,), (0,)), ((), ()))
NN = (((1,), (0,)), ((), ()))
bf16, f32 = jnp.bfloat16, jnp.float32


def mm(a, b, dims):
    return lax.dot_general(a, b, dims, preferred_element_type=f32)


def mm_exact(a, b, dims):
    return lax.dot_general(a, b, dims, precision=lax.Precision.HIGHEST, preferred_element_type=f32)


def spread(columns, width):
    rows = columns.shape[0]
    return jnp.concatenate(
        [jnp.broadcast_to(columns[:, h : h + 1], (rows, width)) for h in range(columns.shape[1])],
        axis=1,
    )


def iota(shape, axis):
    return lax.broadcasted_iota(jnp.int32, shape, axis)


def three_parts(value):
    first = value.astype(bf16).astype(f32)
    second = (value - first).astype(bf16).astype(f32)
    return first, second, value - first - second


def cumulate(n_heads, log_tiles, cum, cum_t):
    parts = jnp.concatenate([tile[...] for tile in log_tiles], axis=0)
    rows = parts.shape[0]
    source, head = iota((LANES, LANES), 0), iota((LANES, LANES), 1)
    pick = (source < 3 * n_heads) & (lax.rem(source, n_heads) == head)
    logs = mm(parts, pick.astype(f32).astype(bf16), NN)
    upto = (iota((rows, rows), 0) <= iota((rows, rows), 1)).astype(f32)
    cum[...] = mm_exact(upto, logs, TN)
    if cum_t is not None:
        cum_t[...] = mm_exact(logs, upto, TN)


def group_of(value, g, heads, axis):
    shift = lax.rem(LANES - g * heads, LANES)
    value = pltpu.roll(value, shift, axis)
    return value[:, :heads] if axis == 1 else value[:heads]


def diagonal(heads, half, lo, col, row, each):
    later = iota((half, half), 1) >= iota((half, half), 0)
    for h in range(heads):
        log = row[h : h + 1, lo : lo + half] - col[lo : lo + half, h : h + 1]
        each(h, jnp.exp(jnp.where(later, log, -jnp.inf)))


def cumulate_own(log_t, cum, cum_t):
    n_heads, rows = log_t.shape
    logs = jnp.concatenate([log_t[...], jnp.zeros((LANES - n_heads, rows), f32)], axis=0)
    upto = (iota((rows, rows), 0) <= iota((rows, rows), 1)).astype(f32)
    cum[...] = mm_exact(upto, logs, (((0,), (1,)), ((), ())))
    if cum_t is not None:
        cum_t[...] = mm_exact(logs, upto, NN)


def edge_kernel(n_heads, at, x, dy, b, c, log_t, *refs):
    messages, cum = refs[:RING], refs[RING]
    g = pl.program_id(0)
    heads = n_heads // RING
    rows = x.shape[0]
    width = x.shape[1] // heads
    n = b.shape[1]

    @pl.when(g == 0)
    def _():
        cumulate_own(log_t, cum, None)

    col = group_of(cum[...], g, heads, 1)
    last = col[rows - 1 : rows, :]
    tailed = (x[...].astype(f32) * spread(jnp.exp(last - col), width)).astype(bf16)
    decayed = (dy[...].astype(f32) * spread(jnp.exp(col), width)).astype(bf16)
    ends = mm(b[...], tailed, TN).astype(bf16)
    fronts = mm(c[...], decayed, TN).astype(bf16)
    log = spread(last, width)
    for j in range(RING):

        @pl.when(lax.bitwise_xor(at[0], g) == j)
        def _():
            messages[j][:n] = ends
            messages[j][n : 2 * n] = fronts
            write_log(messages[j], log)


def pack_kernel(n_heads, dy, b, c, log_t, out):
    rows, columns = dy.shape
    fill = jnp.zeros((LANES - 3 * n_heads, rows), f32)
    logs = jnp.concatenate([*three_parts(log_t[...]), fill], axis=0)
    out[:, :columns] = dy[...]
    out[:, columns : columns + LANES] = b[...]
    out[:, columns + LANES : columns + 2 * LANES] = c[...]
    out[:, columns + 2 * LANES :] = logs.T.astype(bf16)


def own_kernel(n_heads, x, dy, b, c, log_t, write_local, read_local, total, cum, cum_t):
    g = pl.program_id(0)
    heads = n_heads // RING
    rows = x.shape[0]
    half = rows // 2
    width = x.shape[1] // heads

    @pl.when(g == 0)
    def _():
        total[...] = jnp.zeros_like(total)
        cumulate_own(log_t, cum, cum_t)

    col, row = group_of(cum[...], g, heads, 1), group_of(cum_t[...], g, heads, 0)
    mid = col[half - 1 : half, :]
    for i in range(2):
        lo = i * half
        parts = []

        def add(h, decay):
            span = slice(h * width, (h + 1) * width)
            parts.append(decay * mm(x[lo : lo + half, span], dy[lo : lo + half, span], NT))

        diagonal(heads, half, lo, col, row, add)
        total[lo : lo + half, lo : lo + half] += sum(parts)
    early = (x[:half].astype(f32) * spread(jnp.exp(mid - col[:half]), width)).astype(bf16)
    late = (dy[half:].astype(f32) * spread(jnp.exp(col[half:] - mid), width)).astype(bf16)
    total[:half, half:] += mm(early, late, NT)

    @pl.when(g == pl.num_programs(0) - 1)
    def _():
        write_local[...] = mm_exact(total[...], c[...].astype(f32), NN)
        read_local[...] = mm_exact(total[...], b[...].astype(f32), TN)


def block_kernel(n_heads, top, bottom, *refs):
    tiles, (act, fronts, log_row, cum_out, cum_t) = refs[:6], refs[6:]
    b = jnp.concatenate([tiles[0][...], tiles[1][...]], axis=0)
    c = jnp.concatenate([tiles[2][...], tiles[3][...]], axis=0)
    g = pl.program_id(0)
    heads = n_heads // RING
    half = top.shape[0]
    rows = 2 * half
    width = top.shape[1] // heads

    @pl.when(g == 0)
    def _():
        cumulate(n_heads, tiles[4:], cum_out, cum_t)

    col, row = group_of(cum_out[...], g, heads, 1), group_of(cum_t[...], g, heads, 0)
    mid, last = col[half - 1 : half, :], col[rows - 1 : rows, :]
    log_row[...] = spread(last, width)
    scores = mm(b, c, NT)
    late_f = bottom[...].astype(f32) * spread(jnp.exp(col[half:] - mid), width)
    late = late_f.astype(bf16)
    first = (top[...].astype(f32) * spread(jnp.exp(col[:half]), width)).astype(bf16)
    second = (late_f * spread(jnp.exp(mid), width)).astype(bf16)
    fronts[0] = (mm(c[:half], first, TN) + mm(c[half:], second, TN)).astype(bf16)
    cross = mm(scores[:half, half:].astype(bf16), late, NN)
    to_mid = jnp.exp(mid - col[:half])
    for i, dy in enumerate((top, bottom)):
        lo = i * half
        score = scores[lo : lo + half, lo : lo + half]

        def put(h, decay):
            span = slice(h * width, (h + 1) * width)
            out = mm((decay * score).astype(bf16), dy[:, span], NN)
            if i == 0:
                out += cross[:, span] * to_mid[:, h : h + 1]
            act[lo : lo + half, span] = out.astype(act.dtype)

        diagonal(heads, half, lo, col, row, put)


def log_over(p, logs, wanted):
    total = jnp.zeros_like(logs[0])
    for k in range(RING):
        total += jnp.where(wanted(lax.bitwise_xor(p, k)), logs[k], 0.0)
    return total


def combine_kernel(at, *refs):
    parts, (state_out, grad_out) = refs[:RING], refs[RING:]
    n = state_out.shape[0] - EXTRA
    logs = [log_of(part) for part in parts]
    p = at[0]
    state, grad = 0.0, 0.0
    for j in range(RING):
        own = lax.bitwise_xor(p, j)
        state += parts[j][:n].astype(f32) * jnp.exp(log_over(p, logs, lambda k: k > own))
        grad += parts[j][n : 2 * n].astype(f32) * jnp.exp(log_over(p, logs, lambda k: k < own))
    for out, value in ((state_out, state), (grad_out, grad)):
        out[:n] = value.astype(bf16)
        write_log(out, sum(logs))


def write_log(out, log):
    n, width = out.shape
    row = iota((EXTRA, width), 0)
    rows = jnp.zeros((EXTRA, width), f32)
    for i, part in enumerate(three_parts(log)):
        rows = jnp.where(row == i, part, rows)
    out[n - EXTRA :] = rows.astype(bf16)


def log_of(message):
    n = message.shape[0] - EXTRA
    tail = message[n:].astype(f32)
    return tail[0:1] + tail[1:2] + tail[2:3]


def merge_kernel(*refs):
    for near, far, out in ((*refs[:2], refs[4]), (*refs[2:4], refs[5])):
        n = near.shape[0] - EXTRA
        log = log_of(near)
        out[:n] = (near[:n].astype(f32) + far[:n].astype(f32) * jnp.exp(log)).astype(bf16)
        write_log(out, log + log_of(far))


def merged(near, far, weight=1.0):
    n = near.shape[0] - EXTRA
    log = log_of(near)
    value = near[:n].astype(f32) + far[:n].astype(f32) * (jnp.exp(log) * weight)
    return value, log + log_of(far)


def across_kernel(outer, at, state, state_far, grad, grad_far, out):
    n = out.shape[0] - EXTRA
    lower = at[1] < outer // 2
    (state_value, state_log), (grad_value, grad_log) = merged(state, state_far), merged(grad, grad_far)
    out[:n] = jnp.where(lower, state_value, grad_value).astype(bf16)
    write_log(out, jnp.where(lower, state_log, grad_log))


def settle_kernel(outer, at, state, grad, got, state_out, grad_out):
    lower = (at[1] < outer // 2).astype(f32)
    for near, weight, out in ((state, 1.0 - lower, state_out), (grad, lower, grad_out)):
        n = near.shape[0] - EXTRA
        value, log = merged(near, got, weight)
        out[:n] = value.astype(bf16)
        write_log(out, log)


def finish_kernel(n_heads, n_w, outer, share, at, *refs):
    locals_, refs = refs[:RING], refs[RING:]
    fronts, refs = refs[:RING], refs[RING:]
    quarters, refs = refs[:RING], refs[RING:]
    logs, refs = [r[...] for r in refs[:RING]], refs[RING:]
    tops, refs = refs[:RING], refs[RING:]
    bottoms, refs = refs[:RING], refs[RING:]
    cums, refs = refs[:RING], refs[RING:]
    w, refs = refs[:n_w], refs[n_w:]
    x, acts, own, write, *tiles, total = refs
    g, p = pl.program_id(0), at[0]
    heads = n_heads // RING
    rows = own.shape[0]
    width = own.shape[1] // heads
    n = quarters[0].shape[0] - EXTRA
    source = lax.bitwise_xor(p, g)
    carried = quarters[0][:n].astype(f32)
    for j in range(1, RING):
        carried = jnp.where(source == j, quarters[j][:n].astype(f32), carried)

    @pl.when(g == 0)
    def _():
        write[...] = jnp.zeros_like(write)
        total[...] = jnp.zeros_like(total)

    added = [front[0].astype(f32) for front in fronts]
    for j in range(RING):
        col = group_of(cums[j][...], g, heads, 1)
        tail = spread(jnp.exp(col[rows - 1 : rows, :] - col), width)
        place = lax.bitwise_xor(p, j)
        grads = carried * jnp.exp(log_over(p, logs, lambda k: k > place))
        for i in range(RING):
            if i != j:
                there = lax.bitwise_xor(p, i)
                weight = jnp.exp(log_over(p, logs, lambda k: (k > place) & (k < there)))
                grads += added[i] * jnp.where(there > place, weight, 0.0)
        grads = grads.astype(bf16)
        b = jnp.concatenate([tops[j][...], bottoms[j][...]], axis=0)
        out = mm(b, grads, NN) * tail + locals_[j][...].astype(f32)
        out = out.astype(acts.dtype)
        acts[j * rows : (j + 1) * rows, :] = out
        if j == 0:
            own[...] = out
            write[...] += mm((x[...].astype(f32) * tail).astype(bf16), grads, NT)
    for k in range(n_w):
        n_rows = w[k].shape[0]
        total[:, k * n_rows : (k + 1) * n_rows] += mm(acts[...], w[k][...], NT)

    @pl.when(g == pl.num_programs(0) - 1)
    def _():
        if len(tiles) == 1:
            for k in range(n_w):
                put_tile(tiles[0], lax.rem(at[1] + k, outer), total, k, n_rows)
        else:
            for tile in tiles:
                tile[...] = jnp.zeros_like(tile)
            for k in range(n_w):
                o = lax.rem(at[1] + k, outer)
                for tile, side in zip(tiles, (at[2], 1 - at[2])):

                    @pl.when(lax.div(o, share) == side)
                    def _():
                        put_tile(tile, lax.rem(o, share), total, k, n_rows)


def put_tile(tile, slot, total, k, n_rows):
    rows = total.shape[0] // RING
    for j in range(RING):
        part = total[j * rows : (j + 1) * rows, k * n_rows : (k + 1) * n_rows]
        tile[j, slot] = part.astype(tile.dtype)


def read_kernel(n_heads, at, *refs):
    tops, refs = refs[:RING], refs[RING:]
    bottoms, refs = refs[:RING], refs[RING:]
    cums, refs = list(refs[: RING - 1]), refs[RING - 1 :]
    log_tiles, refs = refs[:2], refs[2:]
    parts, (carried, *outs, last_cum) = refs[:RING], refs[RING:]
    cumulate(n_heads, log_tiles, last_cum, None)
    cums.append(last_cum)
    logs = [log_of(part) for part in parts]
    p = at[0]
    heads = n_heads // RING
    half = tops[0].shape[0]
    n = carried.shape[0] - EXTRA
    width = carried.shape[1] // heads
    for j in range(RING):
        own = lax.bitwise_xor(p, j)
        total = carried[:n].astype(f32) * jnp.exp(log_over(p, logs, lambda k: k < own))
        for i in range(RING):
            if i != j:
                there = lax.bitwise_xor(p, i)
                weight = jnp.exp(log_over(p, logs, lambda k: (k < own) & (k > there)))
                total += parts[i][:n].astype(f32) * jnp.where(there < own, weight, 0.0)
        states = total.astype(bf16)
        decay = spread(jnp.exp(group_of(cums[j][...], p, heads, 1)), width)
        for i, dy in enumerate((tops[j], bottoms[j])):
            at_rows = slice(i * half, (i + 1) * half)
            scaled = (dy[...].astype(f32) * decay[at_rows]).astype(bf16)
            outs[j][at_rows] = mm(scaled, states, NT).astype(bf16)


def early_kernel(at, mine, got, *refs):
    reads, outs = refs[:RING], refs[RING:]
    width = mine.shape[3]
    for j in range(RING):
        for slot in range(mine.shape[1]):
            value = mine[j, slot].astype(f32) + got[j, slot].astype(f32)
            outs[j][:, slot * width : (slot + 1) * width] = value.astype(bf16)
        outs[j][:, mine.shape[1] * width :] = reads[j][...]


def place_kernel(outer, share, at, *refs):
    blocks, late, out = refs[:RING], refs[RING:-1], refs[-1]
    p, z, side = at[0], at[1], at[2]
    width = out.shape[1] // (share * RING)
    last = lax.rem(z + outer - 1, outer)
    for slot in range(share):
        for j in range(RING):
            column = pl.multiple_of((slot * RING + lax.bitwise_xor(p, j)) * width, width)

            @pl.when(side * share + slot == last)
            def _():
                out[:, pl.ds(column, width)] = late[j][...]

            @pl.when(side * share + slot != last)
            def _():
                out[:, pl.ds(column, width)] = blocks[j][:, slot * width : (slot + 1) * width]


def call(kernel, name, grid, in_specs, out_specs, out_shape, scratch=(), after=()):
    n_in, n_after = len(in_specs), len(after)

    def body(at, *refs):
        kernel(at, *refs[:n_in], *refs[n_in + n_after :])

    fn = pl.pallas_call(
        body,
        grid_spec=pltpu.PrefetchScalarGridSpec(
            num_scalar_prefetch=1,
            grid=grid,
            in_specs=list(in_specs) + [pl.BlockSpec(memory_space=pl.ANY)] * n_after,
            out_specs=out_specs,
            scratch_shapes=list(scratch),
        ),
        out_shape=out_shape,
        compiler_params=pltpu.CompilerParams(vmem_limit_bytes=56 * 2**20),
        cost_estimate=pl.CostEstimate(flops=0, bytes_accessed=0, transcendentals=0),
        name=name,
    )
    return lambda *operands: fn(*operands, *after)


def local(x, dy, write_proj, read_proj, log_decay, w_in):
    rows, columns = x.shape
    half = rows // 2
    state_dim = write_proj.shape[1]
    n_heads = log_decay.shape[1]
    heads = n_heads // RING
    width = columns // n_heads
    part = heads * width
    w_rows = w_in.shape[0]
    n_seq, n_head = lax.axis_size("seq"), lax.axis_size("head")
    outer = n_seq // RING
    place = lax.axis_index("seq")
    side = lax.axis_index("head")
    p, z = place % RING, place // RING
    at = jnp.stack([p, z, side]).astype(jnp.int32)

    def swap(value, j):
        return lax.ppermute(value, "seq", [(s, s ^ j) for s in range(n_seq)])

    def along(value, d):
        return lax.ppermute(
            value, "seq", [(s, s + d * RING) for s in range(n_seq) if 0 <= s + d * RING < n_seq]
        )

    w_blocks = [w_in]

    def turn_w():
        turn = [(s, (s - RING) % n_seq) for s in range(n_seq)]
        w_blocks.append(lax.ppermute(w_blocks[-1], "seq", turn))

    turn_w()

    def const(*shape):
        return pl.BlockSpec(shape, lambda g, q: (0,) * len(shape))

    by_group = pl.BlockSpec((rows, part), lambda g, q: (0, g))
    state_spec = pl.BlockSpec((1, state_dim, part), lambda g, q: (g, 0, 0))
    log_spec = pl.BlockSpec((1, part), lambda g, q: (0, g))
    cum_spec = const(rows, LANES)
    proj_spec = const(rows, state_dim)
    message_spec = const(state_dim + EXTRA, part)
    shape = jax.ShapeDtypeStruct
    state_shape = shape((RING, state_dim, part), bf16)
    log_shape = shape((1, columns), f32)
    cum_shape = shape((rows, LANES), f32)
    message_shape = shape((state_dim + EXTRA, part), bf16)
    cum_scratch, cum_t_scratch = pltpu.VMEM((rows, LANES), f32), pltpu.VMEM((LANES, rows), f32)

    log_in_spec = const(n_heads, rows)
    log_t = log_decay.T
    own_specs = [by_group, by_group, proj_spec, proj_spec, log_in_spec]
    part_spec = const(2 * state_dim + EXTRA, part)
    parts = call(
        functools.partial(edge_kernel, n_heads),
        "edges",
        (RING,),
        own_specs,
        [part_spec] * RING,
        [shape((2 * state_dim + EXTRA, part), bf16)] * RING,
        [cum_scratch],
    )(at, x, dy, write_proj, read_proj, log_t)
    parts = [parts[0]] + [swap(parts[j], j) for j in range(1, RING)]

    write_local, read_local = call(
        functools.partial(lambda *refs: own_kernel(n_heads, *refs[1:])),
        "own_tokens",
        (RING,),
        own_specs,
        [proj_spec] * 2,
        [shape((rows, state_dim), f32)] * 2,
        [pltpu.VMEM((rows, rows), f32), cum_scratch, cum_t_scratch],
    )(at, x, dy, write_proj, read_proj, log_t)

    packed = call(
        functools.partial(lambda *refs: pack_kernel(n_heads, *refs[1:])),
        "pack",
        (1,),
        [const(rows, columns), proj_spec, proj_spec, log_in_spec],
        const(rows, columns + 3 * LANES),
        shape((rows, columns + 3 * LANES), bf16),
    )(at, dy, write_proj, read_proj, log_t)

    def halves(width, column):
        upper = pl.BlockSpec((half, width), lambda g, q: (0, column(g, q)))
        lower = pl.BlockSpec((half, width), lambda g, q: (1, column(g, q)))
        return [(upper, lower)] * (RING - 1) + [(upper, upper)]

    half_specs = halves(part, lambda g, q: g)
    mine_specs = halves(part, lambda g, q: q[0])
    tile_specs = [halves(LANES, lambda g, q, i=i: columns // LANES + i) for i in range(3)]

    def block(j, top, bottom, after=()):
        return call(
            functools.partial(lambda *refs: block_kernel(n_heads, *refs[1:])),
            "tokens",
            (RING,),
            [*half_specs[j]] + [spec for specs in tile_specs for spec in specs[j]],
            [by_group, state_spec, log_spec, cum_spec],
            [shape((rows, columns), bf16), state_shape, log_shape, cum_shape],
            [cum_t_scratch],
            after,
        )(at, top, bottom, *([top, bottom] * 3))

    results = [block(0, packed, packed)]
    logs = [results[0][2]]
    packed, parts, logs, read_local = lax.optimization_barrier((packed, parts, logs, read_local))
    from_x, from_y = lax.optimization_barrier((swap(packed, 1), swap(packed, 2)))

    def combine():
        return call(
            combine_kernel,
            "messages",
            (1,),
            [part_spec] * RING,
            [message_spec] * 2,
            [message_shape] * 2,
        )(at, *parts)

    def merge(*pairs):
        return call(
            lambda q, *refs: merge_kernel(*refs),
            "merge",
            (1,),
            [message_spec] * 4,
            [message_spec] * 2,
            [message_shape] * 2,
        )(at, *pairs)

    state_span, grad_span = combine()
    d = 1
    while d < outer:
        if outer == 4 and d == 2:
            got = lax.ppermute(across, "seq", [(s, s ^ (d * RING)) for s in range(n_seq)])
            state_part, grad_part = call(
                functools.partial(settle_kernel, outer),
                "settle",
                (1,),
                [message_spec] * 3,
                [message_spec] * 2,
                [message_shape] * 2,
            )(at, state_part, grad_part, got)
            got, w_blocks[-1] = lax.optimization_barrier((got, w_blocks[-1]))
            break
        state_got, grad_got = along(state_span, d), along(grad_span, -d)
        if d == 1:
            state_part, grad_part = state_got, grad_got
        else:
            state_part, grad_part = merge(state_part, state_got, grad_part, grad_got)
        if outer == 4:
            across = call(
                functools.partial(across_kernel, outer),
                "across",
                (1,),
                [message_spec] * 4,
                message_spec,
                message_shape,
            )(at, state_span, state_got, grad_span, grad_got)
        elif 2 * d < outer:
            state_span, grad_span = merge(state_span, state_got, grad_span, grad_got)
        d *= 2
    turn_w()
    from_x, from_y, grad_part = lax.optimization_barrier((from_x, from_y, grad_part))
    blocks = [(packed, packed), (from_x, from_x), (from_y, from_y)]
    blocks.append((swap(from_x[:half], 2), swap(from_y[half:], 1)))
    results += [block(j, *blocks[j]) for j in range(1, RING - 1)]
    logs += [v[2] for v in results[1:]]
    logs, grad_part = lax.optimization_barrier((logs, grad_part))
    grad_parts = [grad_part] + [swap(grad_part, j) for j in range(1, RING)]

    read_parts = call(
        functools.partial(read_kernel, n_heads),
        "read_carry",
        (1,),
        [spec[0] for spec in mine_specs]
        + [spec[1] for spec in mine_specs]
        + [cum_spec] * (RING - 1)
        + list(tile_specs[2][-1])
        + [part_spec] * RING
        + [message_spec],
        [proj_spec] * RING,
        [shape((rows, state_dim), bf16)] * RING,
        [cum_scratch],
    )(
        at,
        *[top for top, _ in blocks],
        *[bottom for _, bottom in blocks],
        *[v[3] for v in results],
        *blocks[-1],
        *parts,
        state_part,
    )

    read_parts, w_blocks[-1] = lax.optimization_barrier((read_parts, w_blocks[-1]))
    after = [read_parts[0]]
    if outer > 2:
        after.append(w_blocks[-1])
    results.append(block(RING - 1, *blocks[-1], after))
    logs.append(results[-1][2])
    while len(w_blocks) < outer:
        turn_w()
    local_acts, fronts, _, cums = zip(*results)
    two = n_head == 2 and w_rows % LANES == 0
    share = outer // n_head
    n_w = outer - 1 if two else outer
    tall = pl.BlockSpec((RING * rows, part), lambda g, q: (0, g))
    w_spec = pl.BlockSpec((w_rows, part), lambda g, q: (0, g))
    tile_shapes = [(RING, share, rows, w_rows)] * 2 if two else [(RING, outer, rows, w_rows)]
    acts, act_grad, write_carry, *tiles = call(
        functools.partial(finish_kernel, n_heads, n_w, outer, share),
        "finish",
        (RING,),
        [by_group] * RING
        + [state_spec] * RING
        + [message_spec] * RING
        + [log_spec] * RING
        + [spec[0] for spec in tile_specs[0]]
        + [spec[1] for spec in tile_specs[0]]
        + [cum_spec] * RING
        + [w_spec] * n_w
        + [by_group],
        [tall, by_group, proj_spec] + [const(*v) for v in tile_shapes],
        [
            shape((RING * rows, columns), bf16),
            shape((rows, columns), bf16),
            shape((rows, state_dim), f32),
        ]
        + [shape(v, bf16) for v in tile_shapes],
        [pltpu.VMEM((RING * rows, n_w * w_rows), f32)],
    )(
        at,
        *local_acts,
        *fronts,
        *grad_parts,
        *logs,
        *[top for top, _ in blocks],
        *[bottom for _, bottom in blocks],
        *cums,
        *w_blocks[:n_w],
        x,
    )

    def to_owners(tile):
        return [tile[0]] + [swap(tile[j], j) for j in range(1, RING)]

    if two:
        mine, theirs = tiles
        got = lax.ppermute(theirs, "head", [(0, 1), (1, 0)])
        pack_width = share * w_rows + state_dim
        early = call(
            early_kernel,
            "early_sums",
            (1,),
            [const(*mine.shape)] * 2 + [proj_spec] * RING,
            [const(rows, pack_width)] * RING,
            [shape((rows, pack_width), bf16)] * RING,
        )(at, mine, got, *read_parts)
        early, w_last = lax.optimization_barrier((early, w_blocks[-1]))
        tile = mm(acts, w_last, NT).astype(bf16)

        def owner(s):
            return (s // RING + outer - 1) % outer // share

        both_axes = ("seq", "head")
        got = lax.ppermute(
            tile, both_axes, [(2 * s + 1 - owner(s), 2 * s + owner(s)) for s in range(n_seq)]
        )
        tile = (tile.astype(f32) + got.astype(f32)).astype(bf16).reshape(RING, rows, w_rows)
        late = [tile[0]] + [
            lax.ppermute(
                tile[j],
                both_axes,
                [(2 * s + owner(s), 2 * (s ^ j) + owner(s)) for s in range(n_seq)],
            )
            for j in range(1, RING)
        ]
        early, late = lax.optimization_barrier((to_owners(early), late))
        read_got = [v[:, share * w_rows :] for v in early[1:]]
        input_grad = pl.pallas_call(
            functools.partial(place_kernel, outer, share),
            in_specs=[pl.BlockSpec(memory_space=pltpu.SMEM)]
            + [pl.BlockSpec(memory_space=pltpu.VMEM)] * (2 * RING),
            out_specs=pl.BlockSpec(memory_space=pltpu.VMEM),
            out_shape=shape((rows, share * RING * w_rows), bf16),
            compiler_params=pltpu.CompilerParams(vmem_limit_bytes=32 * 2**20),
            name="place",
        )(at, *early, *late)
    else:
        summed = lax.psum_scatter(tiles[0], "head", scatter_dimension=1, tiled=True)
        pieces = jnp.take(jnp.stack(to_owners(summed)), p ^ jnp.arange(RING), axis=0)
        input_grad = pieces.transpose(2, 1, 0, 3).reshape(rows, share * RING * w_rows)
    if not two:
        read_got = [swap(read_parts[j], j) for j in range(1, RING)]
    read_carry = read_parts[0].astype(f32) + sum(v.astype(f32) for v in read_got)
    both = jnp.stack([write_local + write_carry, read_local + read_carry])
    if n_head == 2:
        both = both + lax.ppermute(both, "head", [(0, 1), (1, 0)])
    else:
        both = lax.psum(both, "head")
    return (input_grad, act_grad, both[0], both[1])


def solution(mesh):
    return jax.shard_map(
        local,
        mesh=mesh,
        in_specs=(
            P("seq", "head"),
            P("seq", "head"),
            P("seq", None),
            P("seq", None),
            P("seq", "head"),
            P("seq", "head"),
        ),
        out_specs=(P("seq", "head"), P("seq", "head"), P("seq", None), P("seq", None)),
        check_vma=False,
    )
```
